32 devices in a mesh: body: 2 (over x), gx: 4 (over z), yz: 4 (over y, core).
Axes of the slice: x: 2, y: 2, z: 4, core: 2. Of those that a mesh axis runs over, the one named last changes fastest.
Arguments:
- displacement: float32 [2, 3, 64, 256, 128], P('body', None, 'gx', 'yz'), may hold values from -1.75 to 1.75
- velocity: float32 [2, 3, 64, 256, 128], P('body', None, 'gx', 'yz'), may hold values from -3 to 3
- material: int32 [2, 64, 256, 128], P('body', 'gx', 'yz'), may hold values from 0 to 7
- moduli: float32 [8], replicated, may hold values from 0.5 to 2
- density: float32 [8], replicated, may hold values from 1 to 4
- partner: int32 [256], replicated, may hold values from 0 to 255, as said below
- active: int32 [256], replicated, may hold values 0 or 1
Outputs:
- final_displacement: float32 [2, 3, 64, 256, 128], P('body', None, 'gx', 'yz')
- final_velocity: float32 [2, 3, 64, 256, 128], P('body', None, 'gx', 'yz')
The draws below stay inside these ranges and needn't reach their ends.
Inputs may be any that keep to these rules, and one draw needn't show every extreme that they name: partner is a permutation of the rows of body 1's face; in every aligned block of 64 rows of partner, exactly 32 values lie in the same-numbered block of 64 rows and the others in the next block, the last block's next being the first.
All inputs are finite; a program needn't handle non-finite values.
Results may differ from the reference program's by a relative error of at most 0.0001.
Values sent between devices are 32-bit elements; how exact they have to be, the bound alone decides.
No kernel may reach another device: no remote copies, remote signals or barrier semaphores. Data moves between devices by JAX's collectives and lax.ppermute only.
A program may use at most 64 MiB of HBM per device.

```python
import math
import jax
import jax.numpy as jnp
from jax import lax

CY = 64
NZ = 128
STEPS = 4
MATS = 8
NX = 64
NY = 256


def draw_partner(key, part):
    blocks = NY // CY
    half_rows = CY // 2
    row_keys = jax.random.split(jax.random.fold_in(key, 7), 2 * blocks)
    starting = jax.vmap(lambda subkey: jax.random.permutation(subkey, CY))(row_keys[:blocks])
    starting = starting + (jnp.arange(blocks) * CY)[:, None]
    joined = jnp.concatenate([starting[:, :half_rows], jnp.roll(starting, -1, axis=0)[:, half_rows:]], axis=1)
    orders = jax.vmap(lambda subkey: jax.random.permutation(subkey, CY))(row_keys[blocks:])
    mixed = jnp.take_along_axis(joined, orders, axis=1)
    return mixed.reshape(NY).astype(jnp.int32)


def set_ends(entries, key, smallest, largest):
    place = [jax.random.randint(jax.random.fold_in(key, axis), (), 0, length) for axis, length in enumerate(entries.shape)]
    widest = entries.shape.index(max(entries.shape))
    next_to = place[:widest] + [(place[widest] + 1) % entries.shape[widest]] + place[widest + 1:]
    return entries.at[tuple(place)].set(smallest).at[tuple(next_to)].set(largest)


def levels(key, shape, pieces, least, high):
    level = 1.0
    for dim, parts in pieces:
        draws = jax.random.uniform(jax.random.fold_in(jax.random.fold_in(key, 6), dim), (parts,), jnp.float32, least / len(pieces), high / len(pieces))
        level = level * jnp.repeat(jnp.exp(draws), shape[dim] // parts).reshape((-1,) + (1,) * (len(shape) - 1 - dim))
    return level


def noise(rng, shape, deviation, limit, shards=(), kind=jnp.bfloat16):
    factor_of = levels(rng, shape, shards, -0.22, 0.18) if shards else 1.0
    values = jax.random.normal(rng, shape, jnp.float32) * deviation * factor_of
    return jnp.minimum(jnp.maximum(values, -limit), limit).astype(kind)


def setup_inputs(seed: int = 0) -> dict:
    key_list = jax.random.split(jax.random.key(seed), 8)
    return {
        "displacement": noise(key_list[0], (2, 3, NX, NY, NZ), 0.3, 1.75, ((0, 2), (2, 4), (3, 4)), jnp.float32),
        "velocity": noise(key_list[1], (2, 3, NX, NY, NZ), 0.5, 3.0, ((0, 2), (2, 4), (3, 4)), jnp.float32),
        "material": set_ends(jax.random.randint(key_list[2], (2, NX, NY, NZ), 0, MATS), jax.random.fold_in(key_list[2], 1), 0, MATS - 1).astype(jnp.int32),
        "moduli": jnp.clip(jnp.exp(jax.random.uniform(key_list[3], (MATS,), jnp.float32, math.log(0.5), math.log(2.0))), 0.5, 2.0),
        "density": jnp.clip(jnp.exp(jax.random.uniform(key_list[4], (MATS,), jnp.float32, math.log(1.0), math.log(4.0))), 1.0, 4.0),
        "partner": draw_partner(jax.random.fold_in(key_list[7], 71), 0),
        "active": set_ends((jax.random.randint(key_list[6], (NY,), 0, 4) < 3).astype(jnp.int32), jax.random.fold_in(key_list[6], 1), 0, 1),
    }


STEP_TIME = 0.2
YIELD_SPAN = 0.5
PENALTY = 4.0
SOFT_WIDTH = 0.1
KERNEL_WIDTH = 1.5


def tension(stretch):
    return YIELD_SPAN * jnp.tanh(stretch / YIELD_SPAN)


def pair_pressure(own_surface, far_surface):
    column = jnp.arange(own_surface.shape[-1]).astype(jnp.float32)
    opening = -own_surface[0][:, :, None] - far_surface[0][:, None, :]
    along_z = (column + own_surface[2])[:, :, None] - (column + far_surface[2])[:, None, :]
    along_y = own_surface[1][:, :, None] - far_surface[1][:, None, :]
    weight = jnp.exp(-(along_y * along_y + along_z * along_z) / (2.0 * KERNEL_WIDTH * KERNEL_WIDTH))
    return weight * (PENALTY * SOFT_WIDTH) * jax.nn.softplus(-opening / SOFT_WIDTH)


def axis_forces(displace, stiffness, dimension):
    extent = displace.shape[dimension]
    zero_plane = jnp.zeros_like(lax.slice_in_dim(displace, 0, 1, axis=dimension))
    ahead = jnp.concatenate([lax.slice_in_dim(displace, 1, extent, axis=dimension), zero_plane], axis=dimension)
    pulls = stiffness * tension(ahead - displace)
    behind = jnp.concatenate([zero_plane, lax.slice_in_dim(pulls, 0, extent - 1, axis=dimension)], axis=dimension)
    return pulls - behind


def reference(displacement, velocity, material, moduli, density, partner, active):
    inside = ((jnp.arange(NX) < NX - 1)[:, None, None]
              & (jnp.arange(NY) < NY - 1)[None, :, None]
              & (jnp.arange(NZ) < NZ - 1)[None, None, :])
    elements = jnp.where(inside[None], moduli[material], 0.0)
    node_mass = density[material][:, None]
    padded = jnp.pad(elements, ((0, 0), (1, 0), (1, 0), (1, 0)))
    stiff_x = 0.25 * (padded[:, 1:, 1:, 1:] + padded[:, 1:, :-1, 1:] + padded[:, 1:, 1:, :-1] + padded[:, 1:, :-1, :-1])
    stiff_y = 0.25 * (padded[:, 1:, 1:, 1:] + padded[:, :-1, 1:, 1:] + padded[:, 1:, 1:, :-1] + padded[:, :-1, 1:, :-1])
    stiff_z = 0.25 * (padded[:, 1:, 1:, 1:] + padded[:, :-1, 1:, 1:] + padded[:, 1:, :-1, 1:] + padded[:, :-1, :-1, 1:])
    active_rows = active.astype(jnp.float32)[:, None]
    for repeat in range(STEPS):
        forces = axis_forces(displacement, stiff_x[:, None], 2)
        forces = forces + axis_forces(displacement, stiff_y[:, None], 3)
        forces = forces + axis_forces(displacement, stiff_z[:, None], 4)
        own_surface = displacement[0, :, NX - 1]
        far_surface = displacement[1, :, NX - 1]
        matched = jnp.take(far_surface, partner, axis=1)
        pressure = pair_pressure(own_surface, matched)
        pushes = -jnp.sum(pressure, axis=2) * active_rows
        reaction = -jnp.sum(pressure, axis=1) * active_rows
        placed = jnp.zeros((NY, NZ), jnp.float32).at[partner].add(reaction)
        forces = forces.at[0, 0, NX - 1].add(pushes)
        forces = forces.at[1, 0, NX - 1].add(placed)
        velocity = velocity + STEP_TIME * forces / node_mass
        displacement = displacement + STEP_TIME * velocity
    return displacement, velocity
```

```python
import functools
import math

import jax
import jax.numpy as jnp
from jax import lax
from jax.experimental import pallas as pl
from jax.experimental.pallas import tpu as pltpu
from jax.sharding import PartitionSpec as P

STEPS = 4
STEP_TIME = 0.2
YIELD_SPAN = 0.5
PENALTY = 4.0
SOFT_WIDTH = 0.1
KERNEL_WIDTH = 1.5

U_SCALE = 1.0 / YIELD_SPAN
W_SCALE = STEP_TIME / YIELD_SPAN
KICK = STEP_TIME * STEP_TIME / YIELD_SPAN
LOG2E = math.log2(math.e)
GAP_SCALE = YIELD_SPAN / SOFT_WIDTH * LOG2E
SPAN = math.sqrt(LOG2E / (2.0 * KERNEL_WIDTH * KERNEL_WIDTH))
PRESSURE_SCALE = PENALTY * SOFT_WIDTH / LOG2E

AXES = ("body", "gx", "yz")
VMEM_LIMIT = 48 * 1024 * 1024


def vmem(shape):
    return pltpu.VMEM(shape, jnp.float32)


def call(kernel, outs, args, spaces=None, aliases=None, scratch=(), flops=0, moved=0):
    spaces = spaces or [None] * len(args)
    specs, placed = [], []
    for arg, space in zip(args, spaces):
        if space is None:
            placed.append(pltpu.with_memory_space_constraint(arg, pltpu.VMEM))
            specs.append(pl.BlockSpec(memory_space=pltpu.VMEM))
        else:
            placed.append(arg)
            specs.append(pl.BlockSpec(memory_space=space))
    return pl.pallas_call(
        kernel,
        out_shape=outs,
        in_specs=specs,
        out_specs=[pl.BlockSpec(memory_space=pltpu.VMEM)] * len(outs),
        input_output_aliases=aliases or {},
        scratch_shapes=list(scratch),
        compiler_params=pltpu.CompilerParams(vmem_limit_bytes=VMEM_LIMIT),
        cost_estimate=pl.CostEstimate(flops=flops, bytes_accessed=moved, transcendentals=0),
    )(*placed)


def prepare_kernel(d_ref, v_ref, mat_ref, moduli_ref, density_ref, place_ref, u_ref, w_ref, el_ref, kick_ref):
    planes, rows, cols = mat_ref.shape
    last_x = place_ref[0] == place_ref[1] - 1
    last_y = place_ref[2] == place_ref[3] - 1
    row = lax.broadcasted_iota(jnp.int32, (rows, cols), 0)
    col = lax.broadcasted_iota(jnp.int32, (rows, cols), 1)
    inside = (col < cols - 1) & ((row < rows - 1) | jnp.logical_not(last_y))

    @pl.loop(0, planes)
    def _(i):
        for c in range(3):
            u_ref[c, i] = d_ref[c, i] * U_SCALE
            w_ref[c, i] = v_ref[c, i] * W_SCALE
        kinds = mat_ref[i]
        stiff = jnp.zeros((rows, cols), jnp.float32)
        mass = jnp.ones((rows, cols), jnp.float32)
        for m in range(moduli_ref.shape[0]):
            hit = kinds == m
            stiff = jnp.where(hit, moduli_ref[m], stiff)
            mass = jnp.where(hit, density_ref[m], mass)
        keep = inside & ((i < planes - 1) | jnp.logical_not(last_x))
        el_ref[i] = jnp.where(keep, stiff, 0.0)
        kick_ref[i] = KICK / mass


def stiffness_kernel(
    el_ref, kick_ref, ra_ref, rb_ref, rc_ref, rd_ref, corner_ref, moduli_ref, place_ref, contact_ref,
    kx_ref, ky_ref, kz_ref, xlow_ref, xhigh_ref, ylow_ref, yhigh_ref, push_ref,
):
    planes, rows, cols = el_ref.shape
    even_x = place_ref[0] % 2 == 0
    even_y = place_ref[2] % 2 == 0
    inner_x = place_ref[0] > 0
    inner_y = place_ref[2] > 0
    factor = 0.25 * YIELD_SPAN

    def looked_up(kinds, keep):
        stiff = jnp.zeros(kinds.shape, jnp.float32)
        for m in range(moduli_ref.shape[0]):
            stiff = jnp.where(kinds == m, moduli_ref[m], stiff)
        col = lax.broadcasted_iota(jnp.int32, kinds.shape, 1)
        return jnp.where((col < cols - 1) & keep, stiff, 0.0)

    def with_behind(value):
        return value + pltpu.roll(value, 1, 1)

    row = lax.broadcasted_iota(jnp.int32, (rows, cols), 0)
    last_y = place_ref[2] == place_ref[3] - 1
    last_x = place_ref[0] == place_ref[1] - 1
    below_x = looked_up(
        jnp.where(even_x, rb_ref[3], ra_ref[3]), inner_x & ((row < rows - 1) | jnp.logical_not(last_y))
    )
    below_y = looked_up(jnp.where(even_y, rd_ref[3], rc_ref[3]), inner_y)
    plane_of = lax.broadcasted_iota(jnp.int32, (planes, cols), 0)
    below_y = jnp.where((plane_of < planes - 1) | jnp.logical_not(last_x), below_y, 0.0)
    corner = looked_up(corner_ref[...], inner_x & inner_y)[:1]

    def row_behind(value, first):
        return jnp.where(row == 0, first, pltpu.roll(value, 1, 0))

    def one_plane(i, value, first, earlier, earlier_first):
        s, s_first = with_behind(value), with_behind(first)
        t, t_first = with_behind(earlier), with_behind(earlier_first)
        z, z_first = value + earlier, first + earlier_first
        kx = factor * (s + row_behind(s, s_first))
        ky = factor * (s + t)
        kx_ref[i] = kx
        kz_ref[i] = factor * (z + row_behind(z, z_first))
        kick = kick_ref[i]
        ylow_ref[pl.ds(i, 1)] = kick[0:1] * factor * (s_first + t_first)
        yhigh_ref[pl.ds(i, 1)] = kick[rows - 1 : rows] * ky[rows - 1 : rows]
        ky_ref[i] = jnp.where(row < rows - 1, ky, 0.0)

    s, s_first = with_behind(below_x), with_behind(corner)
    xlow_ref[...] = kick_ref[0] * factor * (s + row_behind(s, s_first))
    earlier, earlier_first = below_x, corner
    for i in range(planes):
        value, first = el_ref[i], below_y[i : i + 1]
        one_plane(i, value, first, earlier, earlier_first)
        earlier, earlier_first = value, first
    xhigh_ref[...] = kick_ref[planes - 1] * kx_ref[planes - 1]
    push_ref[...] = contact_ref[...] * kick_ref[planes - 1] * (-PRESSURE_SCALE)


def interior_kernel(first, *refs):
    if first:
        u_in, w_in, kx_ref, ky_ref, kz_ref, kick_ref, u_ref, w_ref, y0_ref, y1_ref = refs
    else:
        (u_in, w_in, kx_ref, ky_ref, kz_ref, kick_ref, dx0_ref, dx1_ref, dy0_ref, dy1_ref,
         u_ref, w_ref, y0_ref, y1_ref) = refs
    _, planes, rows, cols = u_ref.shape
    if not first:
        patch(u_ref, w_ref, dx0_ref, dx1_ref, dy0_ref, dy1_ref)

    def plane(i, c, carried, ahead):
        here = u_ref[c, i]
        force = -carried
        pull_x = None
        if ahead is not None:
            pull_x = kx_ref[i] * jnp.tanh(ahead - here)
            force = force + pull_x
        pull_y = ky_ref[i] * jnp.tanh(pltpu.roll(here, rows - 1, 0) - here)
        force = force + (pull_y - pltpu.roll(pull_y, 1, 0))
        pull_z = kz_ref[i] * jnp.tanh(pltpu.roll(here, cols - 1, 1) - here)
        force = force + (pull_z - pltpu.roll(pull_z, 1, 1))
        w = w_ref[c, i] + kick_ref[i] * force
        u = here + w
        w_ref[c, i] = w
        u_ref[c, i] = u
        y0_ref[c, pl.ds(i, 1)] = u[0:1]
        y1_ref[c, pl.ds(i, 1)] = u[rows - 1 : rows]
        return pull_x

    def step(i, carried):
        return tuple(plane(i, c, carried[c], u_ref[c, i + 1]) for c in range(3))

    zero = jnp.zeros((rows, cols), jnp.float32)
    carried = lax.fori_loop(0, planes - 1, step, (zero, zero, zero))
    for c in range(3):
        plane(planes - 1, c, carried[c], None)


def patch(u_ref, w_ref, dx0_ref, dx1_ref, dy0_ref, dy1_ref):
    _, planes, rows, cols = u_ref.shape
    tile = math.gcd(8, rows)
    row = lax.broadcasted_iota(jnp.int32, (tile, cols), 0)
    low = jnp.where(row == 0, 1.0, 0.0)
    high = jnp.where(row == tile - 1, 1.0, 0.0)
    for ref in (u_ref, w_ref):
        ref[:, 0] += dx0_ref[...]
        ref[:, planes - 1] += dx1_ref[...]
        for c in range(3):
            for i in range(planes):
                ref[c, i, 0:tile] += low * dy0_ref[c, i : i + 1]
                ref[c, i, rows - tile : rows] += high * dy1_ref[c, i : i + 1]


def contact_kernel(scale, own_ref, near_ref, far_ref, pick_ref, push_ref, face_ref, out_ref, fx_ref, fy_ref, fz_ref):
    rows, cols = out_ref.shape
    lanes = pick_ref.shape[1]
    parts = lanes // rows
    deep = cols // parts
    is_face = face_ref[0] != 0

    @pl.when(jnp.logical_not(is_face))
    def _():
        out_ref[...] = jnp.zeros_like(out_ref)

    @pl.when(is_face)
    def _():
        pick = pick_ref[...]

        def matched(c):
            pool = jnp.concatenate([near_ref[c], far_ref[c]], axis=0)
            return lax.dot_general(
                pool, pick, (((0,), (0,)), ((), ())),
                precision=lax.Precision.HIGHEST, preferred_element_type=jnp.float32,
            )

        def own(c):
            turned = own_ref[c].T
            return jnp.concatenate([turned[h * deep : (h + 1) * deep] for h in range(parts)], axis=1)

        gap = scale * GAP_SCALE
        along = scale * YIELD_SPAN * SPAN
        fx_ref[...] = matched(0) * gap
        fy_ref[...] = matched(1) * along
        spot = lax.broadcasted_iota(jnp.int32, (cols, lanes), 0).astype(jnp.float32)
        fz_ref[...] = matched(2) * along + spot * SPAN
        lane = lax.broadcasted_iota(jnp.int32, (deep, lanes), 1)
        depth = lax.broadcasted_iota(jnp.int32, (deep, lanes), 0)
        mine = (depth + lane // rows * deep).astype(jnp.float32)
        ox = own(0) * gap
        oy = own(1) * along
        oz = own(2) * along + mine * SPAN

        def term(m, total):
            t = ox + fx_ref[pl.ds(m, 1)]
            dy = oy - fy_ref[pl.ds(m, 1)]
            dz = oz - fz_ref[pl.ds(m, 1)]
            weight = jnp.exp2(-(dy * dy + dz * dz))
            soft = jnp.maximum(t, 0.0) + jnp.log2(1.0 + jnp.exp2(-jnp.abs(t)))
            return total + weight * soft

        total = lax.fori_loop(0, cols, term, jnp.zeros((deep, lanes), jnp.float32), unroll=2)
        turned = jnp.concatenate([total[:, h * rows : (h + 1) * rows] for h in range(parts)], axis=0)
        out_ref[...] = turned.T * push_ref[...]


def boundary_kernel(
    scale, u_ref, y0_ref, y1_ref, sa_ref, sb_ref, sc_ref, sd_ref, ra_ref, rb_ref, rc_ref, rd_ref,
    xlow_ref, xhigh_ref, ylow_ref, yhigh_ref, push_ref, place_ref,
    na_ref, nb_ref, nc_ref, nd_ref, dx0_ref, dx1_ref, dy0_ref, dy1_ref,
):
    _, planes, rows, cols = u_ref.shape

    def halves(place, sent_a, sent_b, got_a, got_b, low_ref, high_ref):
        even = place % 2 == 0
        for c in range(3):
            a, b, x, y = sent_a[c], sent_b[c], got_a[c], got_b[c]
            first, last = jnp.where(even, b, a), jnp.where(even, a, b)
            before, after = jnp.where(even, y, x), jnp.where(even, x, y)
            yield (
                c,
                low_ref[...] * jnp.tanh((before - first) * scale),
                high_ref[...] * jnp.tanh((after - last) * scale),
            )

    for c, low, high in halves(place_ref[0], sa_ref, sb_ref, ra_ref, rb_ref, xlow_ref, xhigh_ref):
        if c == 0:
            high = high + push_ref[...]
        dx0_ref[c], dx1_ref[c] = low, high
    for c, low, high in halves(place_ref[2], sc_ref, sd_ref, rc_ref, rd_ref, ylow_ref, yhigh_ref):
        dy0_ref[c], dy1_ref[c] = low, high

    def send(first_ref, last_ref, side_first, side_last):
        for c in range(3):
            first_ref[c] = u_ref[c, 0] + dx0_ref[c]
            last_ref[c] = u_ref[c, planes - 1] + dx1_ref[c]
            side_first[c] = y0_ref[c] + dy0_ref[c]
            side_last[c] = y1_ref[c] + dy1_ref[c]
            for ref, i in ((first_ref, 0), (last_ref, planes - 1)):
                ref[c, 0:1] += dy0_ref[c, i : i + 1]
                ref[c, rows - 1 : rows] += dy1_ref[c, i : i + 1]
            for ref, j in ((side_first, 0), (side_last, rows - 1)):
                ref[c, 0:1] += dx0_ref[c, j : j + 1]
                ref[c, planes - 1 : planes] += dx1_ref[c, j : j + 1]

    even_x = place_ref[0] % 2 == 0
    even_y = place_ref[2] % 2 == 0
    for flag_x in (True, False):
        for flag_y in (True, False):

            @pl.when((even_x == flag_x) & (even_y == flag_y))
            def _(flag_x=flag_x, flag_y=flag_y):
                xs = (nb_ref, na_ref) if flag_x else (na_ref, nb_ref)
                ys = (nd_ref, nc_ref) if flag_y else (nc_ref, nd_ref)
                send(*xs, *ys)


def finish_kernel(u_in, w_in, dx0_ref, dx1_ref, dy0_ref, dy1_ref, d_ref, v_ref, u_ref, w_ref):
    planes = u_in.shape[1]
    patch(u_ref, w_ref, dx0_ref, dx1_ref, dy0_ref, dy1_ref)

    @pl.loop(0, planes)
    def _(i):
        for c in range(3):
            d_ref[c, i] = u_ref[c, i] * (1.0 / U_SCALE)
            v_ref[c, i] = w_ref[c, i] * (1.0 / W_SCALE)


def routes(count_body, count_x, count_y):
    def number(b, g, y):
        return (b * count_x + g) * count_y + y

    every = [(b, g, y) for b in range(count_body) for g in range(count_x) for y in range(count_y)]

    def pairs(target):
        return [(number(*at), number(*target(*at))) for at in every]

    def outer_x(b, g, y):
        if g in (0, count_x - 1):
            return 1 - b, g, y
        return b, (g + 1 if g % 2 else g - 1), y

    return {
        "a": pairs(lambda b, g, y: (b, g ^ 1, y)),
        "b": pairs(outer_x),
        "c": pairs(lambda b, g, y: (b, g, y ^ 1)),
        "d": pairs(lambda b, g, y: (b, g, (y + 1 if y % 2 else y - 1) % count_y)),
        "e": pairs(lambda b, g, y: (1 - b, g, (y - 1 if b else y + 1) % count_y)),
        "corner": pairs(lambda b, g, y: (b, (g + 1) % count_x, (y + 1) % count_y)),
    }


def contact_tables(partner, active, place_body, place_y, rows, rows_all, lanes):
    own = place_y * rows + jnp.arange(rows)
    index = jnp.arange(2 * rows)
    turn = jnp.where(place_body == 0, 1, -1)
    block = (place_y + turn * (index // rows)) % (rows_all // rows)
    pool = block * rows + index % rows
    both = jnp.concatenate([partner, partner])
    live = active.astype(jnp.float32)
    both_live = jnp.concatenate([live, live])

    def rows_of(table, first):
        return lax.dynamic_slice_in_dim(table, first, rows)

    start = place_y * rows
    other = (place_y + turn) % (rows_all // rows) * rows
    own_partner = rows_of(both, start)
    pool_partner = jnp.concatenate([own_partner, rows_of(both, other)])
    own_live = rows_of(both_live, start)
    pool_live = jnp.concatenate([own_live, rows_of(both_live, other)])
    near = own_partner[None, :] == pool[:, None]
    far = pool_partner[:, None] == own[None, :]
    match = jnp.where(place_body == 0, near, far).astype(jnp.float32)
    by_row = jnp.where(place_body == 0, own_live, jnp.sum(match * pool_live[:, None], axis=0))
    pick = jnp.concatenate([match] * (lanes // rows), axis=1)
    return pick, by_row


def local(displacement, velocity, material, moduli, density, partner, active):
    planes, rows, cols = displacement.shape[2:]
    count_x, count_y = lax.axis_size("gx"), lax.axis_size("yz")
    place_x, place_y, place_body = lax.axis_index("gx"), lax.axis_index("yz"), lax.axis_index("body")
    route = routes(lax.axis_size("body"), count_x, count_y)
    lanes = 128
    shape = (3, planes, rows, cols)
    d, v, kinds = displacement[0], velocity[0], material[0]
    place = jnp.stack([place_x, jnp.int32(count_x), place_y, jnp.int32(count_y)])
    face = jnp.stack([(place_x == count_x - 1).astype(jnp.int32)])
    smem = pltpu.SMEM

    def passed(block, name):
        return lax.ppermute(block, AXES, route[name])

    def packed(block, kind):
        return jnp.concatenate([block, kind[None].astype(jnp.float32)], axis=0)

    even_x, even_y = place_x % 2 == 0, place_y % 2 == 0
    first_x, last_x = packed(d[:, 0], kinds[0]), packed(d[:, planes - 1], kinds[planes - 1])
    first_y, last_y = packed(d[:, :, 0], kinds[:, 0]), packed(d[:, :, rows - 1], kinds[:, rows - 1])
    sent = [
        jnp.where(even_x, last_x, first_x),
        jnp.where(even_x, first_x, last_x),
        jnp.where(even_y, last_y, first_y),
        jnp.where(even_y, first_y, last_y),
    ]
    corner = kinds[planes - 1, rows - 1 :].astype(jnp.float32)

    def exchange(sent):
        got_e = passed(sent[1][:3], "e")
        got_b = passed(sent[1], "b")
        got_c = passed(sent[2], "c")
        got_d = passed(sent[3], "d")
        got_a = passed(sent[0], "a")
        return got_a, got_b, got_c, got_d, got_e

    got = exchange(sent)
    corner = passed(corner, "corner")
    pick, by_row = contact_tables(partner, active, place_body, place_y, rows, rows * count_y, lanes)
    by_node = jnp.broadcast_to(by_row[:, None], (rows, cols))

    u, w, el, kick = call(
        prepare_kernel,
        [vmem(shape), vmem(shape), vmem(shape[1:]), vmem(shape[1:])],
        [d, v, kinds, moduli, density, place],
        [pltpu.VMEM] * 3 + [smem] * 3,
        flops=8_000_000, moved=0,
    )
    kx, ky, kz, xlow, xhigh, ylow, yhigh, push_scale = call(
        stiffness_kernel,
        [vmem(shape[1:])] * 3 + [vmem((rows, cols))] * 2 + [vmem((planes, cols))] * 2 + [vmem((rows, cols))],
        [el, kick, *got[:4], corner, moduli, place, by_node],
        [None] * 7 + [smem] * 2 + [None],
    )
    edges = [xlow, xhigh, ylow, yhigh]
    fixes = []
    for step in range(STEPS):
        scale = U_SCALE if step == 0 else 1.0
        if step:
            got = exchange(sent)
        u, w, y0, y1 = call(
            functools.partial(interior_kernel, step == 0),
            [vmem(shape), vmem(shape), vmem((3, planes, cols)), vmem((3, planes, cols))],
            [u, w, kx, ky, kz, kick, *fixes],
            aliases={0: 0, 1: 1},
            flops=20_000_000,
        )
        (push,) = call(
            functools.partial(contact_kernel, scale),
            [vmem((rows, cols))],
            [sent[1], got[1], got[4], pick, push_scale, face],
            [None] * 5 + [smem],
            scratch=[vmem((cols, lanes))] * 3,
            flops=20_000_000,
        )
        *sent, dx0, dx1, dy0, dy1 = call(
            functools.partial(boundary_kernel, scale),
            [vmem((3, rows, cols))] * 2 + [vmem((3, planes, cols))] * 2
            + [vmem((3, rows, cols))] * 2 + [vmem((3, planes, cols))] * 2,
            [u, y0, y1, *sent, *got[:4], *edges, push, place],
            [None] * 16 + [smem],
        )
        fixes = [dx0, dx1, dy0, dy1]
    d, v, _, _ = call(
        finish_kernel,
        [jax.ShapeDtypeStruct(shape, jnp.float32)] * 2 + [vmem(shape)] * 2,
        [u, w, *fixes],
        aliases={0: 2, 1: 3},
    )
    return d[None], v[None]


def solution(mesh):
    in_specs = (
        P("body", None, "gx", "yz", None),
        P("body", None, "gx", "yz", None),
        P("body", "gx", "yz", None),
        P(),
        P(),
        P(),
        P(),
    )
    out_specs = (P("body", None, "gx", "yz", None), P("body", None, "gx", "yz", None))
    return jax.shard_map(local, mesh=mesh, in_specs=in_specs, out_specs=out_specs, check_vma=False)
```

```python
import functools
import math

import jax
import jax.numpy as jnp
from jax import lax
from jax.experimental import pallas as pl
from jax.experimental.pallas import tpu as pltpu
from jax.sharding import PartitionSpec as P

STEPS = 4
STEP_TIME = 0.2
YIELD_SPAN = 0.5
PENALTY = 4.0
SOFT_WIDTH = 0.1
KERNEL_WIDTH = 1.5

U_SCALE = 1.0 / YIELD_SPAN
W_SCALE = STEP_TIME / YIELD_SPAN
KICK = STEP_TIME * STEP_TIME / YIELD_SPAN
LOG2E = math.log2(math.e)
GAP_SCALE = YIELD_SPAN / SOFT_WIDTH * LOG2E
SPAN = math.sqrt(LOG2E / (2.0 * KERNEL_WIDTH * KERNEL_WIDTH))
PRESSURE_SCALE = PENALTY * SOFT_WIDTH / LOG2E
STIFF = 0.25 * YIELD_SPAN
TOP = 2.0**126

AXES = ("body", "gx", "yz")
VMEM_LIMIT = 48 * 1024 * 1024


def vmem(shape):
    return pltpu.VMEM(shape, jnp.float32)


def call(kernel, outs, args, spaces=None, aliases=None, scratch=(), flops=0, moved=0, hbm_outs=0):
    spaces = spaces or [None] * len(args)
    specs, placed = [], []
    for arg, space in zip(args, spaces):
        if space is None:
            placed.append(pltpu.with_memory_space_constraint(arg, pltpu.VMEM))
            specs.append(pl.BlockSpec(memory_space=pltpu.VMEM))
        else:
            placed.append(pltpu.with_memory_space_constraint(arg, space) if space == pltpu.HBM else arg)
            specs.append(pl.BlockSpec(memory_space=space))
    return pl.pallas_call(
        kernel,
        out_shape=outs,
        in_specs=specs,
        out_specs=[
            pl.BlockSpec(memory_space=pl.ANY if n < hbm_outs else getattr(out, "memory_space", pltpu.VMEM))
            for n, out in enumerate(outs)
        ],
        input_output_aliases=aliases or {},
        scratch_shapes=list(scratch),
        compiler_params=pltpu.CompilerParams(vmem_limit_bytes=VMEM_LIMIT),
        cost_estimate=pl.CostEstimate(flops=flops, bytes_accessed=moved, transcendentals=0),
    )(*placed)


def pack_kernel(
    d_ref, mat_ref, partner_ref, place_ref, sa_ref, sb_ref, sc_ref, sd_ref, inverse_ref,
    plane_ref, rows_ref, kinds_ref, sems,
):
    planes, rows, cols = mat_ref.shape
    ia, ib, jc, jd = links(place_ref, planes, rows)
    tile = rows_ref.shape[3]
    tile_c, tile_d = jc // tile * tile, jd // tile * tile
    copies = []
    for n, (ref, i) in enumerate(((sa_ref, ia), (sb_ref, ib))):
        copies.append(pltpu.make_async_copy(d_ref.at[:, i], ref.at[0:3], sems.at[n]))
        copies.append(pltpu.make_async_copy(mat_ref.at[i], plane_ref.at[n], sems.at[2 + n]))
    for n, at in enumerate((tile_c, tile_d)):
        some = pl.ds(pl.multiple_of(at, tile), tile)
        copies.append(pltpu.make_async_copy(d_ref.at[:, :, some], rows_ref.at[n], sems.at[4 + n]))
        copies.append(pltpu.make_async_copy(mat_ref.at[:, some], kinds_ref.at[n], sems.at[6 + n]))
    for copy in copies:
        copy.start()

    @pl.loop(0, partner_ref.shape[0], unroll=8)
    def _(b):
        inverse_ref[partner_ref[b]] = b

    for copy in copies:
        copy.wait()
    sa_ref[3] = plane_ref[0].astype(jnp.float32)
    sb_ref[3] = plane_ref[1].astype(jnp.float32)
    for n, (ref, j) in enumerate(((sc_ref, jc - tile_c), (sd_ref, jd - tile_d))):
        for i in range(planes):
            for c in range(3):
                ref[c, i : i + 1] = rows_ref[n, c, i, pl.ds(j, 1)]
            ref[3, i : i + 1] = kinds_ref[n, i, pl.ds(j, 1)].astype(jnp.float32)


def links(place_ref, planes, rows):
    ia = jnp.where(place_ref[0] % 2 == 0, planes - 1, 0)
    jc = jnp.where(place_ref[2] % 2 == 0, rows - 1, 0)
    return ia, planes - 1 - ia, jc, rows - 1 - jc


def prepare_kernel(
    d_ref, v_ref, mat_ref, moduli_ref, density_ref, partner_ref, inverse_ref, active_ref, place_ref,
    u_ref, w_ref, kx_ref, ky_ref, kz_ref, kick_ref, row_kick_ref, high_ky_ref, push_ref, yc_ref, yd_ref,
    pick_ref, half_ref, chosen_ref, kinds_ref, turned_ref, slot_ref, sems,
):
    planes, rows, cols = kinds_ref.shape
    last_x = place_ref[0] == place_ref[1] - 1
    last_y = place_ref[2] == place_ref[3] - 1
    row = lax.broadcasted_iota(jnp.int32, (rows, cols), 0)
    col = lax.broadcasted_iota(jnp.int32, (rows, cols), 1)
    inside = (col < cols - 1) & ((row < rows - 1) | jnp.logical_not(last_y))

    def copies(i):
        return (
            pltpu.make_async_copy(d_ref.at[:, i], u_ref.at[:, i], sems.at[0, i]),
            pltpu.make_async_copy(mat_ref.at[i], kinds_ref.at[i], sems.at[1, i]),
            pltpu.make_async_copy(v_ref.at[:, i], w_ref.at[:, i], sems.at[2, i]),
        )

    for i in range(planes):
        for copy in copies(i):
            copy.start()

    body, blocks = place_ref[4], place_ref[3]
    start = place_ref[2] * rows
    other = jnp.where(body == 0, place_ref[2] + 1, place_ref[2] + blocks - 1) % blocks * rows

    def met(q):
        return jnp.where(body == 0, inverse_ref[q], partner_ref[q])

    def arrive(q, slot):
        r = met(other + q) - start
        here = (r >= 0) & (r < rows)
        slot_ref[jnp.where(here, r, rows)] = rows + slot
        return slot + here.astype(jnp.int32)

    lax.fori_loop(0, rows, arrive, jnp.int32(0), unroll=4)
    lane = lax.broadcasted_iota(jnp.int32, (1, turned_ref.shape[2]), 1)

    def leave(r, count):
        q = jnp.where(body == 0, partner_ref[start + r], inverse_ref[start + r])
        beside = (q >= start) & (q < start + rows)
        whole = jnp.where(beside, q - start, rows + q - other)
        half = jnp.where(beside, q - start, slot_ref[r])
        for n in range(turned_ref.shape[1] // rows):
            turned_ref[0, pl.ds(n * rows + r, 1)] = jnp.where(lane == whole, 1.0, 0.0)
            turned_ref[1, pl.ds(n * rows + r, 1)] = jnp.where(lane == half, 1.0, 0.0)
        live = active_ref[jnp.where(body == 0, start + r, q)]
        push_ref[pl.ds(r, 1)] = jnp.where(lane[:, :cols] >= 0, live.astype(jnp.float32) * (-PRESSURE_SCALE), 0.0)
        chosen_ref[jnp.where(beside, rows, count)] = r
        return count + 1 - beside.astype(jnp.int32)

    lax.fori_loop(0, rows, leave, jnp.int32(0), unroll=4)
    pick_ref[...] = turned_ref[0].T
    half_ref[...] = turned_ref[1].T[: half_ref.shape[0]]

    for copy in copies(0):
        copy.wait()

    def elements(i):
        kinds = kinds_ref[i]
        stiff = jnp.zeros((rows, cols), jnp.float32)
        mass = jnp.ones((rows, cols), jnp.float32)
        for m in range(moduli_ref.shape[0]):
            hit = kinds == m
            stiff = jnp.where(hit, moduli_ref[m] * STIFF, stiff)
            mass = jnp.where(hit, density_ref[m], mass)
        keep = inside & ((i < planes - 1) | jnp.logical_not(last_x))
        kick = KICK / mass
        kick_ref[i] = kick
        row_kick_ref[0, pl.ds(i, 1)] = kick[0:1]
        row_kick_ref[1, pl.ds(i, 1)] = kick[rows - 1 : rows]
        return jnp.where(keep, stiff, 0.0)

    even_y = place_ref[2] % 2 == 0

    def plane(i, earlier, carried, ahead):
        here = elements(i)
        s = here + pltpu.roll(here, 1, 1)
        both = here + earlier
        kx = s + rows_behind(s, row)
        ky = both + pltpu.roll(both, 1, 1)
        kz = both + rows_behind(both, row)
        high_ky_ref[pl.ds(i, 1)] = ky[rows - 1 : rows]
        ky = jnp.where(row < rows - 1, ky, 0.0)
        kx_ref[i], ky_ref[i], kz_ref[i] = kx, ky, kz
        pulls = []
        for c in range(3):
            pulls.append(advance_plane(
                c, i, u_ref[c, i] * U_SCALE, ahead and u_ref[c, i + 1] * U_SCALE, w_ref[c, i] * W_SCALE, carried[c],
                kx, ky, kz, kick_ref[i], u_ref, w_ref, yc_ref, yd_ref, even_y,
            ))
        return here, pulls

    def step(i, state):
        for copy in copies(i + 1):
            copy.wait()
        here, pulls = plane(i, state[0], state[1:], True)
        return (here, *pulls)

    zero = jnp.zeros((rows, cols), jnp.float32)
    state = lax.fori_loop(0, planes - 1, step, (zero,) * 4, unroll=math.gcd(3, planes - 1))
    plane(planes - 1, state[0], state[1:], False)
    push_ref[...] = push_ref[...] * kick_ref[planes - 1]


def rows_behind(value, row, first=0.0):
    return jnp.where(row == 0, first, pltpu.roll(value, 1, 0))


def edge_kernel(
    sa_ref, sb_ref, sc_ref, sd_ref, ra_ref, rb_ref, rc_ref, rd_ref, corner_ref,
    kick_ref, row_kick_ref, high_ky_ref, kx_in, ky_in, kz_in, moduli_ref, place_ref,
    kx_ref, ky_ref, kz_ref, ka_ref, kb_ref, kc_ref, kd_ref, ea_ref, eb_ref, ec_ref, ed_ref,
):
    planes, rows, cols = kick_ref.shape
    even_x, even_y = place_ref[0] % 2 == 0, place_ref[2] % 2 == 0
    inner_x, inner_y = place_ref[0] > 0, place_ref[2] > 0
    last_x = place_ref[0] == place_ref[1] - 1
    last_y = place_ref[2] == place_ref[3] - 1
    row = lax.broadcasted_iota(jnp.int32, (rows, cols), 0)
    plane = lax.broadcasted_iota(jnp.int32, (planes, cols), 0)

    def looked_up(kinds, keep):
        stiff = jnp.zeros(kinds.shape, jnp.float32)
        for m in range(moduli_ref.shape[0]):
            stiff = jnp.where(kinds == m, moduli_ref[m] * STIFF, stiff)
        col = lax.broadcasted_iota(jnp.int32, kinds.shape, 1)
        return jnp.where((col < cols - 1) & keep, stiff, 0.0)

    def with_behind(value):
        return value + pltpu.roll(value, 1, 1)

    below_x = looked_up(
        jnp.where(even_x, rb_ref[3], ra_ref[3]), inner_x & ((row < rows - 1) | jnp.logical_not(last_y))
    )
    below_y = looked_up(
        jnp.where(even_y, rd_ref[3], rc_ref[3]), inner_y & ((plane < planes - 1) | jnp.logical_not(last_x))
    )
    corner = looked_up(corner_ref[...], inner_x & inner_y)
    s_x, s_y, s_corner = with_behind(below_x), with_behind(below_y), with_behind(corner)

    x_low = kick_ref[0] * (s_x + rows_behind(s_x, row, s_corner))
    y_low = row_kick_ref[0] * (s_y + rows_behind(s_y, plane, s_corner))
    plane_ky = jnp.where(row < rows - 1, s_x, 0.0)
    plane_kz = below_x + rows_behind(below_x, row, corner)
    rows_kx = jnp.where(plane < planes - 1, s_y, 0.0)
    rows_kz = below_y + rows_behind(below_y, plane)

    ky_ref[0] += plane_ky
    kz_ref[0] += plane_kz
    for i in range(planes):
        kx_ref[i, 0:1] += s_y[i : i + 1]
        kz_ref[i, 0:1] += rows_kz[i : i + 1]
    x_high = kick_ref[planes - 1] * kx_ref[planes - 1]
    y_high = (high_ky_ref[...] + jnp.where(plane == 0, s_x[rows - 1 : rows], 0.0)) * row_kick_ref[1]
    ka_ref[...] = jnp.where(even_x, x_high, x_low)
    kb_ref[...] = jnp.where(even_x, x_low, x_high)
    kc_ref[...] = jnp.where(even_y, y_high, y_low)
    kd_ref[...] = jnp.where(even_y, y_low, y_high)

    for c in range(3):
        u = jnp.where(even_x, sb_ref[c], sa_ref[c]) * U_SCALE
        pull_y = plane_ky * jnp.tanh(pltpu.roll(u, rows - 1, 0) - u)
        pull_z = plane_kz * jnp.tanh(pltpu.roll(u, cols - 1, 1) - u)
        extra = kick_ref[0] * (pull_y - pltpu.roll(pull_y, 1, 0) + (pull_z - pltpu.roll(pull_z, 1, 1)))
        ea_ref[c] = jnp.where(even_x, 0.0, extra)
        eb_ref[c] = jnp.where(even_x, extra, 0.0)
        u = jnp.where(even_y, sd_ref[c], sc_ref[c]) * U_SCALE
        pull_x = rows_kx * jnp.tanh(pltpu.roll(u, planes - 1, 0) - u)
        pull_z = rows_kz * jnp.tanh(pltpu.roll(u, cols - 1, 1) - u)
        extra = row_kick_ref[0] * (pull_x - pltpu.roll(pull_x, 1, 0) + (pull_z - pltpu.roll(pull_z, 1, 1)))
        ec_ref[c] = jnp.where(even_y, 0.0, extra)
        ed_ref[c] = jnp.where(even_y, extra, 0.0)


def interior_kernel(
    u_in, w_in, kx_ref, ky_ref, kz_ref, kick_ref, da_ref, db_ref, dc_ref, dd_ref, place_ref,
    u_ref, w_ref, yc_ref, yd_ref,
):
    patch(u_ref, w_ref, da_ref, db_ref, dc_ref, dd_ref, place_ref)
    advance(u_ref, w_ref, kx_ref, ky_ref, kz_ref, kick_ref, yc_ref, yd_ref, place_ref)


def advance(u_ref, w_ref, kx_ref, ky_ref, kz_ref, kick_ref, yc_ref, yd_ref, place_ref):
    _, planes, rows, cols = u_ref.shape
    even_y = place_ref[2] % 2 == 0

    def plane(i, carried, ahead):
        return tuple(
            advance_plane(
                c, i, u_ref[c, i], ahead and u_ref[c, i + 1], w_ref[c, i], carried[c],
                kx_ref[i], ky_ref[i], kz_ref[i], kick_ref[i], u_ref, w_ref, yc_ref, yd_ref, even_y,
            )
            for c in range(3)
        )

    zero = jnp.zeros((rows, cols), jnp.float32)
    carried = lax.fori_loop(
        0, planes - 1, lambda i, carried: plane(i, carried, True), (zero,) * 3, unroll=math.gcd(3, planes - 1)
    )
    plane(planes - 1, carried, False)


def advance_plane(c, i, here, ahead, w, carried, kx, ky, kz, kick, u_ref, w_ref, yc_ref, yd_ref, even_y):
    rows, cols = here.shape
    force = -carried
    pull_x = None
    if ahead is not False:
        pull_x = kx * jnp.tanh(ahead - here)
        force = force + pull_x
    pull_y = ky * jnp.tanh(pltpu.roll(here, rows - 1, 0) - here)
    force = force + (pull_y - pltpu.roll(pull_y, 1, 0))
    pull_z = kz * jnp.tanh(pltpu.roll(here, cols - 1, 1) - here)
    force = force + (pull_z - pltpu.roll(pull_z, 1, 1))
    w = w + kick * force
    u = here + w
    w_ref[c, i] = w
    u_ref[c, i] = u
    first, last = u[0:1], u[rows - 1 : rows]
    yc_ref[c, pl.ds(i, 1)] = jnp.where(even_y, last, first)
    yd_ref[c, pl.ds(i, 1)] = jnp.where(even_y, first, last)
    return pull_x


def patch(u_ref, w_ref, da_ref, db_ref, dc_ref, dd_ref, place_ref):
    _, planes, rows, cols = u_ref.shape
    even_x, even_y = place_ref[0] % 2 == 0, place_ref[2] % 2 == 0
    tile = math.gcd(8, rows)
    row = lax.broadcasted_iota(jnp.int32, (tile, cols), 0)
    for c in range(3):
        da, db, dc, dd = da_ref[c], db_ref[c], dc_ref[c], dd_ref[c]
        x_low, x_high = jnp.where(even_x, db, da), jnp.where(even_x, da, db)
        y_low, y_high = jnp.where(even_y, dd, dc), jnp.where(even_y, dc, dd)
        for ref in (u_ref, w_ref):
            ref[c, 0] += x_low
            ref[c, planes - 1] += x_high
            for i in range(planes):
                ref[c, i, 0:tile] += jnp.where(row == 0, y_low[i : i + 1], 0.0)
                ref[c, i, rows - tile : rows] += jnp.where(row == tile - 1, y_high[i : i + 1], 0.0)


def contact_kernel(
    scale, own_ref, near_ref, far_ref, pick_ref, push_ref, face_ref,
    out_ref, fx_ref, fp_ref, fy_ref, fz_ref,
):
    rows, cols = out_ref.shape
    lanes = pick_ref.shape[1]
    parts = lanes // rows
    deep = cols // parts
    is_face = face_ref[0] != 0

    @pl.when(jnp.logical_not(is_face))
    def _():
        out_ref[...] = jnp.zeros_like(out_ref)

    @pl.when(is_face)
    def _():
        pick = pick_ref[...]

        def matched(c):
            pool = jnp.concatenate([near_ref[c], far_ref[c]], axis=0)
            return lax.dot_general(
                pool, pick, (((0,), (0,)), ((), ())),
                precision=lax.Precision.HIGHEST, preferred_element_type=jnp.float32,
            )

        def own(c):
            turned = own_ref[c].T
            return jnp.concatenate([turned[h * deep : (h + 1) * deep] for h in range(parts)], axis=1)

        gap = scale * GAP_SCALE
        along = scale * YIELD_SPAN * SPAN
        fx = matched(0) * gap
        fx_ref[...] = fx
        fp_ref[...] = jnp.exp2(fx)
        fy_ref[...] = matched(1) * along
        spot = lax.broadcasted_iota(jnp.int32, (cols, lanes), 0).astype(jnp.float32)
        fz_ref[...] = matched(2) * along + spot * SPAN
        lane = lax.broadcasted_iota(jnp.int32, (deep, lanes), 1)
        depth = lax.broadcasted_iota(jnp.int32, (deep, lanes), 0)
        mine = (depth + lane // rows * deep).astype(jnp.float32)
        ox = own(0) * gap
        op = jnp.exp2(ox)
        oy = own(1) * along
        oz = own(2) * along + mine * SPAN

        def term(m, total):
            at = pl.ds(m, 1)
            dy = oy - fy_ref[at]
            dz = oz - fz_ref[at]
            weight = jnp.exp2(-(dy * dy + dz * dz))
            soft = jnp.maximum(ox + fx_ref[at], jnp.log2(1.0 + jnp.minimum(op * fp_ref[at], TOP)))
            return total + weight * soft

        total = lax.fori_loop(0, cols, term, jnp.zeros((deep, lanes), jnp.float32), unroll=math.gcd(16, cols))
        turned = jnp.concatenate([total[:, h * rows : (h + 1) * rows] for h in range(parts)], axis=0)
        out_ref[...] = turned.T * push_ref[...]


def link_moves(scale, extra, sent, got, edges, push_ref, c):
    moves = []
    for n in range(4):
        stretch = got[n][c] - sent[n][c]
        if scale != 1.0:
            stretch = stretch * scale
        move = edges[n][...] * jnp.tanh(stretch)
        moves.append(move + extra[n][c] if extra else move)
    if c == 0:
        moves[1] = moves[1] + push_ref[...]
    return moves


def boundary_kernel(scale, n_extra, *refs):
    extra, refs = refs[:n_extra], refs[n_extra:]
    u_ref, yc_ref, yd_ref, *refs = refs
    sent, got, edges, refs = refs[:4], refs[4:8], refs[8:12], refs[12:]
    (push_ref, place_ref, chosen_ref, na_ref, nb_ref, nc_ref, nd_ref, ne_ref,
     da_ref, db_ref, dc_ref, dd_ref) = refs
    _, planes, rows, cols = u_ref.shape
    even_x, even_y = place_ref[0] % 2 == 0, place_ref[2] % 2 == 0
    row = lax.broadcasted_iota(jnp.int32, (rows, cols), 0)
    plane = lax.broadcasted_iota(jnp.int32, (planes, cols), 0)

    def ends(value, index, low, high):
        value = jnp.where(index == 0, value + low, value)
        return jnp.where(index == value.shape[0] - 1, value + high, value)

    for c in range(3):
        da, db, dc, dd = link_moves(scale, extra, sent, got, edges, push_ref, c)
        da_ref[c], db_ref[c], dc_ref[c], dd_ref[c] = da, db, dc, dd
        x_low, x_high = jnp.where(even_x, db, da), jnp.where(even_x, da, db)
        y_low, y_high = jnp.where(even_y, dd, dc), jnp.where(even_y, dc, dd)
        low = u_ref[c, 0] + x_low
        low = ends(low, row, y_low[0:1], y_high[0:1])
        high = u_ref[c, planes - 1] + x_high
        high = ends(high, row, y_low[planes - 1 : planes], y_high[planes - 1 : planes])
        na_ref[c], nb_ref[c] = jnp.where(even_x, high, low), jnp.where(even_x, low, high)
        for new, rows_ref, move, at_even in ((nc_ref, yc_ref, dc, rows - 1), (nd_ref, yd_ref, dd, 0)):
            at_odd = rows - 1 - at_even
            side_low = jnp.where(even_y, x_low[at_even : at_even + 1], x_low[at_odd : at_odd + 1])
            side_high = jnp.where(even_y, x_high[at_even : at_even + 1], x_high[at_odd : at_odd + 1])
            new[c] = ends(rows_ref[c] + move, plane, side_low, side_high)
    for r in range(ne_ref.shape[1]):
        at = chosen_ref[r]
        for c in range(3):
            ne_ref[c, r : r + 1] = nb_ref[c, pl.ds(at, 1)]


def finish_kernel(*refs):
    u_in, w_in, *refs = refs
    sent, got, edges, refs = refs[:4], refs[4:8], refs[8:12], refs[12:]
    push_ref, place_ref, d_ref, v_ref, u_ref, w_ref, da_ref, db_ref, dc_ref, dd_ref, sems = refs
    planes = u_in.shape[1]
    for c in range(3):
        da_ref[c], db_ref[c], dc_ref[c], dd_ref[c] = link_moves(1.0, (), sent, got, edges, push_ref, c)
    patch(u_ref, w_ref, da_ref, db_ref, dc_ref, dd_ref, place_ref)

    def copies(i):
        return (
            pltpu.make_async_copy(u_ref.at[:, i], d_ref.at[:, i], sems.at[0, i]),
            pltpu.make_async_copy(w_ref.at[:, i], v_ref.at[:, i], sems.at[1, i]),
        )

    for i in range(planes):
        for c in range(3):
            u_ref[c, i] = u_ref[c, i] * (1.0 / U_SCALE)
            w_ref[c, i] = w_ref[c, i] * (1.0 / W_SCALE)
        for copy in copies(i):
            copy.start()
    for i in range(planes):
        for copy in copies(i):
            copy.wait()


def routes(count_body, count_x, count_y):
    def number(b, g, y):
        return (b * count_x + g) * count_y + y

    every = [(b, g, y) for b in range(count_body) for g in range(count_x) for y in range(count_y)]

    def pairs(target):
        return [(number(*at), number(*target(*at))) for at in every]

    def outer_x(b, g, y):
        if g in (0, count_x - 1):
            return 1 - b, g, y
        return b, (g + 1 if g % 2 else g - 1), y

    return {
        "a": pairs(lambda b, g, y: (b, g ^ 1, y)),
        "b": pairs(outer_x),
        "c": pairs(lambda b, g, y: (b, g, y ^ 1)),
        "d": pairs(lambda b, g, y: (b, g, (y + 1 if y % 2 else y - 1) % count_y)),
        "e": pairs(lambda b, g, y: (1 - b, g, (y - 1 if b else y + 1) % count_y)),
        "corner": pairs(lambda b, g, y: (b, (g + 1) % count_x, (y + 1) % count_y)),
    }


def local(displacement, velocity, material, moduli, density, partner, active):
    planes, rows, cols = displacement.shape[2:]
    count_x, count_y = lax.axis_size("gx"), lax.axis_size("yz")
    place_x, place_y, place_body = lax.axis_index("gx"), lax.axis_index("yz"), lax.axis_index("body")
    route = routes(lax.axis_size("body"), count_x, count_y)
    lanes = max(cols, 2 * rows)
    tile = math.gcd(8, rows)
    block, face_shape, side = (planes, rows, cols), (rows, cols), (planes, cols)
    state, face3, side3 = (3, *block), (3, *face_shape), (3, *side)
    d, v, kinds = displacement[0], velocity[0], material[0]
    place = jnp.stack([place_x, jnp.int32(count_x), place_y, jnp.int32(count_y), place_body])
    face = jnp.stack([(place_x == count_x - 1).astype(jnp.int32)])
    smem, hbm = pltpu.SMEM, pltpu.HBM

    def exchange(a, b, c, d, e):
        e = lax.ppermute(e, AXES, route["e"])
        b = lax.ppermute(b, AXES, route["b"])
        a = lax.ppermute(a, AXES, route["a"])
        c = lax.ppermute(c, AXES, route["c"])
        d = lax.ppermute(d, AXES, route["d"])
        return [a, b, c, d], e

    corner = lax.ppermute(kinds[planes - 1, rows - 1 :].astype(jnp.float32), AXES, route["corner"])
    *sent, inverse = call(
        pack_kernel,
        [vmem((4, *face_shape))] * 2 + [vmem((4, *side))] * 2 + [pltpu.SMEM(partner.shape, jnp.int32)],
        [d, kinds, partner, place],
        [hbm, hbm, smem, smem],
        scratch=[
            pltpu.VMEM((2, *face_shape), jnp.int32),
            vmem((2, 3, planes, tile, cols)),
            pltpu.VMEM((2, planes, tile, cols), jnp.int32),
            pltpu.SemaphoreType.DMA((8,)),
        ],
    )
    got, got_e = exchange(*sent, sent[1])
    u, w, kx, ky, kz, kick, row_kick, high_ky, push_scale, yc, yd, pick, pick_half, chosen = call(
        prepare_kernel,
        [vmem(state)] * 2 + [vmem(block)] * 4 + [vmem((2, *side)), vmem(side), vmem(face_shape)] + [vmem(side3)] * 2
        + [vmem((lanes, lanes)), vmem((rows + rows // 2, lanes)), pltpu.SMEM((rows + 1,), jnp.int32)],
        [d, v, kinds, moduli, density, partner, inverse, active, place],
        [hbm] * 3 + [smem] * 6,
        scratch=[
            pltpu.VMEM(block, jnp.int32),
            vmem((2, lanes, lanes)),
            pltpu.SMEM((rows + 1,), jnp.int32),
            pltpu.SemaphoreType.DMA((3, planes)),
        ],
        flops=20_000_000,
    )
    for step in range(STEPS):
        first = step == 0
        scale = U_SCALE if first else 1.0
        if not first:
            got, got_e = exchange(*sent, spare)
            u, w, yc, yd = call(
                interior_kernel,
                [vmem(state)] * 2 + [vmem(side3)] * 2,
                [u, w, kx, ky, kz, kick, *moves, place],
                [None] * 10 + [smem],
                aliases={0: 0, 1: 1},
                flops=20_000_000,
            )
        (push,) = call(
            functools.partial(contact_kernel, scale),
            [vmem(face_shape)],
            [sent[1], got[1], got_e, pick if first else pick_half, push_scale, face],
            [None] * 5 + [smem],
            scratch=[vmem((cols, lanes))] * 4,
            flops=20_000_000,
        )
        extra = []
        if first:
            kx, ky, kz, *rest = call(
                edge_kernel,
                [vmem(block)] * 3 + [vmem(face_shape)] * 2 + [vmem(side)] * 2 + [vmem(face3)] * 2 + [vmem(side3)] * 2,
                [*sent, *got, corner, kick, row_kick, high_ky, kx, ky, kz, moduli, place],
                [None] * 15 + [smem] * 2,
                aliases={12: 0, 13: 1, 14: 2},
            )
            edges, extra = rest[:4], rest[4:]
        if step < STEPS - 1:
            *sent, spare, da, db, dc, dd = call(
                functools.partial(boundary_kernel, scale, len(extra)),
                [vmem(face3)] * 2 + [vmem(side3)] * 2 + [vmem((3, rows // 2, cols))]
                + [vmem(face3)] * 2 + [vmem(side3)] * 2,
                [*extra, u, yc, yd, *sent, *got, *edges, push, place, chosen],
                [None] * (16 + len(extra)) + [smem] * 2,
            )
            moves = [da, db, dc, dd]
    d, v, _, _ = call(
        finish_kernel,
        [jax.ShapeDtypeStruct(state, jnp.float32)] * 2 + [vmem(state)] * 2,
        [u, w, *sent, *got, *edges, push, place],
        [None] * 15 + [smem],
        aliases={0: 2, 1: 3},
        scratch=[vmem(face3)] * 2 + [vmem(side3)] * 2 + [pltpu.SemaphoreType.DMA((2, planes))],
        hbm_outs=2,
    )
    return d[None], v[None]


def solution(mesh):
    in_specs = (
        P("body", None, "gx", "yz", None),
        P("body", None, "gx", "yz", None),
        P("body", "gx", "yz", None),
        P(),
        P(),
        P(),
        P(),
    )
    out_specs = (P("body", None, "gx", "yz", None), P("body", None, "gx", "yz", None))
    return jax.shard_map(local, mesh=mesh, in_specs=in_specs, out_specs=out_specs, check_vma=False)
```

```python
import functools
import math

import jax
import jax.numpy as jnp
from jax import lax
from jax.experimental import pallas as pl
from jax.experimental.pallas import tpu as pltpu
from jax.sharding import PartitionSpec as P

STEPS = 4
STEP_TIME = 0.2
YIELD_SPAN = 0.5
PENALTY = 4.0
SOFT_WIDTH = 0.1
KERNEL_WIDTH = 1.5

U_SCALE = 1.0 / YIELD_SPAN
W_SCALE = STEP_TIME / YIELD_SPAN
KICK = STEP_TIME * STEP_TIME / YIELD_SPAN
LOG2E = math.log2(math.e)
GAP_SCALE = YIELD_SPAN / SOFT_WIDTH * LOG2E
SPAN = math.sqrt(LOG2E / (2.0 * KERNEL_WIDTH * KERNEL_WIDTH))
PRESSURE_SCALE = PENALTY * SOFT_WIDTH / LOG2E
STIFF = 0.25 * YIELD_SPAN
BIAS = 32.0

AXES = ("body", "gx", "yz")
VMEM_LIMIT = 48 * 1024 * 1024


def vmem(shape):
    return pltpu.VMEM(shape, jnp.float32)


def call(kernel, outs, args, spaces=None, aliases=None, scratch=(), flops=0, moved=0, hbm_outs=0):
    spaces = spaces or [None] * len(args)
    specs, placed = [], []
    for arg, space in zip(args, spaces):
        if space is None:
            placed.append(pltpu.with_memory_space_constraint(arg, pltpu.VMEM))
            specs.append(pl.BlockSpec(memory_space=pltpu.VMEM))
        else:
            placed.append(pltpu.with_memory_space_constraint(arg, space) if space == pltpu.HBM else arg)
            specs.append(pl.BlockSpec(memory_space=space))
    return pl.pallas_call(
        kernel,
        out_shape=outs,
        in_specs=specs,
        out_specs=[
            pl.BlockSpec(memory_space=pl.ANY if n < hbm_outs else getattr(out, "memory_space", pltpu.VMEM))
            for n, out in enumerate(outs)
        ],
        input_output_aliases=aliases or {},
        scratch_shapes=list(scratch),
        compiler_params=pltpu.CompilerParams(vmem_limit_bytes=VMEM_LIMIT),
        cost_estimate=pl.CostEstimate(flops=flops, bytes_accessed=moved, transcendentals=0),
    )(*placed)


def here_in_mesh():
    return (
        lax.axis_index("gx"), lax.axis_size("gx"), lax.axis_index("yz"), lax.axis_size("yz"), lax.axis_index("body")
    )


def pack_kernel(
    d_ref, mat_ref, sa_ref, sb_ref, sc_ref, sd_ref, corner_ref, plane_ref, rows_ref, kinds_ref, sems,
):
    planes, rows, cols = mat_ref.shape
    place = here_in_mesh()
    ia, ib, jc, jd = links(place, planes, rows)
    tile = rows_ref.shape[3]
    tile_c, tile_d = jc // tile * tile, jd // tile * tile
    copies = []
    for n, (ref, i) in enumerate(((sa_ref, ia), (sb_ref, ib))):
        copies.append(pltpu.make_async_copy(d_ref.at[:, i], ref.at[0:3], sems.at[n]))
        copies.append(pltpu.make_async_copy(mat_ref.at[i], plane_ref.at[n], sems.at[2 + n]))
    for n, at in enumerate((tile_c, tile_d)):
        some = pl.ds(pl.multiple_of(at, tile), tile)
        copies.append(pltpu.make_async_copy(d_ref.at[:, :, some], rows_ref.at[n], sems.at[4 + n]))
        copies.append(pltpu.make_async_copy(mat_ref.at[:, some], kinds_ref.at[n], sems.at[6 + n]))
    for copy in copies:
        copy.start()
    for copy in copies:
        copy.wait()
    kinds_a, kinds_b = plane_ref[0].astype(jnp.float32), plane_ref[1].astype(jnp.float32)
    sa_ref[3], sb_ref[3] = kinds_a, kinds_b
    corner_ref[...] = jnp.where(place[0] % 2 == 0, kinds_a[rows - 1 :], kinds_b[rows - 1 :])
    for n, (ref, j) in enumerate(((sc_ref, jc - tile_c), (sd_ref, jd - tile_d))):
        for i in range(planes):
            for c in range(3):
                ref[c, i : i + 1] = rows_ref[n, c, i, pl.ds(j, 1)]
            ref[3, i : i + 1] = kinds_ref[n, i, pl.ds(j, 1)].astype(jnp.float32)


def links(place, planes, rows):
    ia = jnp.where(place[0] % 2 == 0, planes - 1, 0)
    jc = jnp.where(place[2] % 2 == 0, rows - 1, 0)
    return ia, planes - 1 - ia, jc, rows - 1 - jc


def setup_kernel(
    mat_ref, moduli_ref, density_ref, partner_ref, active_ref,
    kx_ref, ky_ref, kz_ref, kick_ref, row_kick_ref, high_ky_ref, push_ref, pick_ref, half_ref, chosen_ref,
    kinds_ref, turned_ref, inverse_ref, slot_ref, sems,
):
    planes, rows, cols = kinds_ref.shape
    place = here_in_mesh()
    last_x = place[0] == place[1] - 1
    last_y = place[2] == place[3] - 1
    row = lax.broadcasted_iota(jnp.int32, (rows, cols), 0)
    col = lax.broadcasted_iota(jnp.int32, (rows, cols), 1)
    inside = (col < cols - 1) & ((row < rows - 1) | jnp.logical_not(last_y))

    def copy(i):
        return pltpu.make_async_copy(mat_ref.at[i], kinds_ref.at[i], sems.at[i])

    for i in range(planes):
        copy(i).start()

    body, blocks = place[4], place[3]
    start = place[2] * rows
    other = jnp.where(body == 0, place[2] + 1, place[2] + blocks - 1) % blocks * rows

    @pl.when(last_x)
    def _():
        def invert(b, _):
            inverse_ref[partner_ref[b]] = b
            return 0

        lax.fori_loop(0, partner_ref.shape[0], invert, 0, unroll=8)

        def arrive(q, slot):
            q = other + q
            r = jnp.where(body == 0, inverse_ref[q], partner_ref[q]) - start
            here = (r >= 0) & (r < rows)
            slot_ref[jnp.where(here, r, rows)] = rows + slot
            return slot + here.astype(jnp.int32)

        lax.fori_loop(0, rows, arrive, jnp.int32(0), unroll=4)
        lane = lax.broadcasted_iota(jnp.int32, (1, turned_ref.shape[2]), 1)

        def leave(r, count):
            q = jnp.where(body == 0, partner_ref[start + r], inverse_ref[start + r])
            beside = (q >= start) & (q < start + rows)
            whole = jnp.where(beside, q - start, rows + q - other)
            half = jnp.where(beside, q - start, slot_ref[r])
            for n in range(turned_ref.shape[1] // rows):
                turned_ref[0, pl.ds(n * rows + r, 1)] = jnp.where(lane == whole, 1.0, 0.0)
                turned_ref[1, pl.ds(n * rows + r, 1)] = jnp.where(lane == half, 1.0, 0.0)
            live = active_ref[jnp.where(body == 0, start + r, q)].astype(jnp.float32)
            push_ref[pl.ds(r, 1)] = jnp.where(lane[:, :cols] >= 0, live * (-PRESSURE_SCALE), 0.0)
            chosen_ref[jnp.where(beside, rows, count)] = r
            return count + 1 - beside.astype(jnp.int32)

        lax.fori_loop(0, rows, leave, jnp.int32(0), unroll=4)
        pick_ref[...] = turned_ref[0].T
        half_ref[...] = turned_ref[1].T[: half_ref.shape[0]]

    @pl.when(jnp.logical_not(last_x))
    def _():
        push_ref[...] = jnp.zeros_like(push_ref)
        pick_ref[...] = jnp.zeros_like(pick_ref)
        half_ref[...] = jnp.zeros_like(half_ref)

        def any_row(r, _):
            chosen_ref[r] = 0
            return 0

        lax.fori_loop(0, rows + 1, any_row, 0, unroll=8)

    def plane(i, earlier):
        copy(i).wait()
        kinds = kinds_ref[i]
        stiff = jnp.zeros((rows, cols), jnp.float32)
        mass = jnp.ones((rows, cols), jnp.float32)
        for m in range(moduli_ref.shape[0]):
            hit = kinds == m
            stiff = jnp.where(hit, moduli_ref[m] * STIFF, stiff)
            mass = jnp.where(hit, density_ref[m], mass)
        keep = inside & ((i < planes - 1) | jnp.logical_not(last_x))
        here = jnp.where(keep, stiff, 0.0)
        kick = KICK / mass
        kick_ref[i] = kick
        row_kick_ref[0, pl.ds(i, 1)] = kick[0:1]
        row_kick_ref[1, pl.ds(i, 1)] = kick[rows - 1 : rows]
        s = here + pltpu.roll(here, 1, 1)
        both = here + earlier
        ky = both + pltpu.roll(both, 1, 1)
        high_ky_ref[pl.ds(i, 1)] = ky[rows - 1 : rows]
        kx_ref[i] = s + rows_behind(s, row)
        ky_ref[i] = jnp.where(row < rows - 1, ky, 0.0)
        kz_ref[i] = both + rows_behind(both, row)
        return here

    lax.fori_loop(0, planes, plane, jnp.zeros((rows, cols), jnp.float32), unroll=math.gcd(4, planes))
    push_ref[...] = push_ref[...] * kick_ref[planes - 1]


def rows_behind(value, row, first=0.0):
    return jnp.where(row == 0, first, pltpu.roll(value, 1, 0))


def first_kernel(
    d_ref, v_ref, kx_ref, ky_ref, kz_ref, kick_ref, u_ref, w_ref, yc_ref, yd_ref, sems,
):
    _, planes, rows, cols = u_ref.shape
    even_y = lax.axis_index("yz") % 2 == 0

    def copies(i):
        return (
            pltpu.make_async_copy(d_ref.at[:, i], u_ref.at[:, i], sems.at[0, i]),
            pltpu.make_async_copy(v_ref.at[:, i], w_ref.at[:, i], sems.at[1, i]),
        )

    for i in range(planes):
        for copy in copies(i):
            copy.start()
    for copy in copies(0):
        copy.wait()

    def plane(i, carried, ahead):
        if ahead:
            for copy in copies(i + 1):
                copy.wait()
        return tuple(
            advance_plane(
                c, i, u_ref[c, i] * U_SCALE, ahead and u_ref[c, i + 1] * U_SCALE, w_ref[c, i] * W_SCALE, carried[c],
                kx_ref[i], ky_ref[i], kz_ref[i], kick_ref[i], u_ref, w_ref, yc_ref, yd_ref, even_y,
            )
            for c in range(3)
        )

    zero = jnp.zeros((rows, cols), jnp.float32)
    carried = lax.fori_loop(
        0, planes - 1, lambda i, carried: plane(i, carried, True), (zero,) * 3, unroll=math.gcd(3, planes - 1)
    )
    plane(planes - 1, carried, False)


def edge_kernel(
    sa_ref, sb_ref, sc_ref, sd_ref, ra_ref, rb_ref, rc_ref, rd_ref, corner_ref,
    kick_ref, row_kick_ref, high_ky_ref, kx_in, ky_in, kz_in, moduli_ref,
    kx_ref, ky_ref, kz_ref, ka_ref, kb_ref, kc_ref, kd_ref, ex_ref, ey_ref,
):
    planes, rows, cols = kick_ref.shape
    place = here_in_mesh()
    even_x, even_y = place[0] % 2 == 0, place[2] % 2 == 0
    inner_x, inner_y = place[0] > 0, place[2] > 0
    last_x = place[0] == place[1] - 1
    last_y = place[2] == place[3] - 1
    row = lax.broadcasted_iota(jnp.int32, (rows, cols), 0)
    plane = lax.broadcasted_iota(jnp.int32, (planes, cols), 0)

    def looked_up(kinds, keep):
        stiff = jnp.zeros(kinds.shape, jnp.float32)
        for m in range(moduli_ref.shape[0]):
            stiff = jnp.where(kinds == m, moduli_ref[m] * STIFF, stiff)
        col = lax.broadcasted_iota(jnp.int32, kinds.shape, 1)
        return jnp.where((col < cols - 1) & keep, stiff, 0.0)

    def with_behind(value):
        return value + pltpu.roll(value, 1, 1)

    below_x = looked_up(
        jnp.where(even_x, rb_ref[3], ra_ref[3]), inner_x & ((row < rows - 1) | jnp.logical_not(last_y))
    )
    below_y = looked_up(
        jnp.where(even_y, rd_ref[3], rc_ref[3]), inner_y & ((plane < planes - 1) | jnp.logical_not(last_x))
    )
    corner = looked_up(corner_ref[...], inner_x & inner_y)
    s_x, s_y, s_corner = with_behind(below_x), with_behind(below_y), with_behind(corner)

    x_low = kick_ref[0] * (s_x + rows_behind(s_x, row, s_corner))
    y_low = row_kick_ref[0] * (s_y + rows_behind(s_y, plane, s_corner))
    plane_ky = jnp.where(row < rows - 1, s_x, 0.0)
    plane_kz = below_x + rows_behind(below_x, row, corner)
    rows_kx = jnp.where(plane < planes - 1, s_y, 0.0)
    rows_kz = below_y + rows_behind(below_y, plane)

    ky_ref[0] += plane_ky
    kz_ref[0] += plane_kz
    for i in range(planes):
        kx_ref[i, 0:1] += s_y[i : i + 1]
        kz_ref[i, 0:1] += rows_kz[i : i + 1]
    x_high = kick_ref[planes - 1] * kx_ref[planes - 1]
    y_high = (high_ky_ref[...] + jnp.where(plane == 0, s_x[rows - 1 : rows], 0.0)) * row_kick_ref[1]
    ka_ref[...] = jnp.where(even_x, x_high, x_low)
    kb_ref[...] = jnp.where(even_x, x_low, x_high)
    kc_ref[...] = jnp.where(even_y, y_high, y_low)
    kd_ref[...] = jnp.where(even_y, y_low, y_high)

    for c in range(3):
        u = jnp.where(even_x, sb_ref[c], sa_ref[c]) * U_SCALE
        pull_y = plane_ky * jnp.tanh(pltpu.roll(u, rows - 1, 0) - u)
        pull_z = plane_kz * jnp.tanh(pltpu.roll(u, cols - 1, 1) - u)
        ex_ref[c] = kick_ref[0] * (pull_y - pltpu.roll(pull_y, 1, 0) + (pull_z - pltpu.roll(pull_z, 1, 1)))
        u = jnp.where(even_y, sd_ref[c], sc_ref[c]) * U_SCALE
        pull_x = rows_kx * jnp.tanh(pltpu.roll(u, planes - 1, 0) - u)
        pull_z = rows_kz * jnp.tanh(pltpu.roll(u, cols - 1, 1) - u)
        ey_ref[c] = row_kick_ref[0] * (pull_x - pltpu.roll(pull_x, 1, 0) + (pull_z - pltpu.roll(pull_z, 1, 1)))


def interior_kernel(
    u_scale, w_scale, u_in, w_in, kx_ref, ky_ref, kz_ref, kick_ref, xl_ref, xh_ref, yl_ref, yh_ref,
    u_ref, w_ref, yc_ref, yd_ref,
):
    _, planes, rows, cols = u_ref.shape
    even_y = lax.axis_index("yz") % 2 == 0
    for ref in (u_ref, w_ref):
        for c in range(3):
            ref[c, 0] += xl_ref[c]
            ref[c, planes - 1] += xh_ref[c]

    def fixed(ref, c, i):
        return with_sides(ref[c, i], yl_ref[c, pl.ds(i, 1)], yh_ref[c, pl.ds(i, 1)])

    def plane(i, carried, ahead):
        return tuple(
            advance_plane(
                c, i, fixed(u_ref, c, i), ahead and fixed(u_ref, c, i + 1), fixed(w_ref, c, i), carried[c],
                kx_ref[i], ky_ref[i], kz_ref[i], kick_ref[i], u_ref, w_ref, yc_ref, yd_ref, even_y, u_scale, w_scale,
            )
            for c in range(3)
        )

    zero = jnp.zeros((rows, cols), jnp.float32)
    carried = lax.fori_loop(
        0, planes - 1, lambda i, carried: plane(i, carried, True), (zero,) * 3, unroll=math.gcd(3, planes - 1)
    )
    plane(planes - 1, carried, False)


def with_sides(value, low, high):
    rows, cols = value.shape
    tile = math.gcd(8, rows)
    row = lax.broadcasted_iota(jnp.int32, (tile, cols), 0)
    low, high = jnp.where(row == 0, low, 0.0), jnp.where(row == tile - 1, high, 0.0)
    if rows == tile:
        return value + (low + high)
    middle = [value[tile : rows - tile]] if rows > 2 * tile else []
    return jnp.concatenate([value[0:tile] + low, *middle, value[rows - tile :] + high], axis=0)


def advance_plane(
    c, i, here, ahead, w, carried, kx, ky, kz, kick, u_ref, w_ref, yc_ref, yd_ref, even_y, u_scale=1.0, w_scale=1.0
):
    rows, cols = here.shape
    force = -carried
    pull_x = None
    if ahead is not False:
        pull_x = kx * jnp.tanh(ahead - here)
        force = force + pull_x
    pull_y = ky * jnp.tanh(pltpu.roll(here, rows - 1, 0) - here)
    force = force + (pull_y - pltpu.roll(pull_y, 1, 0))
    pull_z = kz * jnp.tanh(pltpu.roll(here, cols - 1, 1) - here)
    force = force + (pull_z - pltpu.roll(pull_z, 1, 1))
    w = w + kick * force
    u = here + w
    if u_scale != 1.0:
        u, w = u * u_scale, w * w_scale
    w_ref[c, i] = w
    u_ref[c, i] = u
    first, last = u[0:1], u[rows - 1 : rows]
    yc_ref[c, pl.ds(i, 1)] = jnp.where(even_y, last, first)
    yd_ref[c, pl.ds(i, 1)] = jnp.where(even_y, first, last)
    return pull_x


def contact_kernel(
    scale, own_ref, near_ref, far_ref, pick_ref, push_ref, out_ref, fp_ref, fy_ref, fz_ref,
):
    rows, cols = out_ref.shape
    lanes = pick_ref.shape[1]
    parts = lanes // rows
    deep = cols // parts
    is_face = lax.axis_index("gx") == lax.axis_size("gx") - 1

    @pl.when(jnp.logical_not(is_face))
    def _():
        out_ref[...] = jnp.zeros_like(out_ref)

    @pl.when(is_face)
    def _():
        pick = pick_ref[...]

        def matched(c):
            pool = jnp.concatenate([near_ref[c], far_ref[c]], axis=0)
            return lax.dot_general(
                pool, pick, (((0,), (0,)), ((), ())),
                precision=lax.Precision.HIGHEST, preferred_element_type=jnp.float32,
            )

        def own(c):
            turned = own_ref[c].T
            return jnp.concatenate([turned[h * deep : (h + 1) * deep] for h in range(parts)], axis=1)

        gap = scale * GAP_SCALE
        along = scale * YIELD_SPAN * SPAN
        fp_ref[...] = jnp.exp2(matched(0) * gap - BIAS / 2.0)
        fy_ref[...] = matched(1) * along
        spot = lax.broadcasted_iota(jnp.int32, (cols, lanes), 0).astype(jnp.float32)
        fz_ref[...] = matched(2) * along + spot * SPAN
        lane = lax.broadcasted_iota(jnp.int32, (deep, lanes), 1)
        depth = lax.broadcasted_iota(jnp.int32, (deep, lanes), 0)
        mine = (depth + lane // rows * deep).astype(jnp.float32)
        op = jnp.exp2(own(0) * gap - BIAS / 2.0)
        oy = own(1) * along
        oz = own(2) * along + mine * SPAN

        def term(m, total):
            at = pl.ds(m, 1)
            dy = oy - fy_ref[at]
            dz = oz - fz_ref[at]
            weight = jnp.exp2(-(dy * dy + dz * dz))
            soft = jnp.log2(op * fp_ref[at] + 2.0**-BIAS) + BIAS
            return total + weight * soft

        total = lax.fori_loop(0, cols, term, jnp.zeros((deep, lanes), jnp.float32), unroll=math.gcd(16, cols))
        turned = jnp.concatenate([total[:, h * rows : (h + 1) * rows] for h in range(parts)], axis=0)
        out_ref[...] = turned.T * push_ref[...]


def last_contact_kernel(
    own_ref, near_ref, far_ref, pick_ref, push_ref, u_ref, w_ref, d_ref, v_ref, out_ref, fp_ref, fy_ref, fz_ref, sems,
):
    copies = [
        pltpu.make_async_copy(u_ref, d_ref, sems.at[0]),
        pltpu.make_async_copy(w_ref, v_ref, sems.at[1]),
    ]
    for copy in copies:
        copy.start()
    contact_kernel(1.0, own_ref, near_ref, far_ref, pick_ref, push_ref, out_ref, fp_ref, fy_ref, fz_ref)
    for copy in copies:
        copy.wait()


def link_moves(scale, extra, sent, got, edges, push_ref, c):
    moves = []
    for n in range(4):
        stretch = got[n][c] - sent[n][c]
        if scale != 1.0:
            stretch = stretch * scale
        moves.append(edges[n][...] * jnp.tanh(stretch))
    if c == 0:
        moves[1] = moves[1] + push_ref[...]
    a, b, c_, d = moves
    even_x, even_y = lax.axis_index("gx") % 2 == 0, lax.axis_index("yz") % 2 == 0
    moves = [jnp.where(even_x, b, a), jnp.where(even_x, a, b), jnp.where(even_y, d, c_), jnp.where(even_y, c_, d)]
    if extra:
        moves[0] = moves[0] + extra[0][c]
        moves[2] = moves[2] + extra[1][c]
    return moves


def boundary_kernel(scale, n_extra, *refs):
    extra, refs = refs[:n_extra], refs[n_extra:]
    u_ref, yc_ref, yd_ref, *refs = refs
    sent, got, edges, refs = refs[:4], refs[4:8], refs[8:12], refs[12:]
    push_ref, chosen_ref, na_ref, nb_ref, nc_ref, nd_ref, ne_ref, xl_ref, xh_ref, yl_ref, yh_ref = refs
    _, planes, rows, cols = u_ref.shape
    even_x, even_y = lax.axis_index("gx") % 2 == 0, lax.axis_index("yz") % 2 == 0
    for c in range(3):
        xl, xh, yl, yh = link_moves(scale, extra, sent, got, edges, push_ref, c)
        xl_ref[c], xh_ref[c], yl_ref[c], yh_ref[c] = xl, xh, yl, yh
        low = with_sides(u_ref[c, 0] + xl, yl[0:1], yh[0:1])
        high = with_sides(u_ref[c, planes - 1] + xh, yl[planes - 1 :], yh[planes - 1 :])
        na_ref[c], nb_ref[c] = jnp.where(even_x, high, low), jnp.where(even_x, low, high)
        first = xl[0:1], xh[0:1]
        last = xl[rows - 1 :], xh[rows - 1 :]
        c_low, c_high = (jnp.where(even_y, y, x) for x, y in zip(first, last))
        d_low, d_high = (jnp.where(even_y, x, y) for x, y in zip(first, last))
        nc_ref[c] = with_sides(yc_ref[c] + jnp.where(even_y, yh, yl), c_low, c_high)
        nd_ref[c] = with_sides(yd_ref[c] + jnp.where(even_y, yl, yh), d_low, d_high)
    for r in range(ne_ref.shape[1]):
        at = chosen_ref[r]
        for c in range(3):
            ne_ref[c, r : r + 1] = nb_ref[c, pl.ds(at, 1)]


def finish_kernel(*refs):
    u_ref, w_ref, _, _, *refs = refs
    sent, got, edges, refs = refs[:4], refs[4:8], refs[8:12], refs[12:]
    push_ref, d_ref, v_ref, planes_ref, rows_ref, sems = refs
    _, planes, rows, cols = u_ref.shape
    tile = rows_ref.shape[4]
    inner = slice(1, planes - 1)
    copies = []
    moves = [link_moves(1.0, (), sent, got, edges, push_ref, c) for c in range(3)]
    results = ((u_ref, d_ref, 1.0 / U_SCALE), (w_ref, v_ref, 1.0 / W_SCALE))
    for n, (ref, out, scale) in enumerate(results):
        for side, at in ((0, 0), (1, rows - tile)):
            for c in range(3):
                fix = moves[c][2 + side] * scale
                for i in range(1, planes - 1):
                    value = ref[c, i, at : at + tile]
                    line = fix[i : i + 1]
                    row = lax.broadcasted_iota(jnp.int32, (tile, cols), 0)
                    rows_ref[n, side, c, i - 1] = value + jnp.where(row == (tile - 1 if side else 0), line, 0.0)
            copies.append(
                pltpu.make_async_copy(
                    rows_ref.at[n, side], out.at[:, inner, at : at + tile], sems.at[len(copies)]
                )
            )
            copies[-1].start()
    for n, (ref, out, scale) in enumerate(results):
        for side, i in ((0, 0), (1, planes - 1)):
            for c in range(3):
                xl, xh, yl, yh = moves[c]
                value = ref[c, i] + (xh if side else xl) * scale
                planes_ref[n, side, c] = with_sides(value, yl[i : i + 1] * scale, yh[i : i + 1] * scale)
            copies.append(pltpu.make_async_copy(planes_ref.at[n, side], out.at[:, i], sems.at[len(copies)]))
            copies[-1].start()
    for copy in copies:
        copy.wait()


def routes(count_body, count_x, count_y):
    def number(b, g, y):
        return (b * count_x + g) * count_y + y

    every = [(b, g, y) for b in range(count_body) for g in range(count_x) for y in range(count_y)]

    def pairs(target):
        return [(number(*at), number(*target(*at))) for at in every]

    def outer_x(b, g, y):
        if g in (0, count_x - 1):
            return 1 - b, g, y
        return b, (g + 1 if g % 2 else g - 1), y

    return {
        "a": pairs(lambda b, g, y: (b, g ^ 1, y)),
        "b": pairs(outer_x),
        "c": pairs(lambda b, g, y: (b, g, y ^ 1)),
        "d": pairs(lambda b, g, y: (b, g, (y + 1 if y % 2 else y - 1) % count_y)),
        "e": pairs(lambda b, g, y: (1 - b, g, (y - 1 if b else y + 1) % count_y)),
        "corner": pairs(lambda b, g, y: (b, (g + 1) % count_x, (y + 1) % count_y)),
    }


def local(displacement, velocity, material, moduli, density, partner, active):
    planes, rows, cols = displacement.shape[2:]
    route = routes(lax.axis_size("body"), lax.axis_size("gx"), lax.axis_size("yz"))
    lanes = max(cols, 2 * rows)
    tile = math.gcd(8, rows)
    block, face, side = (planes, rows, cols), (rows, cols), (planes, cols)
    state, face3, side3 = (3, *block), (3, *face), (3, *side)
    d, v, kinds = displacement[0], velocity[0], material[0]
    smem, hbm = pltpu.SMEM, pltpu.HBM

    def exchange(a, b, c, d, e):
        e = lax.ppermute(e, AXES, route["e"])
        b = lax.ppermute(b, AXES, route["b"])
        a = lax.ppermute(a, AXES, route["a"])
        c = lax.ppermute(c, AXES, route["c"])
        d = lax.ppermute(d, AXES, route["d"])
        return [a, b, c, d], e

    *sent, corner = call(
        pack_kernel,
        [vmem((4, *face))] * 2 + [vmem((4, *side))] * 2 + [vmem((1, cols))],
        [d, kinds],
        [hbm, hbm],
        scratch=[
            pltpu.VMEM((2, *face), jnp.int32),
            vmem((2, 3, planes, tile, cols)),
            pltpu.VMEM((2, planes, tile, cols), jnp.int32),
            pltpu.SemaphoreType.DMA((8,)),
        ],
    )
    got, got_e = exchange(*sent, sent[1])
    kx, ky, kz, kick, row_kick, high_ky, push_scale, pick, pick_half, chosen = call(
        setup_kernel,
        [vmem(block)] * 4 + [vmem((2, *side)), vmem(side), vmem(face)]
        + [vmem((lanes, lanes)), vmem((rows + rows // 2, lanes)), pltpu.SMEM((rows + 1,), jnp.int32)],
        [kinds, moduli, density, partner, active],
        [hbm] + [smem] * 4,
        scratch=[
            pltpu.VMEM(block, jnp.int32),
            vmem((2, lanes, lanes)),
            pltpu.SMEM(partner.shape, jnp.int32),
            pltpu.SMEM((rows + 1,), jnp.int32),
            pltpu.SemaphoreType.DMA((planes,)),
        ],
        flops=8_000_000,
    )
    pair_scratch = [vmem((cols, lanes))] * 3
    for step in range(STEPS):
        first, last = step == 0, step == STEPS - 1
        scale = U_SCALE if first else 1.0
        if not first:
            got, got_e = exchange(*sent, spare)
            u, w, yc, yd = call(
                functools.partial(interior_kernel, *((1.0 / U_SCALE, 1.0 / W_SCALE) if last else (1.0, 1.0))),
                [vmem(state)] * 2 + [vmem(side3)] * 2,
                [u, w, kx, ky, kz, kick, *moves],
                aliases={0: 0, 1: 1},
                flops=20_000_000,
            )
        meet = [sent[1], got[1], got_e, pick if first else pick_half, push_scale]
        if last:
            d, v, push = call(
                last_contact_kernel,
                [jax.ShapeDtypeStruct(state, jnp.float32)] * 2 + [vmem(face)],
                [*meet, u, w],
                scratch=pair_scratch + [pltpu.SemaphoreType.DMA((2,))],
                hbm_outs=2,
                flops=20_000_000,
            )
            break
        (push,) = call(
            functools.partial(contact_kernel, scale), [vmem(face)], meet, scratch=pair_scratch, flops=20_000_000
        )
        extra = []
        if first:
            corner, push = lax.optimization_barrier((corner, push))
            corner = lax.ppermute(corner, AXES, route["corner"])
            u, w, yc, yd = call(
                first_kernel,
                [vmem(state)] * 2 + [vmem(side3)] * 2,
                [d, v, kx, ky, kz, kick],
                [hbm] * 2 + [None] * 4,
                scratch=[pltpu.SemaphoreType.DMA((2, planes))],
                flops=20_000_000,
            )
            kx, ky, kz, *rest = call(
                edge_kernel,
                [vmem(block)] * 3 + [vmem(face)] * 2 + [vmem(side)] * 2 + [vmem(face3), vmem(side3)],
                [*sent, *got, corner, kick, row_kick, high_ky, kx, ky, kz, moduli],
                [None] * 15 + [smem],
                aliases={12: 0, 13: 1, 14: 2},
            )
            edges, extra = rest[:4], rest[4:]
        *sent, spare, xl, xh, yl, yh = call(
            functools.partial(boundary_kernel, scale, len(extra)),
            [vmem(face3)] * 2 + [vmem(side3)] * 2 + [vmem((3, rows // 2, cols))]
            + [vmem(face3)] * 2 + [vmem(side3)] * 2,
            [*extra, u, yc, yd, *sent, *got, *edges, push, chosen],
            [None] * (16 + len(extra)) + [smem],
        )
        moves = [xl, xh, yl, yh]
    d, v = call(
        finish_kernel,
        [jax.ShapeDtypeStruct(state, jnp.float32)] * 2,
        [u, w, d, v, *sent, *got, *edges, push],
        [None, None, hbm, hbm] + [None] * 13,
        aliases={2: 0, 3: 1},
        scratch=[vmem((2, 2, *face3)), vmem((2, 2, 3, planes - 2, tile, cols)), pltpu.SemaphoreType.DMA((8,))],
        hbm_outs=2,
    )
    return d[None], v[None]


def solution(mesh):
    in_specs = (
        P("body", None, "gx", "yz", None),
        P("body", None, "gx", "yz", None),
        P("body", "gx", "yz", None),
        P(),
        P(),
        P(),
        P(),
    )
    out_specs = (P("body", None, "gx", "yz", None), P("body", None, "gx", "yz", None))
    return jax.shard_map(local, mesh=mesh, in_specs=in_specs, out_specs=out_specs, check_vma=False)
```

```python
import functools
import math

import jax
import jax.numpy as jnp
from jax import lax
from jax.experimental import pallas as pl
from jax.experimental.pallas import tpu as pltpu
from jax.sharding import PartitionSpec as P

STEPS = 4
STEP_TIME = 0.2
YIELD_SPAN = 0.5
PENALTY = 4.0
SOFT_WIDTH = 0.1
KERNEL_WIDTH = 1.5

U_SCALE = 1.0 / YIELD_SPAN
W_SCALE = STEP_TIME / YIELD_SPAN
KICK = STEP_TIME * STEP_TIME / YIELD_SPAN
LOG2E = math.log2(math.e)
GAP_SCALE = YIELD_SPAN / SOFT_WIDTH * LOG2E
SPAN = math.sqrt(LOG2E / (2.0 * KERNEL_WIDTH * KERNEL_WIDTH))
PRESSURE_SCALE = PENALTY * SOFT_WIDTH / LOG2E
STIFF = 0.25 * YIELD_SPAN
BIAS = 32.0

AXES = ("body", "gx", "yz")
VMEM_LIMIT = 48 * 1024 * 1024


def vmem(shape):
    return pltpu.VMEM(shape, jnp.float32)


def call(kernel, outs, args, spaces=None, aliases=None, scratch=(), flops=0, moved=0, hbm_outs=0):
    spaces = spaces or [None] * len(args)
    specs, placed = [], []
    for arg, space in zip(args, spaces):
        if space is None:
            placed.append(pltpu.with_memory_space_constraint(arg, pltpu.VMEM))
            specs.append(pl.BlockSpec(memory_space=pltpu.VMEM))
        else:
            placed.append(pltpu.with_memory_space_constraint(arg, space) if space == pltpu.HBM else arg)
            specs.append(pl.BlockSpec(memory_space=space))
    return pl.pallas_call(
        kernel,
        out_shape=outs,
        in_specs=specs,
        out_specs=[
            pl.BlockSpec(memory_space=pl.ANY if n < hbm_outs else getattr(out, "memory_space", pltpu.VMEM))
            for n, out in enumerate(outs)
        ],
        input_output_aliases=aliases or {},
        scratch_shapes=list(scratch),
        compiler_params=pltpu.CompilerParams(vmem_limit_bytes=VMEM_LIMIT),
        cost_estimate=pl.CostEstimate(flops=flops, bytes_accessed=moved, transcendentals=0),
    )(*placed)


def here_in_mesh():
    return (
        lax.axis_index("gx"), lax.axis_size("gx"), lax.axis_index("yz"), lax.axis_size("yz"), lax.axis_index("body")
    )


def pack_kernel(
    d_ref, mat_ref, sa_ref, sb_ref, sc_ref, sd_ref, se_ref, corner_ref, plane_ref, rows_ref, kinds_ref, sems,
):
    planes, rows, cols = mat_ref.shape
    place = here_in_mesh()
    ia, ib, jc, jd = links(place, planes, rows)
    tile = rows_ref.shape[3]
    tile_c, tile_d = jc // tile * tile, jd // tile * tile
    copies = []
    for n, (ref, i) in enumerate(((sa_ref, ia), (sb_ref, ib))):
        copies.append(pltpu.make_async_copy(d_ref.at[:, i], ref.at[0:3], sems.at[n]))
        copies.append(pltpu.make_async_copy(mat_ref.at[i], plane_ref.at[n], sems.at[2 + n]))
    for n, at in enumerate((tile_c, tile_d)):
        some = pl.ds(pl.multiple_of(at, tile), tile)
        copies.append(pltpu.make_async_copy(d_ref.at[:, :, some], rows_ref.at[n], sems.at[4 + n]))
        copies.append(pltpu.make_async_copy(mat_ref.at[:, some], kinds_ref.at[n], sems.at[6 + n]))
    for copy in copies:
        copy.start()
    for copy in copies:
        copy.wait()
    kinds_a, kinds_b = plane_ref[0].astype(jnp.float32), plane_ref[1].astype(jnp.float32)
    sa_ref[3], sb_ref[3] = kinds_a, kinds_b
    for c in range(3):
        se_ref[c] = sb_ref[c]
    corner_ref[...] = jnp.where(place[0] % 2 == 0, kinds_a[rows - 1 :], kinds_b[rows - 1 :])
    for n, (ref, j) in enumerate(((sc_ref, jc - tile_c), (sd_ref, jd - tile_d))):
        for i in range(planes):
            for c in range(3):
                ref[c, i : i + 1] = rows_ref[n, c, i, pl.ds(j, 1)]
            ref[3, i : i + 1] = kinds_ref[n, i, pl.ds(j, 1)].astype(jnp.float32)


def links(place, planes, rows):
    ia = jnp.where(place[0] % 2 == 0, planes - 1, 0)
    jc = jnp.where(place[2] % 2 == 0, rows - 1, 0)
    return ia, planes - 1 - ia, jc, rows - 1 - jc


def setup_kernel(
    kinds_ref, v_ref, moduli_ref, density_ref, partner_ref, active_ref,
    kx_ref, ky_ref, kz_ref, kick_ref, row_kick_ref, high_ky_ref, push_ref, pick_ref, half_ref, chosen_ref, held_ref,
    turned_ref, inverse_ref, slot_ref, sem,
):
    planes, rows, cols = kinds_ref.shape
    place = here_in_mesh()
    last_x = place[0] == place[1] - 1
    last_y = place[2] == place[3] - 1
    row = lax.broadcasted_iota(jnp.int32, (rows, cols), 0)
    col = lax.broadcasted_iota(jnp.int32, (rows, cols), 1)
    inside = (col < cols - 1) & ((row < rows - 1) | jnp.logical_not(last_y))

    velocities = pltpu.make_async_copy(v_ref, held_ref, sem)
    velocities.start()

    body, blocks = place[4], place[3]
    start = place[2] * rows
    other = jnp.where(body == 0, place[2] + 1, place[2] + blocks - 1) % blocks * rows

    @pl.when(last_x)
    def _():
        def invert(b, _):
            inverse_ref[partner_ref[b]] = b
            return 0

        lax.fori_loop(0, partner_ref.shape[0], invert, 0, unroll=8)

        def arrive(q, slot):
            q = other + q
            r = jnp.where(body == 0, inverse_ref[q], partner_ref[q]) - start
            here = (r >= 0) & (r < rows)
            slot_ref[jnp.where(here, r, rows)] = rows + slot
            return slot + here.astype(jnp.int32)

        lax.fori_loop(0, rows, arrive, jnp.int32(0), unroll=4)
        lane = lax.broadcasted_iota(jnp.int32, (1, turned_ref.shape[2]), 1)

        def leave(r, count):
            q = jnp.where(body == 0, partner_ref[start + r], inverse_ref[start + r])
            beside = (q >= start) & (q < start + rows)
            whole = jnp.where(beside, q - start, rows + q - other)
            half = jnp.where(beside, q - start, slot_ref[r])
            for n in range(turned_ref.shape[1] // rows):
                turned_ref[0, pl.ds(n * rows + r, 1)] = jnp.where(lane == whole, 1.0, 0.0)
                turned_ref[1, pl.ds(n * rows + r, 1)] = jnp.where(lane == half, 1.0, 0.0)
            live = active_ref[jnp.where(body == 0, start + r, q)].astype(jnp.float32)
            push_ref[pl.ds(r, 1)] = jnp.where(lane[:, :cols] >= 0, live * (-PRESSURE_SCALE), 0.0)
            chosen_ref[jnp.where(beside, rows, count)] = r
            return count + 1 - beside.astype(jnp.int32)

        lax.fori_loop(0, rows, leave, jnp.int32(0), unroll=4)
        pick_ref[...] = turned_ref[0].T
        half_ref[...] = turned_ref[1].T[: half_ref.shape[0]]

    @pl.when(jnp.logical_not(last_x))
    def _():
        push_ref[...] = jnp.zeros_like(push_ref)
        pick_ref[...] = jnp.zeros_like(pick_ref)
        half_ref[...] = jnp.zeros_like(half_ref)

        def any_row(r, _):
            chosen_ref[r] = 0
            return 0

        lax.fori_loop(0, rows + 1, any_row, 0, unroll=8)

    def plane(i, earlier):
        kinds = kinds_ref[i]
        stiff = jnp.zeros((rows, cols), jnp.float32)
        mass = jnp.ones((rows, cols), jnp.float32)
        for m in range(moduli_ref.shape[0]):
            hit = kinds == m
            stiff = jnp.where(hit, moduli_ref[m] * STIFF, stiff)
            mass = jnp.where(hit, density_ref[m], mass)
        keep = inside & ((i < planes - 1) | jnp.logical_not(last_x))
        here = jnp.where(keep, stiff, 0.0)
        kick = KICK / mass
        kick_ref[i] = kick
        row_kick_ref[0, pl.ds(i, 1)] = kick[0:1]
        row_kick_ref[1, pl.ds(i, 1)] = kick[rows - 1 : rows]
        s = here + pltpu.roll(here, 1, 1)
        both = here + earlier
        ky = both + pltpu.roll(both, 1, 1)
        high_ky_ref[pl.ds(i, 1)] = ky[rows - 1 : rows]
        kx_ref[i] = s + rows_behind(s, row)
        ky_ref[i] = jnp.where(row < rows - 1, ky, 0.0)
        kz_ref[i] = both + rows_behind(both, row)
        return here

    lax.fori_loop(0, planes, plane, jnp.zeros((rows, cols), jnp.float32), unroll=math.gcd(4, planes))
    push_ref[...] = push_ref[...] * kick_ref[planes - 1]
    velocities.wait()


def rows_behind(value, row, first=0.0):
    return jnp.where(row == 0, first, pltpu.roll(value, 1, 0))


def first_kernel(d_ref, v_ref, kx_ref, ky_ref, kz_ref, kick_ref, u_ref, w_ref, yc_ref, yd_ref):
    _, planes, rows, cols = u_ref.shape
    even_y = lax.axis_index("yz") % 2 == 0

    def plane(i, carried, ahead):
        return tuple(
            advance_plane(
                c, i, d_ref[c, i] * U_SCALE, ahead and d_ref[c, i + 1] * U_SCALE, v_ref[c, i] * W_SCALE, carried[c],
                kx_ref[i], ky_ref[i], kz_ref[i], kick_ref[i], u_ref, w_ref, yc_ref, yd_ref, even_y,
            )
            for c in range(3)
        )

    zero = jnp.zeros((rows, cols), jnp.float32)
    carried = lax.fori_loop(
        0, planes - 1, lambda i, carried: plane(i, carried, True), (zero,) * 3, unroll=math.gcd(3, planes - 1)
    )
    plane(planes - 1, carried, False)


def edge_kernel(
    sa_ref, sb_ref, sc_ref, sd_ref, ra_ref, rb_ref, rc_ref, rd_ref, corner_ref,
    kick_ref, row_kick_ref, high_ky_ref, kx_in, ky_in, kz_in, moduli_ref,
    kx_ref, ky_ref, kz_ref, ka_ref, kb_ref, kc_ref, kd_ref, ex_ref, ey_ref,
):
    planes, rows, cols = kick_ref.shape
    place = here_in_mesh()
    even_x, even_y = place[0] % 2 == 0, place[2] % 2 == 0
    inner_x, inner_y = place[0] > 0, place[2] > 0
    last_x = place[0] == place[1] - 1
    last_y = place[2] == place[3] - 1
    row = lax.broadcasted_iota(jnp.int32, (rows, cols), 0)
    plane = lax.broadcasted_iota(jnp.int32, (planes, cols), 0)

    def looked_up(kinds, keep):
        stiff = jnp.zeros(kinds.shape, jnp.float32)
        for m in range(moduli_ref.shape[0]):
            stiff = jnp.where(kinds == m, moduli_ref[m] * STIFF, stiff)
        col = lax.broadcasted_iota(jnp.int32, kinds.shape, 1)
        return jnp.where((col < cols - 1) & keep, stiff, 0.0)

    def with_behind(value):
        return value + pltpu.roll(value, 1, 1)

    below_x = looked_up(
        jnp.where(even_x, rb_ref[3], ra_ref[3]), inner_x & ((row < rows - 1) | jnp.logical_not(last_y))
    )
    below_y = looked_up(
        jnp.where(even_y, rd_ref[3], rc_ref[3]), inner_y & ((plane < planes - 1) | jnp.logical_not(last_x))
    )
    corner = looked_up(corner_ref[...], inner_x & inner_y)
    s_x, s_y, s_corner = with_behind(below_x), with_behind(below_y), with_behind(corner)

    x_low = kick_ref[0] * (s_x + rows_behind(s_x, row, s_corner))
    y_low = row_kick_ref[0] * (s_y + rows_behind(s_y, plane, s_corner))
    plane_ky = jnp.where(row < rows - 1, s_x, 0.0)
    plane_kz = below_x + rows_behind(below_x, row, corner)
    rows_kx = jnp.where(plane < planes - 1, s_y, 0.0)
    rows_kz = below_y + rows_behind(below_y, plane)

    ky_ref[0] += plane_ky
    kz_ref[0] += plane_kz
    for i in range(planes):
        kx_ref[i, 0:1] += s_y[i : i + 1]
        kz_ref[i, 0:1] += rows_kz[i : i + 1]
    x_high = kick_ref[planes - 1] * kx_ref[planes - 1]
    y_high = (high_ky_ref[...] + jnp.where(plane == 0, s_x[rows - 1 : rows], 0.0)) * row_kick_ref[1]
    ka_ref[...] = jnp.where(even_x, x_high, x_low)
    kb_ref[...] = jnp.where(even_x, x_low, x_high)
    kc_ref[...] = jnp.where(even_y, y_high, y_low)
    kd_ref[...] = jnp.where(even_y, y_low, y_high)

    for c in range(3):
        u = jnp.where(even_x, sb_ref[c], sa_ref[c]) * U_SCALE
        pull_y = plane_ky * jnp.tanh(pltpu.roll(u, rows - 1, 0) - u)
        pull_z = plane_kz * jnp.tanh(pltpu.roll(u, cols - 1, 1) - u)
        ex_ref[c] = kick_ref[0] * (pull_y - pltpu.roll(pull_y, 1, 0) + (pull_z - pltpu.roll(pull_z, 1, 1)))
        u = jnp.where(even_y, sd_ref[c], sc_ref[c]) * U_SCALE
        pull_x = rows_kx * jnp.tanh(pltpu.roll(u, planes - 1, 0) - u)
        pull_z = rows_kz * jnp.tanh(pltpu.roll(u, cols - 1, 1) - u)
        ey_ref[c] = row_kick_ref[0] * (pull_x - pltpu.roll(pull_x, 1, 0) + (pull_z - pltpu.roll(pull_z, 1, 1)))


def interior_kernel(
    u_scale, w_scale, u_in, w_in, kx_ref, ky_ref, kz_ref, kick_ref, xl_ref, xh_ref, yl_ref, yh_ref,
    u_ref, w_ref, yc_ref, yd_ref,
):
    _, planes, rows, cols = u_ref.shape
    even_y = lax.axis_index("yz") % 2 == 0
    for ref in (u_ref, w_ref):
        for c in range(3):
            ref[c, 0] += xl_ref[c]
            ref[c, planes - 1] += xh_ref[c]

    def fixed(ref, c, i):
        return with_sides(ref[c, i], yl_ref[c, pl.ds(i, 1)], yh_ref[c, pl.ds(i, 1)])

    def plane(i, carried, ahead):
        return tuple(
            advance_plane(
                c, i, fixed(u_ref, c, i), ahead and fixed(u_ref, c, i + 1), fixed(w_ref, c, i), carried[c],
                kx_ref[i], ky_ref[i], kz_ref[i], kick_ref[i], u_ref, w_ref, yc_ref, yd_ref, even_y, u_scale, w_scale,
            )
            for c in range(3)
        )

    zero = jnp.zeros((rows, cols), jnp.float32)
    carried = lax.fori_loop(
        0, planes - 1, lambda i, carried: plane(i, carried, True), (zero,) * 3, unroll=math.gcd(3, planes - 1)
    )
    plane(planes - 1, carried, False)


def with_sides(value, low, high):
    rows, cols = value.shape
    tile = math.gcd(8, rows)
    row = lax.broadcasted_iota(jnp.int32, (tile, cols), 0)
    low, high = jnp.where(row == 0, low, 0.0), jnp.where(row == tile - 1, high, 0.0)
    if rows == tile:
        return value + (low + high)
    middle = [value[tile : rows - tile]] if rows > 2 * tile else []
    return jnp.concatenate([value[0:tile] + low, *middle, value[rows - tile :] + high], axis=0)


def advance_plane(
    c, i, here, ahead, w, carried, kx, ky, kz, kick, u_ref, w_ref, yc_ref, yd_ref, even_y, u_scale=1.0, w_scale=1.0
):
    rows, cols = here.shape
    force = -carried
    pull_x = None
    if ahead is not False:
        pull_x = kx * jnp.tanh(ahead - here)
        force = force + pull_x
    pull_y = ky * jnp.tanh(pltpu.roll(here, rows - 1, 0) - here)
    force = force + (pull_y - pltpu.roll(pull_y, 1, 0))
    pull_z = kz * jnp.tanh(pltpu.roll(here, cols - 1, 1) - here)
    force = force + (pull_z - pltpu.roll(pull_z, 1, 1))
    w = w + kick * force
    u = here + w
    if u_scale != 1.0:
        u, w = u * u_scale, w * w_scale
    w_ref[c, i] = w
    u_ref[c, i] = u
    first, last = u[0:1], u[rows - 1 : rows]
    yc_ref[c, pl.ds(i, 1)] = jnp.where(even_y, last, first)
    yd_ref[c, pl.ds(i, 1)] = jnp.where(even_y, first, last)
    return pull_x


def contact_kernel(
    scale, own_ref, near_ref, far_ref, pick_ref, push_ref, out_ref, fp_ref, fy_ref, fz_ref,
):
    rows, cols = out_ref.shape
    lanes = pick_ref.shape[1]
    parts = lanes // rows
    deep = cols // parts
    is_face = lax.axis_index("gx") == lax.axis_size("gx") - 1

    @pl.when(jnp.logical_not(is_face))
    def _():
        out_ref[...] = jnp.zeros_like(out_ref)

    @pl.when(is_face)
    def _():
        pick = pick_ref[...]

        def matched(c):
            pool = jnp.concatenate([near_ref[c], far_ref[c]], axis=0)
            return lax.dot_general(
                pool, pick, (((0,), (0,)), ((), ())),
                precision=lax.Precision.HIGHEST, preferred_element_type=jnp.float32,
            )

        def own(c):
            turned = own_ref[c].T
            return jnp.concatenate([turned[h * deep : (h + 1) * deep] for h in range(parts)], axis=1)

        gap = scale * GAP_SCALE
        along = scale * YIELD_SPAN * SPAN
        fp_ref[...] = jnp.exp2(matched(0) * gap - BIAS / 2.0)
        fy_ref[...] = matched(1) * along
        spot = lax.broadcasted_iota(jnp.int32, (cols, lanes), 0).astype(jnp.float32)
        fz_ref[...] = matched(2) * along + spot * SPAN
        lane = lax.broadcasted_iota(jnp.int32, (deep, lanes), 1)
        depth = lax.broadcasted_iota(jnp.int32, (deep, lanes), 0)
        mine = (depth + lane // rows * deep).astype(jnp.float32)
        op = jnp.exp2(own(0) * gap - BIAS / 2.0)
        oy = own(1) * along
        oz = own(2) * along + mine * SPAN

        def term(m, total):
            at = pl.ds(m, 1)
            dy = oy - fy_ref[at]
            dz = oz - fz_ref[at]
            weight = jnp.exp2(-(dy * dy + dz * dz))
            soft = jnp.log2(op * fp_ref[at] + 2.0**-BIAS) + BIAS
            return total + weight * soft

        total = lax.fori_loop(0, cols, term, jnp.zeros((deep, lanes), jnp.float32), unroll=math.gcd(16, cols))
        turned = jnp.concatenate([total[:, h * rows : (h + 1) * rows] for h in range(parts)], axis=0)
        out_ref[...] = turned.T * push_ref[...]


def last_contact_kernel(
    own_ref, near_ref, far_ref, pick_ref, push_ref, u_ref, w_ref, d_ref, v_ref, out_ref, fp_ref, fy_ref, fz_ref, sems,
):
    copies = [
        pltpu.make_async_copy(u_ref, d_ref, sems.at[0]),
        pltpu.make_async_copy(w_ref, v_ref, sems.at[1]),
    ]
    for copy in copies:
        copy.start()
    contact_kernel(1.0, own_ref, near_ref, far_ref, pick_ref, push_ref, out_ref, fp_ref, fy_ref, fz_ref)
    for copy in copies:
        copy.wait()


def link_moves(scale, extra, sent, got, edges, push_ref, c):
    moves = []
    for n in range(4):
        stretch = got[n][c] - sent[n][c]
        if scale != 1.0:
            stretch = stretch * scale
        moves.append(edges[n][...] * jnp.tanh(stretch))
    if c == 0:
        moves[1] = moves[1] + push_ref[...]
    a, b, c_, d = moves
    even_x, even_y = lax.axis_index("gx") % 2 == 0, lax.axis_index("yz") % 2 == 0
    moves = [jnp.where(even_x, b, a), jnp.where(even_x, a, b), jnp.where(even_y, d, c_), jnp.where(even_y, c_, d)]
    if extra:
        moves[0] = moves[0] + extra[0][c]
        moves[2] = moves[2] + extra[1][c]
    return moves


def boundary_kernel(scale, n_extra, *refs):
    extra, refs = refs[:n_extra], refs[n_extra:]
    u_ref, yc_ref, yd_ref, *refs = refs
    sent, got, edges, refs = refs[:4], refs[4:8], refs[8:12], refs[12:]
    push_ref, chosen_ref, na_ref, nb_ref, nc_ref, nd_ref, ne_ref, xl_ref, xh_ref, yl_ref, yh_ref = refs
    _, planes, rows, cols = u_ref.shape
    even_x, even_y = lax.axis_index("gx") % 2 == 0, lax.axis_index("yz") % 2 == 0
    for c in range(3):
        xl, xh, yl, yh = link_moves(scale, extra, sent, got, edges, push_ref, c)
        xl_ref[c], xh_ref[c], yl_ref[c], yh_ref[c] = xl, xh, yl, yh
        low = with_sides(u_ref[c, 0] + xl, yl[0:1], yh[0:1])
        high = with_sides(u_ref[c, planes - 1] + xh, yl[planes - 1 :], yh[planes - 1 :])
        na_ref[c], nb_ref[c] = jnp.where(even_x, high, low), jnp.where(even_x, low, high)
        first = xl[0:1], xh[0:1]
        last = xl[rows - 1 :], xh[rows - 1 :]
        c_low, c_high = (jnp.where(even_y, y, x) for x, y in zip(first, last))
        d_low, d_high = (jnp.where(even_y, x, y) for x, y in zip(first, last))
        nc_ref[c] = with_sides(yc_ref[c] + jnp.where(even_y, yh, yl), c_low, c_high)
        nd_ref[c] = with_sides(yd_ref[c] + jnp.where(even_y, yl, yh), d_low, d_high)
    for r in range(ne_ref.shape[1]):
        at = chosen_ref[r]
        for c in range(3):
            ne_ref[c, r : r + 1] = nb_ref[c, pl.ds(at, 1)]


def finish_kernel(*refs):
    u_ref, w_ref, _, _, *refs = refs
    sent, got, edges, refs = refs[:4], refs[4:8], refs[8:12], refs[12:]
    push_ref, d_ref, v_ref, planes_ref, rows_ref, sems = refs
    _, planes, rows, cols = u_ref.shape
    tile = rows_ref.shape[4]
    inner = slice(1, planes - 1)
    copies = []
    moves = [link_moves(1.0, (), sent, got, edges, push_ref, c) for c in range(3)]
    results = ((u_ref, d_ref, 1.0 / U_SCALE), (w_ref, v_ref, 1.0 / W_SCALE))
    for n, (ref, out, scale) in enumerate(results):
        for side, at in ((0, 0), (1, rows - tile)):
            for c in range(3):
                fix = moves[c][2 + side] * scale
                for i in range(1, planes - 1):
                    value = ref[c, i, at : at + tile]
                    line = fix[i : i + 1]
                    row = lax.broadcasted_iota(jnp.int32, (tile, cols), 0)
                    rows_ref[n, side, c, i - 1] = value + jnp.where(row == (tile - 1 if side else 0), line, 0.0)
            copies.append(
                pltpu.make_async_copy(
                    rows_ref.at[n, side], out.at[:, inner, at : at + tile], sems.at[len(copies)]
                )
            )
            copies[-1].start()
    for n, (ref, out, scale) in enumerate(results):
        for side, i in ((0, 0), (1, planes - 1)):
            for c in range(3):
                xl, xh, yl, yh = moves[c]
                value = ref[c, i] + (xh if side else xl) * scale
                planes_ref[n, side, c] = with_sides(value, yl[i : i + 1] * scale, yh[i : i + 1] * scale)
            copies.append(pltpu.make_async_copy(planes_ref.at[n, side], out.at[:, i], sems.at[len(copies)]))
            copies[-1].start()
    for copy in copies:
        copy.wait()


def routes(count_body, count_x, count_y):
    def number(b, g, y):
        return (b * count_x + g) * count_y + y

    every = [(b, g, y) for b in range(count_body) for g in range(count_x) for y in range(count_y)]

    def pairs(target):
        return [(number(*at), number(*target(*at))) for at in every]

    def outer_x(b, g, y):
        if g == count_x - 1:
            return 1 - b, g, y
        return (b, (g + 1 if g % 2 else g - 1), y) if g else (b, g, y ^ 1)

    def diagonal(b, g, y):
        if g == count_x - 1:
            return 1 - b, g, (y - 1 if b else y + 1) % count_y
        return b, g, y ^ 1

    return {
        "a": pairs(lambda b, g, y: (b, g ^ 1, y)),
        "b": pairs(outer_x),
        "c": pairs(lambda b, g, y: (b, g, y ^ 1)),
        "d": pairs(lambda b, g, y: (b, g, (y + 1 if y % 2 else y - 1) % count_y)),
        "e": pairs(diagonal),
        "corner": pairs(lambda b, g, y: (b, (g + 1) % count_x, (y + 1) % count_y)),
    }


def local(displacement, velocity, material, moduli, density, partner, active):
    planes, rows, cols = displacement.shape[2:]
    route = routes(lax.axis_size("body"), lax.axis_size("gx"), lax.axis_size("yz"))
    lanes = max(cols, 2 * rows)
    tile = math.gcd(8, rows)
    block, face, side = (planes, rows, cols), (rows, cols), (planes, cols)
    state, face3, side3 = (3, *block), (3, *face), (3, *side)
    d, v, kinds = displacement[0], velocity[0], material[0]
    smem, hbm = pltpu.SMEM, pltpu.HBM

    def passed(block, name):
        return lax.ppermute(block, AXES, route[name])

    *sent, spare, corner = call(
        pack_kernel,
        [vmem((4, *face))] * 2 + [vmem((4, *side))] * 2 + [vmem(face3), vmem((1, cols))],
        [d, kinds],
        [hbm, hbm],
        scratch=[
            pltpu.VMEM((2, *face), jnp.int32),
            vmem((2, 3, planes, tile, cols)),
            pltpu.VMEM((2, planes, tile, cols), jnp.int32),
            pltpu.SemaphoreType.DMA((8,)),
        ],
    )
    got_e = passed(spare, "e")
    got = [passed(block, name) for block, name in zip(sent, "abcd")]
    kx, ky, kz, kick, row_kick, high_ky, push_scale, pick, pick_half, chosen, v = call(
        setup_kernel,
        [vmem(block)] * 4 + [vmem((2, *side)), vmem(side), vmem(face)]
        + [vmem((lanes, lanes)), vmem((rows + rows // 2, lanes)), pltpu.SMEM((rows + 1,), jnp.int32)]
        + [vmem(state)],
        [kinds, v, moduli, density, partner, active],
        [None, hbm] + [smem] * 4,
        scratch=[
            vmem((2, lanes, lanes)),
            pltpu.SMEM(partner.shape, jnp.int32),
            pltpu.SMEM((rows + 1,), jnp.int32),
            pltpu.SemaphoreType.DMA,
        ],
        flops=8_000_000,
    )
    pair_scratch = [vmem((cols, lanes))] * 3
    for step in range(STEPS):
        first, last = step == 0, step == STEPS - 1
        scale = U_SCALE if first else 1.0
        if first:
            u, w, yc, yd = call(
                first_kernel,
                [vmem(state)] * 2 + [vmem(side3)] * 2,
                [d, v, kx, ky, kz, kick],
                flops=20_000_000,
            )
            corner, push_scale, yc = lax.optimization_barrier((corner, push_scale, yc))
            corner = passed(corner, "corner")
        else:
            got_e = passed(spare, "e")
            got = [passed(block, name) for block, name in zip(sent, "abcd")]
            u, w, yc, yd = call(
                functools.partial(interior_kernel, *((1.0 / U_SCALE, 1.0 / W_SCALE) if last else (1.0, 1.0))),
                [vmem(state)] * 2 + [vmem(side3)] * 2,
                [u, w, kx, ky, kz, kick, *moves],
                aliases={0: 0, 1: 1},
                flops=20_000_000,
            )
        meet = [sent[1], got[1], got_e, pick if first else pick_half, push_scale]
        if last:
            d, v, push = call(
                last_contact_kernel,
                [jax.ShapeDtypeStruct(state, jnp.float32)] * 2 + [vmem(face)],
                [*meet, u, w],
                scratch=pair_scratch + [pltpu.SemaphoreType.DMA((2,))],
                hbm_outs=2,
                flops=20_000_000,
            )
            break
        (push,) = call(
            functools.partial(contact_kernel, scale), [vmem(face)], meet, scratch=pair_scratch,
            flops=0 if first else 20_000_000,
        )
        extra = []
        if first:
            kx, ky, kz, *rest = call(
                edge_kernel,
                [vmem(block)] * 3 + [vmem(face)] * 2 + [vmem(side)] * 2 + [vmem(face3), vmem(side3)],
                [*sent, *got, corner, kick, row_kick, high_ky, kx, ky, kz, moduli],
                [None] * 15 + [smem],
                aliases={12: 0, 13: 1, 14: 2},
            )
            edges, extra = rest[:4], rest[4:]
        *sent, spare, xl, xh, yl, yh = call(
            functools.partial(boundary_kernel, scale, len(extra)),
            [vmem(face3)] * 2 + [vmem(side3)] * 2 + [vmem((3, rows // 2, cols))]
            + [vmem(face3)] * 2 + [vmem(side3)] * 2,
            [*extra, u, yc, yd, *sent, *got, *edges, push, chosen],
            [None] * (16 + len(extra)) + [smem],
        )
        moves = [xl, xh, yl, yh]
    d, v = call(
        finish_kernel,
        [jax.ShapeDtypeStruct(state, jnp.float32)] * 2,
        [u, w, d, v, *sent, *got, *edges, push],
        [None, None, hbm, hbm] + [None] * 13,
        aliases={2: 0, 3: 1},
        scratch=[vmem((2, 2, *face3)), vmem((2, 2, 3, planes - 2, tile, cols)), pltpu.SemaphoreType.DMA((8,))],
        hbm_outs=2,
    )
    return d[None], v[None]


def solution(mesh):
    in_specs = (
        P("body", None, "gx", "yz", None),
        P("body", None, "gx", "yz", None),
        P("body", "gx", "yz", None),
        P(),
        P(),
        P(),
        P(),
    )
    out_specs = (P("body", None, "gx", "yz", None), P("body", None, "gx", "yz", None))
    return jax.shard_map(local, mesh=mesh, in_specs=in_specs, out_specs=out_specs, check_vma=False)
```

```python
import functools
import math

import jax
import jax.numpy as jnp
from jax import lax
from jax.experimental import pallas as pl
from jax.experimental.pallas import tpu as pltpu
from jax.sharding import PartitionSpec as P

STEPS = 4
STEP_TIME = 0.2
YIELD_SPAN = 0.5
PENALTY = 4.0
SOFT_WIDTH = 0.1
KERNEL_WIDTH = 1.5

U_SCALE = 1.0 / YIELD_SPAN
W_SCALE = STEP_TIME / YIELD_SPAN
KICK = STEP_TIME * STEP_TIME / YIELD_SPAN
LOG2E = math.log2(math.e)
GAP_SCALE = YIELD_SPAN / SOFT_WIDTH * LOG2E
SPAN = math.sqrt(LOG2E / (2.0 * KERNEL_WIDTH * KERNEL_WIDTH))
PRESSURE_SCALE = PENALTY * SOFT_WIDTH / LOG2E
STIFF = 0.25 * YIELD_SPAN
BIAS = 32.0

AXES = ("body", "gx", "yz")
VMEM_LIMIT = 48 * 1024 * 1024


def vmem(shape):
    return pltpu.VMEM(shape, jnp.float32)


def call(kernel, outs, args, spaces=None, aliases=None, scratch=(), flops=0, moved=0, hbm_outs=0):
    spaces = spaces or [None] * len(args)
    specs, placed = [], []
    for arg, space in zip(args, spaces):
        if space is None:
            placed.append(pltpu.with_memory_space_constraint(arg, pltpu.VMEM))
            specs.append(pl.BlockSpec(memory_space=pltpu.VMEM))
        else:
            placed.append(pltpu.with_memory_space_constraint(arg, space) if space == pltpu.HBM else arg)
            specs.append(pl.BlockSpec(memory_space=space))
    return pl.pallas_call(
        kernel,
        out_shape=outs,
        in_specs=specs,
        out_specs=[
            pl.BlockSpec(memory_space=pl.ANY if n < hbm_outs else getattr(out, "memory_space", pltpu.VMEM))
            for n, out in enumerate(outs)
        ],
        input_output_aliases=aliases or {},
        scratch_shapes=list(scratch),
        compiler_params=pltpu.CompilerParams(vmem_limit_bytes=VMEM_LIMIT),
        cost_estimate=pl.CostEstimate(flops=flops, bytes_accessed=moved, transcendentals=0),
    )(*placed)


def here_in_mesh():
    return (
        lax.axis_index("gx"), lax.axis_size("gx"), lax.axis_index("yz"), lax.axis_size("yz"), lax.axis_index("body")
    )


def pack_kernel(
    d_ref, mat_ref, sa_ref, sb_ref, sc_ref, sd_ref, se_ref, corner_ref, plane_ref, rows_ref, kinds_ref, sems,
):
    planes, rows, cols = mat_ref.shape
    place = here_in_mesh()
    ia, ib, jc, jd = links(place, planes, rows)
    tile = rows_ref.shape[3]
    tile_c, tile_d = jc // tile * tile, jd // tile * tile
    copies = []
    for n, (ref, i) in enumerate(((sa_ref, ia), (sb_ref, ib))):
        copies.append(pltpu.make_async_copy(d_ref.at[:, i], ref.at[0:3], sems.at[n]))
        copies.append(pltpu.make_async_copy(mat_ref.at[i], plane_ref.at[n], sems.at[2 + n]))
    for n, at in enumerate((tile_c, tile_d)):
        some = pl.ds(pl.multiple_of(at, tile), tile)
        copies.append(pltpu.make_async_copy(d_ref.at[:, :, some], rows_ref.at[n], sems.at[4 + n]))
        copies.append(pltpu.make_async_copy(mat_ref.at[:, some], kinds_ref.at[n], sems.at[6 + n]))
    for copy in copies:
        copy.start()
    for copy in copies:
        copy.wait()
    kinds_a, kinds_b = plane_ref[0].astype(jnp.float32), plane_ref[1].astype(jnp.float32)
    sa_ref[3], sb_ref[3] = kinds_a, kinds_b
    for c in range(3):
        se_ref[c] = sb_ref[c]
    corner_ref[...] = jnp.where(place[0] % 2 == 0, kinds_a[rows - 1 :], kinds_b[rows - 1 :])
    for n, (ref, j) in enumerate(((sc_ref, jc - tile_c), (sd_ref, jd - tile_d))):
        for i in range(planes):
            for c in range(3):
                ref[c, i : i + 1] = rows_ref[n, c, i, pl.ds(j, 1)]
            ref[3, i : i + 1] = kinds_ref[n, i, pl.ds(j, 1)].astype(jnp.float32)


def links(place, planes, rows):
    ia = jnp.where(place[0] % 2 == 0, planes - 1, 0)
    jc = jnp.where(place[2] % 2 == 0, rows - 1, 0)
    return ia, planes - 1 - ia, jc, rows - 1 - jc


def setup_kernel(
    kinds_ref, v_ref, moduli_ref, density_ref, partner_ref, active_ref,
    kx_ref, ky_ref, kz_ref, kick_ref, row_kick_ref, high_ky_ref, push_ref, pick_ref, half_ref, chosen_ref, held_ref,
    turned_ref, inverse_ref, slot_ref, sem,
):
    planes, rows, cols = kinds_ref.shape
    place = here_in_mesh()
    last_x = place[0] == place[1] - 1
    last_y = place[2] == place[3] - 1
    row = lax.broadcasted_iota(jnp.int32, (rows, cols), 0)
    col = lax.broadcasted_iota(jnp.int32, (rows, cols), 1)
    inside = (col < cols - 1) & ((row < rows - 1) | jnp.logical_not(last_y))

    velocities = pltpu.make_async_copy(v_ref, held_ref, sem)
    velocities.start()

    body, blocks = place[4], place[3]
    start = place[2] * rows
    other = jnp.where(body == 0, place[2] + 1, place[2] + blocks - 1) % blocks * rows

    @pl.when(last_x)
    def _():
        def invert(b, _):
            inverse_ref[partner_ref[b]] = b
            return 0

        lax.fori_loop(0, partner_ref.shape[0], invert, 0, unroll=8)

        def arrive(q, slots):
            new = []
            for n, (first, slot) in enumerate(zip((start, other), slots)):
                r = jnp.where(body == 0, inverse_ref[first + q], partner_ref[first + q]) - start
                here = (r >= 0) & (r < rows)
                slot_ref[jnp.where(here, r, rows)] = slot
                new.append(slot + here.astype(jnp.int32))
            return tuple(new)

        lax.fori_loop(0, rows, arrive, (jnp.int32(0), jnp.int32(rows // 2)), unroll=4)
        lane = lax.broadcasted_iota(jnp.int32, (1, turned_ref.shape[2]), 1)

        def leave(r, counts):
            q = jnp.where(body == 0, partner_ref[start + r], inverse_ref[start + r])
            beside = (q >= start) & (q < start + rows)
            whole = jnp.where(beside, q - start, rows + q - other)
            half = slot_ref[r]
            for n in range(turned_ref.shape[1] // rows):
                turned_ref[0, pl.ds(n * rows + r, 1)] = jnp.where(lane == whole, 1.0, 0.0)
                turned_ref[1, pl.ds(n * rows + r, 1)] = jnp.where(lane == half, 1.0, 0.0)
            live = active_ref[jnp.where(body == 0, start + r, q)].astype(jnp.float32)
            push_ref[pl.ds(r, 1)] = jnp.where(lane[:, :cols] >= 0, live * (-PRESSURE_SCALE), 0.0)
            near, far = counts
            chosen_ref[jnp.where(beside, near, far)] = r
            return near + beside.astype(jnp.int32), far + 1 - beside.astype(jnp.int32)

        lax.fori_loop(0, rows, leave, (jnp.int32(0), jnp.int32(rows // 2)), unroll=4)
        pick_ref[...] = turned_ref[0].T
        half_ref[...] = turned_ref[1].T[: half_ref.shape[0]]

    @pl.when(jnp.logical_not(last_x))
    def _():
        push_ref[...] = jnp.zeros_like(push_ref)
        pick_ref[...] = jnp.zeros_like(pick_ref)
        half_ref[...] = jnp.zeros_like(half_ref)

        def any_row(r, _):
            chosen_ref[r] = 0
            return 0

        lax.fori_loop(0, chosen_ref.shape[0], any_row, 0, unroll=8)

    def plane(i, earlier):
        kinds = kinds_ref[i]
        stiff = jnp.zeros((rows, cols), jnp.float32)
        mass = jnp.ones((rows, cols), jnp.float32)
        for m in range(moduli_ref.shape[0]):
            hit = kinds == m
            stiff = jnp.where(hit, moduli_ref[m] * STIFF, stiff)
            mass = jnp.where(hit, density_ref[m], mass)
        keep = inside & ((i < planes - 1) | jnp.logical_not(last_x))
        here = jnp.where(keep, stiff, 0.0)
        kick = KICK / mass
        kick_ref[i] = kick
        row_kick_ref[0, pl.ds(i, 1)] = kick[0:1]
        row_kick_ref[1, pl.ds(i, 1)] = kick[rows - 1 : rows]
        s = here + pltpu.roll(here, 1, 1)
        both = here + earlier
        ky = both + pltpu.roll(both, 1, 1)
        high_ky_ref[pl.ds(i, 1)] = ky[rows - 1 : rows]
        kx_ref[i] = s + rows_behind(s, row)
        ky_ref[i] = jnp.where(row < rows - 1, ky, 0.0)
        kz_ref[i] = both + rows_behind(both, row)
        return here

    lax.fori_loop(0, planes, plane, jnp.zeros((rows, cols), jnp.float32), unroll=math.gcd(4, planes))
    push_ref[...] = push_ref[...] * kick_ref[planes - 1]
    velocities.wait()


def rows_behind(value, row, first=0.0):
    return jnp.where(row == 0, first, pltpu.roll(value, 1, 0))


def first_kernel(d_ref, v_ref, kx_ref, ky_ref, kz_ref, kick_ref, u_ref, w_ref, yc_ref, yd_ref):
    _, planes, rows, cols = u_ref.shape
    even_y = lax.axis_index("yz") % 2 == 0

    def plane(i, carried, ahead):
        return tuple(
            advance_plane(
                c, i, d_ref[c, i] * U_SCALE, ahead and d_ref[c, i + 1] * U_SCALE, v_ref[c, i] * W_SCALE, carried[c],
                kx_ref[i], ky_ref[i], kz_ref[i], kick_ref[i], u_ref, w_ref, yc_ref, yd_ref, even_y,
            )
            for c in range(3)
        )

    zero = jnp.zeros((rows, cols), jnp.float32)
    carried = lax.fori_loop(
        0, planes - 1, lambda i, carried: plane(i, carried, True), (zero,) * 3, unroll=math.gcd(3, planes - 1)
    )
    plane(planes - 1, carried, False)


def edge_kernel(
    sa_ref, sb_ref, sc_ref, sd_ref, ra_ref, rb_ref, rc_ref, rd_ref, corner_ref,
    kick_ref, row_kick_ref, high_ky_ref, kx_in, ky_in, kz_in, moduli_ref,
    kx_ref, ky_ref, kz_ref, ka_ref, kb_ref, kc_ref, kd_ref, ex_ref, ey_ref,
):
    planes, rows, cols = kick_ref.shape
    place = here_in_mesh()
    even_x, even_y = place[0] % 2 == 0, place[2] % 2 == 0
    inner_x, inner_y = place[0] > 0, place[2] > 0
    last_x = place[0] == place[1] - 1
    last_y = place[2] == place[3] - 1
    row = lax.broadcasted_iota(jnp.int32, (rows, cols), 0)
    plane = lax.broadcasted_iota(jnp.int32, (planes, cols), 0)

    def looked_up(kinds, keep):
        stiff = jnp.zeros(kinds.shape, jnp.float32)
        for m in range(moduli_ref.shape[0]):
            stiff = jnp.where(kinds == m, moduli_ref[m] * STIFF, stiff)
        col = lax.broadcasted_iota(jnp.int32, kinds.shape, 1)
        return jnp.where((col < cols - 1) & keep, stiff, 0.0)

    def with_behind(value):
        return value + pltpu.roll(value, 1, 1)

    below_x = looked_up(
        jnp.where(even_x, rb_ref[3], ra_ref[3]), inner_x & ((row < rows - 1) | jnp.logical_not(last_y))
    )
    below_y = looked_up(
        jnp.where(even_y, rd_ref[3], rc_ref[3]), inner_y & ((plane < planes - 1) | jnp.logical_not(last_x))
    )
    corner = looked_up(corner_ref[...], inner_x & inner_y)
    s_x, s_y, s_corner = with_behind(below_x), with_behind(below_y), with_behind(corner)

    x_low = kick_ref[0] * (s_x + rows_behind(s_x, row, s_corner))
    y_low = row_kick_ref[0] * (s_y + rows_behind(s_y, plane, s_corner))
    plane_ky = jnp.where(row < rows - 1, s_x, 0.0)
    plane_kz = below_x + rows_behind(below_x, row, corner)
    rows_kx = jnp.where(plane < planes - 1, s_y, 0.0)
    rows_kz = below_y + rows_behind(below_y, plane)

    ky_ref[0] += plane_ky
    kz_ref[0] += plane_kz
    for i in range(planes):
        kx_ref[i, 0:1] += s_y[i : i + 1]
        kz_ref[i, 0:1] += rows_kz[i : i + 1]
    x_high = kick_ref[planes - 1] * kx_ref[planes - 1]
    y_high = (high_ky_ref[...] + jnp.where(plane == 0, s_x[rows - 1 : rows], 0.0)) * row_kick_ref[1]
    ka_ref[...] = jnp.where(even_x, x_high, x_low)
    kb_ref[...] = jnp.where(even_x, x_low, x_high)
    kc_ref[...] = jnp.where(even_y, y_high, y_low)
    kd_ref[...] = jnp.where(even_y, y_low, y_high)

    for c in range(3):
        u = jnp.where(even_x, sb_ref[c], sa_ref[c]) * U_SCALE
        pull_y = plane_ky * jnp.tanh(pltpu.roll(u, rows - 1, 0) - u)
        pull_z = plane_kz * jnp.tanh(pltpu.roll(u, cols - 1, 1) - u)
        ex_ref[c] = kick_ref[0] * (pull_y - pltpu.roll(pull_y, 1, 0) + (pull_z - pltpu.roll(pull_z, 1, 1)))
        u = jnp.where(even_y, sd_ref[c], sc_ref[c]) * U_SCALE
        pull_x = rows_kx * jnp.tanh(pltpu.roll(u, planes - 1, 0) - u)
        pull_z = rows_kz * jnp.tanh(pltpu.roll(u, cols - 1, 1) - u)
        ey_ref[c] = row_kick_ref[0] * (pull_x - pltpu.roll(pull_x, 1, 0) + (pull_z - pltpu.roll(pull_z, 1, 1)))


def interior_kernel(
    u_scale, w_scale, u_in, w_in, kx_ref, ky_ref, kz_ref, kick_ref, xl_ref, xh_ref, yl_ref, yh_ref,
    u_ref, w_ref, yc_ref, yd_ref,
):
    _, planes, rows, cols = u_ref.shape
    even_y = lax.axis_index("yz") % 2 == 0
    for ref in (u_ref, w_ref):
        for c in range(3):
            ref[c, 0] += xl_ref[c]
            ref[c, planes - 1] += xh_ref[c]

    def fixed(ref, c, i):
        return with_sides(ref[c, i], yl_ref[c, pl.ds(i, 1)], yh_ref[c, pl.ds(i, 1)])

    def plane(i, carried, ahead):
        return tuple(
            advance_plane(
                c, i, fixed(u_ref, c, i), ahead and fixed(u_ref, c, i + 1), fixed(w_ref, c, i), carried[c],
                kx_ref[i], ky_ref[i], kz_ref[i], kick_ref[i], u_ref, w_ref, yc_ref, yd_ref, even_y, u_scale, w_scale,
            )
            for c in range(3)
        )

    zero = jnp.zeros((rows, cols), jnp.float32)
    carried = lax.fori_loop(
        0, planes - 1, lambda i, carried: plane(i, carried, True), (zero,) * 3, unroll=math.gcd(3, planes - 1)
    )
    plane(planes - 1, carried, False)


def with_sides(value, low, high):
    rows, cols = value.shape
    tile = math.gcd(8, rows)
    row = lax.broadcasted_iota(jnp.int32, (tile, cols), 0)
    low, high = jnp.where(row == 0, low, 0.0), jnp.where(row == tile - 1, high, 0.0)
    if rows == tile:
        return value + (low + high)
    middle = [value[tile : rows - tile]] if rows > 2 * tile else []
    return jnp.concatenate([value[0:tile] + low, *middle, value[rows - tile :] + high], axis=0)


def advance_plane(
    c, i, here, ahead, w, carried, kx, ky, kz, kick, u_ref, w_ref, yc_ref, yd_ref, even_y, u_scale=1.0, w_scale=1.0
):
    rows, cols = here.shape
    force = -carried
    pull_x = None
    if ahead is not False:
        pull_x = kx * jnp.tanh(ahead - here)
        force = force + pull_x
    pull_y = ky * jnp.tanh(pltpu.roll(here, rows - 1, 0) - here)
    force = force + (pull_y - pltpu.roll(pull_y, 1, 0))
    pull_z = kz * jnp.tanh(pltpu.roll(here, cols - 1, 1) - here)
    force = force + (pull_z - pltpu.roll(pull_z, 1, 1))
    w = w + kick * force
    u = here + w
    if u_scale != 1.0:
        u, w = u * u_scale, w * w_scale
    w_ref[c, i] = w
    u_ref[c, i] = u
    first, last = u[0:1], u[rows - 1 : rows]
    yc_ref[c, pl.ds(i, 1)] = jnp.where(even_y, last, first)
    yd_ref[c, pl.ds(i, 1)] = jnp.where(even_y, first, last)
    return pull_x


def contact_kernel(
    scale, own_ref, near_ref, far_ref, pick_ref, push_ref, out_ref, fp_ref, fy_ref, fz_ref,
):
    rows, cols = out_ref.shape
    lanes = pick_ref.shape[1]
    parts = lanes // rows
    deep = cols // parts
    is_face = lax.axis_index("gx") == lax.axis_size("gx") - 1

    @pl.when(jnp.logical_not(is_face))
    def _():
        out_ref[...] = jnp.zeros_like(out_ref)

    @pl.when(is_face)
    def _():
        pick = pick_ref[...]

        def matched(c):
            pool = jnp.concatenate([near_ref[c], far_ref[c]], axis=0)
            return lax.dot_general(
                pool, pick, (((0,), (0,)), ((), ())),
                precision=lax.Precision.HIGHEST, preferred_element_type=jnp.float32,
            )

        def own(c):
            turned = own_ref[c].T
            return jnp.concatenate([turned[h * deep : (h + 1) * deep] for h in range(parts)], axis=1)

        gap = scale * GAP_SCALE
        along = scale * YIELD_SPAN * SPAN
        fp_ref[...] = jnp.exp2(matched(0) * gap - BIAS / 2.0)
        fy_ref[...] = matched(1) * along
        spot = lax.broadcasted_iota(jnp.int32, (cols, lanes), 0).astype(jnp.float32)
        fz_ref[...] = matched(2) * along + spot * SPAN
        lane = lax.broadcasted_iota(jnp.int32, (deep, lanes), 1)
        depth = lax.broadcasted_iota(jnp.int32, (deep, lanes), 0)
        mine = (depth + lane // rows * deep).astype(jnp.float32)
        op = jnp.exp2(own(0) * gap - BIAS / 2.0)
        oy = own(1) * along
        oz = own(2) * along + mine * SPAN

        def term(m, total):
            at = pl.ds(m, 1)
            dy = oy - fy_ref[at]
            dz = oz - fz_ref[at]
            weight = jnp.exp2(-(dy * dy + dz * dz))
            soft = jnp.log2(op * fp_ref[at] + 2.0**-BIAS) + BIAS
            return total + weight * soft

        total = lax.fori_loop(0, cols, term, jnp.zeros((deep, lanes), jnp.float32), unroll=math.gcd(16, cols))
        turned = jnp.concatenate([total[:, h * rows : (h + 1) * rows] for h in range(parts)], axis=0)
        out_ref[...] = turned.T * push_ref[...]


def last_contact_kernel(
    own_ref, near_ref, far_ref, pick_ref, push_ref, u_ref, w_ref, d_ref, v_ref, out_ref, fp_ref, fy_ref, fz_ref, sems,
):
    copies = [
        pltpu.make_async_copy(u_ref, d_ref, sems.at[0]),
        pltpu.make_async_copy(w_ref, v_ref, sems.at[1]),
    ]
    for copy in copies:
        copy.start()
    contact_kernel(1.0, own_ref, near_ref, far_ref, pick_ref, push_ref, out_ref, fp_ref, fy_ref, fz_ref)
    for copy in copies:
        copy.wait()


def link_moves(scale, extra, sent, got, edges, push_ref, c):
    moves = []
    for n in range(4):
        arrived = jnp.concatenate([half[c] for half in got[n]], axis=0) if isinstance(got[n], tuple) else got[n][c]
        stretch = arrived - sent[n][c]
        if scale != 1.0:
            stretch = stretch * scale
        moves.append(edges[n][...] * jnp.tanh(stretch))
    if c == 0:
        moves[1] = moves[1] + push_ref[...]
    a, b, c_, d = moves
    even_x, even_y = lax.axis_index("gx") % 2 == 0, lax.axis_index("yz") % 2 == 0
    moves = [jnp.where(even_x, b, a), jnp.where(even_x, a, b), jnp.where(even_y, d, c_), jnp.where(even_y, c_, d)]
    if extra:
        moves[0] = moves[0] + extra[0][c]
        moves[2] = moves[2] + extra[1][c]
    return moves


def arrivals(refs, n_got):
    sent, got, edges, refs = refs[:4], refs[4 : 4 + n_got], refs[4 + n_got : 8 + n_got], refs[8 + n_got :]
    if n_got == 5:
        got = [got[0], tuple(got[1:3]), *got[3:]]
    return sent, got, edges, refs


def boundary_kernel(scale, n_extra, n_got, *refs):
    extra, refs = refs[:n_extra], refs[n_extra:]
    u_ref, yc_ref, yd_ref, *refs = refs
    sent, got, edges, refs = arrivals(refs, n_got)
    push_ref, chosen_ref, na_ref, nb_ref, nc_ref, nd_ref, *refs = refs
    half_ref, rest_ref, xl_ref, xh_ref, yl_ref, yh_ref = refs
    _, planes, rows, cols = u_ref.shape
    even_x, even_y = lax.axis_index("gx") % 2 == 0, lax.axis_index("yz") % 2 == 0
    for c in range(3):
        xl, xh, yl, yh = link_moves(scale, extra, sent, got, edges, push_ref, c)
        xl_ref[c], xh_ref[c], yl_ref[c], yh_ref[c] = xl, xh, yl, yh
        low = with_sides(u_ref[c, 0] + xl, yl[0:1], yh[0:1])
        high = with_sides(u_ref[c, planes - 1] + xh, yl[planes - 1 :], yh[planes - 1 :])
        na_ref[c], nb_ref[c] = jnp.where(even_x, high, low), jnp.where(even_x, low, high)
        first = xl[0:1], xh[0:1]
        last = xl[rows - 1 :], xh[rows - 1 :]
        c_low, c_high = (jnp.where(even_y, y, x) for x, y in zip(first, last))
        d_low, d_high = (jnp.where(even_y, x, y) for x, y in zip(first, last))
        nc_ref[c] = with_sides(yc_ref[c] + jnp.where(even_y, yh, yl), c_low, c_high)
        nd_ref[c] = with_sides(yd_ref[c] + jnp.where(even_y, yl, yh), d_low, d_high)
    half = rows // 2
    is_face = lax.axis_index("gx") == lax.axis_size("gx") - 1

    @pl.when(is_face)
    def _():
        for n, ref in enumerate((half_ref, rest_ref)):
            for r in range(half):
                at = chosen_ref[n * half + r]
                for c in range(3):
                    ref[c, r : r + 1] = nb_ref[c, pl.ds(at, 1)]

    @pl.when(jnp.logical_not(is_face))
    def _():
        for c in range(3):
            half_ref[c], rest_ref[c] = nb_ref[c, :half], nb_ref[c, half:]


def finish_kernel(*refs):
    u_ref, w_ref, _, _, *refs = refs
    sent, got, edges, refs = arrivals(refs, 5)
    push_ref, d_ref, v_ref, planes_ref, rows_ref, sems = refs
    _, planes, rows, cols = u_ref.shape
    tile = rows_ref.shape[4]
    inner = slice(1, planes - 1)
    copies = []
    moves = [link_moves(1.0, (), sent, got, edges, push_ref, c) for c in range(3)]
    results = ((u_ref, d_ref, 1.0 / U_SCALE), (w_ref, v_ref, 1.0 / W_SCALE))
    for n, (ref, out, scale) in enumerate(results):
        for side, at in ((0, 0), (1, rows - tile)):
            for c in range(3):
                fix = moves[c][2 + side] * scale
                for i in range(1, planes - 1):
                    value = ref[c, i, at : at + tile]
                    line = fix[i : i + 1]
                    row = lax.broadcasted_iota(jnp.int32, (tile, cols), 0)
                    rows_ref[n, side, c, i - 1] = value + jnp.where(row == (tile - 1 if side else 0), line, 0.0)
            copies.append(
                pltpu.make_async_copy(
                    rows_ref.at[n, side], out.at[:, inner, at : at + tile], sems.at[len(copies)]
                )
            )
            copies[-1].start()
    for n, (ref, out, scale) in enumerate(results):
        for side, i in ((0, 0), (1, planes - 1)):
            for c in range(3):
                xl, xh, yl, yh = moves[c]
                value = ref[c, i] + (xh if side else xl) * scale
                planes_ref[n, side, c] = with_sides(value, yl[i : i + 1] * scale, yh[i : i + 1] * scale)
            copies.append(pltpu.make_async_copy(planes_ref.at[n, side], out.at[:, i], sems.at[len(copies)]))
            copies[-1].start()
    for copy in copies:
        copy.wait()


def routes(count_body, count_x, count_y):
    def number(b, g, y):
        return (b * count_x + g) * count_y + y

    every = [(b, g, y) for b in range(count_body) for g in range(count_x) for y in range(count_y)]

    def pairs(target):
        return [(number(*at), number(*target(*at))) for at in every]

    def outer_x(b, g, y):
        if g == count_x - 1:
            return 1 - b, g, y
        return (b, (g + 1 if g % 2 else g - 1), y) if g else (b, g, y ^ 1)

    def diagonal(b, g, y):
        if g == count_x - 1:
            return 1 - b, g, (y - 1 if b else y + 1) % count_y
        return b, g, y ^ 1

    return {
        "a": pairs(lambda b, g, y: (b, g ^ 1, y)),
        "b": pairs(outer_x),
        "rest": pairs(lambda b, g, y: diagonal(b, g, y) if g == count_x - 1 else outer_x(b, g, y)),
        "c": pairs(lambda b, g, y: (b, g, y ^ 1)),
        "d": pairs(lambda b, g, y: (b, g, (y + 1 if y % 2 else y - 1) % count_y)),
        "e": pairs(diagonal),
        "corner": pairs(lambda b, g, y: (b, (g + 1) % count_x, (y + 1) % count_y)),
    }


def local(displacement, velocity, material, moduli, density, partner, active):
    planes, rows, cols = displacement.shape[2:]
    route = routes(lax.axis_size("body"), lax.axis_size("gx"), lax.axis_size("yz"))
    lanes = max(cols, 2 * rows)
    tile = math.gcd(8, rows)
    block, face, side = (planes, rows, cols), (rows, cols), (planes, cols)
    state, face3, side3 = (3, *block), (3, *face), (3, *side)
    d, v, kinds = displacement[0], velocity[0], material[0]
    smem, hbm = pltpu.SMEM, pltpu.HBM

    def passed(block, name):
        return lax.ppermute(block, AXES, route[name])

    *sent, spare, corner = call(
        pack_kernel,
        [vmem((4, *face))] * 2 + [vmem((4, *side))] * 2 + [vmem(face3), vmem((1, cols))],
        [d, kinds],
        [hbm, hbm],
        scratch=[
            pltpu.VMEM((2, *face), jnp.int32),
            vmem((2, 3, planes, tile, cols)),
            pltpu.VMEM((2, planes, tile, cols), jnp.int32),
            pltpu.SemaphoreType.DMA((8,)),
        ],
    )
    got_e = passed(spare, "e")
    got = [passed(block, name) for block, name in zip(sent, "abcd")]
    kx, ky, kz, kick, row_kick, high_ky, push_scale, pick, pick_half, chosen, v = call(
        setup_kernel,
        [vmem(block)] * 4 + [vmem((2, *side)), vmem(side), vmem(face)]
        + [vmem((lanes, lanes)), vmem((rows, lanes)), pltpu.SMEM((rows + rows // 2,), jnp.int32)]
        + [vmem(state)],
        [kinds, v, moduli, density, partner, active],
        [None, hbm] + [smem] * 4,
        scratch=[
            vmem((2, lanes, lanes)),
            pltpu.SMEM(partner.shape, jnp.int32),
            pltpu.SMEM((rows + 1,), jnp.int32),
            pltpu.SemaphoreType.DMA,
        ],
        flops=8_000_000,
    )
    pair_scratch = [vmem((cols, lanes))] * 3
    for step in range(STEPS):
        first, last = step == 0, step == STEPS - 1
        scale = U_SCALE if first else 1.0
        if first:
            corner, kick = lax.optimization_barrier((corner, kick))
            corner = passed(corner, "corner")
            u, w, yc, yd = call(
                first_kernel,
                [vmem(state)] * 2 + [vmem(side3)] * 2,
                [d, v, kx, ky, kz, kick],
            )
            push_scale, yc = lax.optimization_barrier((push_scale, yc))
        else:
            got_e, got_half = passed(rest, "rest"), passed(half, "b")
            got = [passed(sent[0], "a"), got_half, got_e, passed(sent[2], "c"), passed(sent[3], "d")]
            u, w, yc, yd = call(
                functools.partial(interior_kernel, *((1.0 / U_SCALE, 1.0 / W_SCALE) if last else (1.0, 1.0))),
                [vmem(state)] * 2 + [vmem(side3)] * 2,
                [u, w, kx, ky, kz, kick, *moves],
                aliases={0: 0, 1: 1},
                flops=20_000_000,
            )
        meet = [sent[1], got[1], got_e, pick if first else pick_half, push_scale]
        if last:
            d, v, push = call(
                last_contact_kernel,
                [jax.ShapeDtypeStruct(state, jnp.float32)] * 2 + [vmem(face)],
                [*meet, u, w],
                scratch=pair_scratch + [pltpu.SemaphoreType.DMA((2,))],
                hbm_outs=2,
                flops=20_000_000,
            )
            break
        (push,) = call(
            functools.partial(contact_kernel, scale), [vmem(face)], meet, scratch=pair_scratch,
            flops=0 if first else 20_000_000,
        )
        extra = []
        if first:
            kx, ky, kz, *rest = call(
                edge_kernel,
                [vmem(block)] * 3 + [vmem(face)] * 2 + [vmem(side)] * 2 + [vmem(face3), vmem(side3)],
                [*sent, *got, corner, kick, row_kick, high_ky, kx, ky, kz, moduli],
                [None] * 15 + [smem],
                aliases={12: 0, 13: 1, 14: 2},
            )
            edges, extra = rest[:4], rest[4:]
        *sent, half, rest, xl, xh, yl, yh = call(
            functools.partial(boundary_kernel, scale, len(extra), len(got)),
            [vmem(face3)] * 2 + [vmem(side3)] * 2 + [vmem((3, rows // 2, cols))] * 2
            + [vmem(face3)] * 2 + [vmem(side3)] * 2,
            [*extra, u, yc, yd, *sent, *got, *edges, push, chosen],
            [None] * (12 + len(got) + len(extra)) + [smem],
        )
        moves = [xl, xh, yl, yh]
    d, v = call(
        finish_kernel,
        [jax.ShapeDtypeStruct(state, jnp.float32)] * 2,
        [u, w, d, v, *sent, *got, *edges, push],
        [None, None, hbm, hbm] + [None] * 14,
        aliases={2: 0, 3: 1},
        scratch=[vmem((2, 2, *face3)), vmem((2, 2, 3, planes - 2, tile, cols)), pltpu.SemaphoreType.DMA((8,))],
        hbm_outs=2,
    )
    return d[None], v[None]


def solution(mesh):
    in_specs = (
        P("body", None, "gx", "yz", None),
        P("body", None, "gx", "yz", None),
        P("body", "gx", "yz", None),
        P(),
        P(),
        P(),
        P(),
    )
    out_specs = (P("body", None, "gx", "yz", None), P("body", None, "gx", "yz", None))
    return jax.shard_map(local, mesh=mesh, in_specs=in_specs, out_specs=out_specs, check_vma=False)
```

```python
import functools
import math

import jax
import jax.numpy as jnp
from jax import lax
from jax.experimental import pallas as pl
from jax.experimental.pallas import tpu as pltpu
from jax.sharding import PartitionSpec as P

STEPS = 4
STEP_TIME = 0.2
YIELD_SPAN = 0.5
PENALTY = 4.0
SOFT_WIDTH = 0.1
KERNEL_WIDTH = 1.5

U_SCALE = 1.0 / YIELD_SPAN
W_SCALE = STEP_TIME / YIELD_SPAN
KICK = STEP_TIME * STEP_TIME / YIELD_SPAN
LOG2E = math.log2(math.e)
GAP_SCALE = YIELD_SPAN / SOFT_WIDTH * LOG2E
SPAN = math.sqrt(LOG2E / (2.0 * KERNEL_WIDTH * KERNEL_WIDTH))
PRESSURE_SCALE = PENALTY * SOFT_WIDTH / LOG2E
STIFF = 0.25 * YIELD_SPAN
BIAS = 32.0

AXES = ("body", "gx", "yz")
VMEM_LIMIT = 48 * 1024 * 1024


def vmem(shape):
    return pltpu.VMEM(shape, jnp.float32)


def call(kernel, outs, args, spaces=None, aliases=None, scratch=(), flops=0, moved=0, hbm_outs=0):
    spaces = spaces or [None] * len(args)
    specs, placed = [], []
    for arg, space in zip(args, spaces):
        if space is None:
            placed.append(pltpu.with_memory_space_constraint(arg, pltpu.VMEM))
            specs.append(pl.BlockSpec(memory_space=pltpu.VMEM))
        else:
            placed.append(pltpu.with_memory_space_constraint(arg, space) if space == pltpu.HBM else arg)
            specs.append(pl.BlockSpec(memory_space=space))
    return pl.pallas_call(
        kernel,
        out_shape=outs,
        in_specs=specs,
        out_specs=[
            pl.BlockSpec(memory_space=pl.ANY if n < hbm_outs else getattr(out, "memory_space", pltpu.VMEM))
            for n, out in enumerate(outs)
        ],
        input_output_aliases=aliases or {},
        scratch_shapes=list(scratch),
        compiler_params=pltpu.CompilerParams(vmem_limit_bytes=VMEM_LIMIT),
        cost_estimate=pl.CostEstimate(flops=flops, bytes_accessed=moved, transcendentals=0),
    )(*placed)


def here_in_mesh():
    return (
        lax.axis_index("gx"), lax.axis_size("gx"), lax.axis_index("yz"), lax.axis_size("yz"), lax.axis_index("body")
    )


def pack_kernel(
    d_ref, mat_ref, sa_ref, sb_ref, sc_ref, sd_ref, se_ref, corner_ref, plane_ref, rows_ref, kinds_ref, sems,
):
    planes, rows, cols = mat_ref.shape
    place = here_in_mesh()
    ia, ib, jc, jd = links(place, planes, rows)
    tile = rows_ref.shape[3]
    tile_c, tile_d = jc // tile * tile, jd // tile * tile
    copies = []
    for n, (ref, i) in enumerate(((sa_ref, ia), (sb_ref, ib))):
        copies.append(pltpu.make_async_copy(d_ref.at[:, i], ref.at[0:3], sems.at[n]))
        copies.append(pltpu.make_async_copy(mat_ref.at[i], plane_ref.at[n], sems.at[2 + n]))
    for n, at in enumerate((tile_c, tile_d)):
        some = pl.ds(pl.multiple_of(at, tile), tile)
        copies.append(pltpu.make_async_copy(d_ref.at[:, :, some], rows_ref.at[n], sems.at[4 + n]))
        copies.append(pltpu.make_async_copy(mat_ref.at[:, some], kinds_ref.at[n], sems.at[6 + n]))
    for copy in copies:
        copy.start()
    for copy in copies:
        copy.wait()
    kinds_a, kinds_b = plane_ref[0].astype(jnp.float32), plane_ref[1].astype(jnp.float32)
    sa_ref[3], sb_ref[3] = kinds_a, kinds_b
    for c in range(3):
        se_ref[c] = sb_ref[c]
    corner_ref[...] = jnp.where(place[0] % 2 == 0, kinds_a[rows - 1 :], kinds_b[rows - 1 :])
    for n, (ref, j) in enumerate(((sc_ref, jc - tile_c), (sd_ref, jd - tile_d))):
        for i in range(planes):
            for c in range(3):
                ref[c, i : i + 1] = rows_ref[n, c, i, pl.ds(j, 1)]
            ref[3, i : i + 1] = kinds_ref[n, i, pl.ds(j, 1)].astype(jnp.float32)


def links(place, planes, rows):
    ia = jnp.where(place[0] % 2 == 0, planes - 1, 0)
    jc = jnp.where(place[2] % 2 == 0, rows - 1, 0)
    return ia, planes - 1 - ia, jc, rows - 1 - jc


def setup_kernel(
    kinds_ref, rc_in, v_ref, moduli_ref, density_ref, partner_ref, active_ref,
    kx_ref, ky_ref, kz_ref, kick_ref, row_kick_ref, high_ky_ref, push_ref, pick_ref, chosen_ref, rc_ref, held_ref,
    turned_ref, live_ref, sem,
):
    planes, rows, cols = kinds_ref.shape
    place = here_in_mesh()
    last_x = place[0] == place[1] - 1
    last_y = place[2] == place[3] - 1
    row = lax.broadcasted_iota(jnp.int32, (rows, cols), 0)
    col = lax.broadcasted_iota(jnp.int32, (rows, cols), 1)
    inside = (col < cols - 1) & ((row < rows - 1) | jnp.logical_not(last_y))

    velocities = pltpu.make_async_copy(v_ref, held_ref, sem)
    velocities.start()

    body, blocks = place[4], place[3]
    start = place[2] * rows
    other = jnp.where(body == 0, place[2] + 1, place[2] + blocks - 1) % blocks * rows

    @pl.when(last_x)
    def _():
        lane = lax.broadcasted_iota(jnp.int32, (1, turned_ref.shape[1]), 1)

        def meet(i, counts):
            new = []
            for n, (block, count) in enumerate(zip((start, other), counts)):
                b = jnp.where(body == 0, start, block) + i
                p = partner_ref[b]
                at = p - jnp.where(body == 0, block, start)
                mine = (at >= 0) & (at < rows)
                r = jnp.where(body == 0, i, at)
                row = pl.ds(jnp.where(mine, r, rows), 1)
                turned_ref[row] = jnp.where(lane == jnp.where(body == 0, at, i) + n * rows, 1.0, 0.0)
                live_ref[row] = jnp.where(lane[:, :cols] >= 0, active_ref[b].astype(jnp.float32), 0.0)
                chosen_ref[jnp.where(mine, count, rows)] = r
                new.append(count + mine.astype(jnp.int32))
            return tuple(new)

        lax.fori_loop(0, rows, meet, (jnp.int32(0), jnp.int32(rows // 2)), unroll=4)
        turned = turned_ref[0:rows]
        pick_ref[...] = jnp.concatenate([turned] * (pick_ref.shape[1] // rows), axis=0).T
        push_ref[...] = live_ref[0:rows] * (-PRESSURE_SCALE)

    @pl.when(jnp.logical_not(last_x))
    def _():
        push_ref[...] = jnp.zeros_like(push_ref)
        pick_ref[...] = jnp.zeros_like(pick_ref)

        def any_row(r, _):
            chosen_ref[r] = 0
            return 0

        lax.fori_loop(0, chosen_ref.shape[0], any_row, 0, unroll=8)

    def plane(i, earlier):
        kinds = kinds_ref[i]
        stiff = jnp.zeros((rows, cols), jnp.float32)
        mass = jnp.ones((rows, cols), jnp.float32)
        for m in range(moduli_ref.shape[0]):
            hit = kinds == m
            stiff = jnp.where(hit, moduli_ref[m] * STIFF, stiff)
            mass = jnp.where(hit, density_ref[m], mass)
        keep = inside & ((i < planes - 1) | jnp.logical_not(last_x))
        here = jnp.where(keep, stiff, 0.0)
        kick = KICK / mass
        kick_ref[i] = kick
        row_kick_ref[0, pl.ds(i, 1)] = kick[0:1]
        row_kick_ref[1, pl.ds(i, 1)] = kick[rows - 1 : rows]
        s = here + pltpu.roll(here, 1, 1)
        both = here + earlier
        ky = both + pltpu.roll(both, 1, 1)
        high_ky_ref[pl.ds(i, 1)] = ky[rows - 1 : rows]
        kx_ref[i] = s + rows_behind(s, row)
        ky_ref[i] = jnp.where(row < rows - 1, ky, 0.0)
        kz_ref[i] = both + rows_behind(both, row)
        return here

    lax.fori_loop(0, planes, plane, jnp.zeros((rows, cols), jnp.float32), unroll=math.gcd(4, planes))
    push_ref[...] = push_ref[...] * kick_ref[planes - 1]
    velocities.wait()


def rows_behind(value, row, first=0.0):
    return jnp.where(row == 0, first, pltpu.roll(value, 1, 0))


def first_kernel(d_ref, v_ref, kx_ref, ky_ref, kz_ref, kick_ref, u_ref, w_ref, yc_ref, yd_ref):
    _, planes, rows, cols = u_ref.shape
    even_y = lax.axis_index("yz") % 2 == 0

    def plane(i, carried, ahead):
        return tuple(
            advance_plane(
                c, i, d_ref[c, i] * U_SCALE, ahead and d_ref[c, i + 1] * U_SCALE, v_ref[c, i] * W_SCALE, carried[c],
                kx_ref[i], ky_ref[i], kz_ref[i], kick_ref[i], u_ref, w_ref, (yc_ref, yd_ref), even_y,
            )
            for c in range(3)
        )

    zero = jnp.zeros((rows, cols), jnp.float32)
    carried = lax.fori_loop(
        0, planes - 1, lambda i, carried: plane(i, carried, True), (zero,) * 3, unroll=math.gcd(3, planes - 1)
    )
    plane(planes - 1, carried, False)


def edge_kernel(
    sa_ref, sb_ref, sc_ref, sd_ref, ra_ref, rb_ref, rc_ref, rd_ref, corner_ref,
    kick_ref, row_kick_ref, high_ky_ref, kx_in, ky_in, kz_in, moduli_ref,
    kx_ref, ky_ref, kz_ref, ka_ref, kb_ref, kc_ref, kd_ref, ex_ref, ey_ref,
):
    planes, rows, cols = kick_ref.shape
    place = here_in_mesh()
    even_x, even_y = place[0] % 2 == 0, place[2] % 2 == 0
    inner_x, inner_y = place[0] > 0, place[2] > 0
    last_x = place[0] == place[1] - 1
    last_y = place[2] == place[3] - 1
    row = lax.broadcasted_iota(jnp.int32, (rows, cols), 0)
    plane = lax.broadcasted_iota(jnp.int32, (planes, cols), 0)

    def looked_up(kinds, keep):
        stiff = jnp.zeros(kinds.shape, jnp.float32)
        for m in range(moduli_ref.shape[0]):
            stiff = jnp.where(kinds == m, moduli_ref[m] * STIFF, stiff)
        col = lax.broadcasted_iota(jnp.int32, kinds.shape, 1)
        return jnp.where((col < cols - 1) & keep, stiff, 0.0)

    def with_behind(value):
        return value + pltpu.roll(value, 1, 1)

    below_x = looked_up(
        jnp.where(even_x, rb_ref[3], ra_ref[3]), inner_x & ((row < rows - 1) | jnp.logical_not(last_y))
    )
    below_y = looked_up(
        jnp.where(even_y, rd_ref[3], rc_ref[3]), inner_y & ((plane < planes - 1) | jnp.logical_not(last_x))
    )
    corner = looked_up(corner_ref[...], inner_x & inner_y)
    s_x, s_y, s_corner = with_behind(below_x), with_behind(below_y), with_behind(corner)

    x_low = kick_ref[0] * (s_x + rows_behind(s_x, row, s_corner))
    y_low = row_kick_ref[0] * (s_y + rows_behind(s_y, plane, s_corner))
    plane_ky = jnp.where(row < rows - 1, s_x, 0.0)
    plane_kz = below_x + rows_behind(below_x, row, corner)
    rows_kx = jnp.where(plane < planes - 1, s_y, 0.0)
    rows_kz = below_y + rows_behind(below_y, plane)

    ky_ref[0] += plane_ky
    kz_ref[0] += plane_kz
    for i in range(planes):
        kx_ref[i, 0:1] += s_y[i : i + 1]
        kz_ref[i, 0:1] += rows_kz[i : i + 1]
    x_high = kick_ref[planes - 1] * kx_ref[planes - 1]
    y_high = (high_ky_ref[...] + jnp.where(plane == 0, s_x[rows - 1 : rows], 0.0)) * row_kick_ref[1]
    ka_ref[...] = jnp.where(even_x, x_high, x_low)
    kb_ref[...] = jnp.where(even_x, x_low, x_high)
    kc_ref[...] = jnp.where(even_y, y_high, y_low)
    kd_ref[...] = jnp.where(even_y, y_low, y_high)

    for c in range(3):
        u = jnp.where(even_x, sb_ref[c], sa_ref[c]) * U_SCALE
        pull_y = plane_ky * jnp.tanh(pltpu.roll(u, rows - 1, 0) - u)
        pull_z = plane_kz * jnp.tanh(pltpu.roll(u, cols - 1, 1) - u)
        ex_ref[c] = kick_ref[0] * (pull_y - pltpu.roll(pull_y, 1, 0) + (pull_z - pltpu.roll(pull_z, 1, 1)))
        u = jnp.where(even_y, sd_ref[c], sc_ref[c]) * U_SCALE
        pull_x = rows_kx * jnp.tanh(pltpu.roll(u, planes - 1, 0) - u)
        pull_z = rows_kz * jnp.tanh(pltpu.roll(u, cols - 1, 1) - u)
        ey_ref[c] = row_kick_ref[0] * (pull_x - pltpu.roll(pull_x, 1, 0) + (pull_z - pltpu.roll(pull_z, 1, 1)))


def interior_kernel(
    last, u_in, w_in, kx_ref, ky_ref, kz_ref, kick_ref, xl_ref, xh_ref, yl_ref, yh_ref, u_ref, w_ref, *side_refs
):
    _, planes, rows, cols = u_ref.shape
    even_y = lax.axis_index("yz") % 2 == 0
    for ref in (u_ref, w_ref):
        for c in range(3):
            ref[c, 0] += xl_ref[c]
            ref[c, planes - 1] += xh_ref[c]

    def fixed(ref, c, i):
        return with_sides(ref[c, i], yl_ref[c, pl.ds(i, 1)], yh_ref[c, pl.ds(i, 1)])

    def plane(i, carried, ahead):
        return tuple(
            advance_plane(
                c, i, fixed(u_ref, c, i), ahead and fixed(u_ref, c, i + 1), fixed(w_ref, c, i), carried[c],
                kx_ref[i], ky_ref[i], kz_ref[i], kick_ref[i], u_ref, w_ref, side_refs, even_y, last,
            )
            for c in range(3)
        )

    zero = jnp.zeros((rows, cols), jnp.float32)
    carried = lax.fori_loop(
        0, planes - 1, lambda i, carried: plane(i, carried, True), (zero,) * 3, unroll=math.gcd(3, planes - 1)
    )
    plane(planes - 1, carried, False)


def with_sides(value, low, high):
    rows, cols = value.shape
    tile = math.gcd(8, rows)
    row = lax.broadcasted_iota(jnp.int32, (tile, cols), 0)
    low, high = jnp.where(row == 0, low, 0.0), jnp.where(row == tile - 1, high, 0.0)
    if rows == tile:
        return value + (low + high)
    middle = [value[tile : rows - tile]] if rows > 2 * tile else []
    return jnp.concatenate([value[0:tile] + low, *middle, value[rows - tile :] + high], axis=0)


def advance_plane(
    c, i, here, ahead, w, carried, kx, ky, kz, kick, u_ref, w_ref, side_refs, even_y, last=False
):
    rows, cols = here.shape
    force = -carried
    pull_x = None
    if ahead is not False:
        pull_x = kx * jnp.tanh(ahead - here)
        force = force + pull_x
    pull_y = ky * jnp.tanh(pltpu.roll(here, rows - 1, 0) - here)
    force = force + (pull_y - pltpu.roll(pull_y, 1, 0))
    pull_z = kz * jnp.tanh(pltpu.roll(here, cols - 1, 1) - here)
    force = force + (pull_z - pltpu.roll(pull_z, 1, 1))
    w = w + kick * force
    u = here + w
    if last:
        u_ref[c, i] = u * (1.0 / U_SCALE)
        w_ref[c, i] = w * (1.0 / W_SCALE)
        return pull_x
    w_ref[c, i] = w
    u_ref[c, i] = u
    low, high = u[0:1], u[rows - 1 : rows]
    yc_ref, yd_ref = side_refs
    yc_ref[c, pl.ds(i, 1)] = jnp.where(even_y, high, low)
    yd_ref[c, pl.ds(i, 1)] = jnp.where(even_y, low, high)
    return pull_x


def contact_kernel(own_ref, near_ref, far_ref, pick_ref, push_ref, out_ref, *scratch):
    @pl.when(on_face())
    def _():
        def matched(c):
            pool = jnp.concatenate([near_ref[c], far_ref[c]], axis=0)
            return lax.dot_general(
                pool, pick_ref[...], (((0,), (0,)), ((), ())),
                precision=lax.Precision.HIGHEST, preferred_element_type=jnp.float32,
            )

        out_ref[...] = pressures(U_SCALE, lambda c: own_ref[c], matched, out_ref.shape, *scratch) * push_ref[...]

    @pl.when(jnp.logical_not(on_face()))
    def _():
        out_ref[...] = jnp.zeros_like(out_ref)


def listed_contact_kernel(
    own_half_ref, own_rest_ref, half_ref, rest_ref, push_ref, chosen_ref, out_ref, list_ref, *scratch
):
    rows, cols = out_ref.shape

    @pl.when(on_face())
    def _():
        def matched(c):
            turned = jnp.concatenate([half_ref[c], rest_ref[c]], axis=0).T
            return jnp.concatenate([turned] * (scratch[0].shape[1] // rows), axis=1)

        def own(c):
            return jnp.concatenate([own_half_ref[c], own_rest_ref[c]], axis=0)

        list_ref[...] = pressures(1.0, own, matched, out_ref.shape, *scratch)
        for r in range(rows):
            out_ref[pl.ds(chosen_ref[r], 1)] = list_ref[r : r + 1]
        out_ref[...] = out_ref[...] * push_ref[...]

    @pl.when(jnp.logical_not(on_face()))
    def _():
        out_ref[...] = jnp.zeros_like(out_ref)


def on_face():
    return lax.axis_index("gx") == lax.axis_size("gx") - 1


def pressures(scale, own_rows, matched, shape, fp_ref, fy_ref, fz_ref, total_ref):
    rows, cols = shape
    lanes = fp_ref.shape[1]
    parts = lanes // rows
    deep = cols // parts

    def own(c):
        turned = own_rows(c).T
        return jnp.concatenate([turned[h * deep : (h + 1) * deep] for h in range(parts)], axis=1)

    gap = scale * GAP_SCALE
    along = scale * YIELD_SPAN * SPAN
    fp_ref[...] = jnp.exp2(matched(0) * gap - BIAS / 2.0)
    fy_ref[...] = matched(1) * along
    spot = lax.broadcasted_iota(jnp.int32, (cols, lanes), 0).astype(jnp.float32)
    fz_ref[...] = matched(2) * along + spot * SPAN
    lane = lax.broadcasted_iota(jnp.int32, (deep, lanes), 1)
    depth = lax.broadcasted_iota(jnp.int32, (deep, lanes), 0)
    mine = (depth + lane // rows * deep).astype(jnp.float32)
    op = jnp.exp2(own(0) * gap - BIAS / 2.0)
    oy = own(1) * along
    oz = own(2) * along + mine * SPAN

    width = math.gcd(16, deep)
    for s in range(0, deep, width):
        some = slice(s, s + width)
        total = jnp.zeros((width, lanes), jnp.float32)
        for m in range(cols):
            dy = oy[some] - fy_ref[m : m + 1]
            dz = oz[some] - fz_ref[m : m + 1]
            weight = jnp.exp2(-(dy * dy + dz * dz))
            soft = jnp.log2(op[some] * fp_ref[m : m + 1] + 2.0**-BIAS) + BIAS
            total = total + weight * soft
        total_ref[some] = total
    total = total_ref[...]
    return jnp.concatenate([total[:, h * rows : (h + 1) * rows] for h in range(parts)], axis=0).T


def last_contact_kernel(*refs):
    meet, (u_ref, w_ref, d_ref, v_ref, out_ref, *scratch, sems) = refs[:6], refs[6:]
    copies = [
        pltpu.make_async_copy(u_ref, d_ref, sems.at[0]),
        pltpu.make_async_copy(w_ref, v_ref, sems.at[1]),
    ]
    for copy in copies:
        copy.start()
    listed_contact_kernel(*meet, out_ref, *scratch)
    for copy in copies:
        copy.wait()


def link_moves(scale, extra, sent, got, edges, push_ref, c):
    moves = []
    for n in range(4):
        arrived = jnp.concatenate([half[c] for half in got[n]], axis=0) if isinstance(got[n], tuple) else got[n][c]
        stretch = arrived - sent[n][c]
        if scale != 1.0:
            stretch = stretch * scale
        moves.append(edges[n][...] * jnp.tanh(stretch))
    if c == 0:
        moves[1] = moves[1] + push_ref[...]
    a, b, c_, d = moves
    even_x, even_y = lax.axis_index("gx") % 2 == 0, lax.axis_index("yz") % 2 == 0
    moves = [jnp.where(even_x, b, a), jnp.where(even_x, a, b), jnp.where(even_y, d, c_), jnp.where(even_y, c_, d)]
    if extra:
        moves[0] = moves[0] + extra[0][c]
        moves[2] = moves[2] + extra[1][c]
    return moves


def arrivals(refs, n_got):
    sent, got, edges, refs = refs[:4], refs[4 : 4 + n_got], refs[4 + n_got : 8 + n_got], refs[8 + n_got :]
    if n_got == 5:
        got = [got[0], tuple(got[1:3]), *got[3:]]
    return sent, got, edges, refs


def boundary_kernel(scale, n_extra, n_got, *refs):
    extra, refs = refs[:n_extra], refs[n_extra:]
    u_ref, yc_ref, yd_ref, *refs = refs
    sent, got, edges, refs = arrivals(refs, n_got)
    push_ref, chosen_ref, na_ref, nb_ref, nc_ref, nd_ref, *refs = refs
    half_ref, rest_ref, xl_ref, xh_ref, yl_ref, yh_ref = refs
    _, planes, rows, cols = u_ref.shape
    even_x, even_y = lax.axis_index("gx") % 2 == 0, lax.axis_index("yz") % 2 == 0
    for c in range(3):
        xl, xh, yl, yh = link_moves(scale, extra, sent, got, edges, push_ref, c)
        xl_ref[c], xh_ref[c], yl_ref[c], yh_ref[c] = xl, xh, yl, yh
        low = with_sides(u_ref[c, 0] + xl, yl[0:1], yh[0:1])
        high = with_sides(u_ref[c, planes - 1] + xh, yl[planes - 1 :], yh[planes - 1 :])
        na_ref[c], nb_ref[c] = jnp.where(even_x, high, low), jnp.where(even_x, low, high)
        first = xl[0:1], xh[0:1]
        last = xl[rows - 1 :], xh[rows - 1 :]
        c_low, c_high = (jnp.where(even_y, y, x) for x, y in zip(first, last))
        d_low, d_high = (jnp.where(even_y, x, y) for x, y in zip(first, last))
        nc_ref[c] = with_sides(yc_ref[c] + jnp.where(even_y, yh, yl), c_low, c_high)
        nd_ref[c] = with_sides(yd_ref[c] + jnp.where(even_y, yl, yh), d_low, d_high)
    half = rows // 2

    @pl.when(on_face())
    def _():
        for n, ref in enumerate((half_ref, rest_ref)):
            for r in range(half):
                at = chosen_ref[n * half + r]
                for c in range(3):
                    ref[c, r : r + 1] = nb_ref[c, pl.ds(at, 1)]

    @pl.when(jnp.logical_not(on_face()))
    def _():
        for c in range(3):
            half_ref[c], rest_ref[c] = nb_ref[c, :half], nb_ref[c, half:]


def finish_kernel(*refs):
    u_ref, w_ref, _, _, *refs = refs
    sent, got, edges, refs = arrivals(refs, 5)
    push_ref, d_ref, v_ref, planes_ref, rows_ref, sems = refs
    _, planes, rows, cols = u_ref.shape
    tile = rows_ref.shape[4]
    inner = slice(1, planes - 1)
    copies = []
    moves = [link_moves(1.0, (), sent, got, edges, push_ref, c) for c in range(3)]
    results = ((u_ref, d_ref, 1.0 / U_SCALE), (w_ref, v_ref, 1.0 / W_SCALE))
    for n, (ref, out, scale) in enumerate(results):
        for side, at in ((0, 0), (1, rows - tile)):
            for c in range(3):
                fix = moves[c][2 + side] * scale
                for i in range(1, planes - 1):
                    value = ref[c, i, at : at + tile]
                    line = fix[i : i + 1]
                    row = lax.broadcasted_iota(jnp.int32, (tile, cols), 0)
                    rows_ref[n, side, c, i - 1] = value + jnp.where(row == (tile - 1 if side else 0), line, 0.0)
            copies.append(
                pltpu.make_async_copy(
                    rows_ref.at[n, side], out.at[:, inner, at : at + tile], sems.at[len(copies)]
                )
            )
            copies[-1].start()
    for n, (ref, out, scale) in enumerate(results):
        for side, i in ((0, 0), (1, planes - 1)):
            for c in range(3):
                xl, xh, yl, yh = moves[c]
                value = ref[c, i] + (xh if side else xl) * scale
                planes_ref[n, side, c] = with_sides(value, yl[i : i + 1] * scale, yh[i : i + 1] * scale)
            copies.append(pltpu.make_async_copy(planes_ref.at[n, side], out.at[:, i], sems.at[len(copies)]))
            copies[-1].start()
    for copy in copies:
        copy.wait()


def routes(count_body, count_x, count_y):
    def number(b, g, y):
        return (b * count_x + g) * count_y + y

    every = [(b, g, y) for b in range(count_body) for g in range(count_x) for y in range(count_y)]

    def pairs(target):
        return [(number(*at), number(*target(*at))) for at in every]

    def outer_x(b, g, y):
        if g == count_x - 1:
            return 1 - b, g, y
        return (b, (g + 1 if g % 2 else g - 1), y) if g else (b, g, y ^ 1)

    def diagonal(b, g, y):
        if g == count_x - 1:
            return 1 - b, g, (y - 1 if b else y + 1) % count_y
        return b, g, y ^ 1

    return {
        "a": pairs(lambda b, g, y: (b, g ^ 1, y)),
        "b": pairs(outer_x),
        "rest": pairs(lambda b, g, y: diagonal(b, g, y) if g == count_x - 1 else outer_x(b, g, y)),
        "c": pairs(lambda b, g, y: (b, g, y ^ 1)),
        "d": pairs(lambda b, g, y: (b, g, (y + 1 if y % 2 else y - 1) % count_y)),
        "e": pairs(diagonal),
        "corner": pairs(lambda b, g, y: (b, (g + 1) % count_x, (y + 1) % count_y)),
    }


def local(displacement, velocity, material, moduli, density, partner, active):
    planes, rows, cols = displacement.shape[2:]
    route = routes(lax.axis_size("body"), lax.axis_size("gx"), lax.axis_size("yz"))
    lanes = max(cols, 2 * rows)
    tile = math.gcd(8, rows)
    block, face, side = (planes, rows, cols), (rows, cols), (planes, cols)
    state, face3, side3 = (3, *block), (3, *face), (3, *side)
    d, v, kinds = displacement[0], velocity[0], material[0]
    smem, hbm = pltpu.SMEM, pltpu.HBM

    def passed(block, name):
        return lax.ppermute(block, AXES, route[name])

    *sent, spare, corner = call(
        pack_kernel,
        [vmem((4, *face))] * 2 + [vmem((4, *side))] * 2 + [vmem(face3), vmem((1, cols))],
        [d, kinds],
        [hbm, hbm],
        scratch=[
            pltpu.VMEM((2, *face), jnp.int32),
            vmem((2, 3, planes, tile, cols)),
            pltpu.VMEM((2, planes, tile, cols), jnp.int32),
            pltpu.SemaphoreType.DMA((8,)),
        ],
    )
    got_e = passed(spare, "e")
    got = [passed(block, name) for block, name in zip(sent, "abcd")]
    kx, ky, kz, kick, row_kick, high_ky, push_scale, pick, chosen, got[2], v = call(
        setup_kernel,
        [vmem(block)] * 4 + [vmem((2, *side)), vmem(side), vmem(face), vmem((lanes, lanes))]
        + [pltpu.SMEM((rows + 1,), jnp.int32), vmem((4, *side)), vmem(state)],
        [kinds, got[2], v, moduli, density, partner, active],
        [None, None, hbm] + [smem] * 4,
        aliases={1: 9},
        scratch=[vmem((rows + tile, lanes)), vmem((rows + tile, cols)), pltpu.SemaphoreType.DMA],
        flops=8_000_000,
    )
    pair_scratch = [vmem((cols, lanes))] * 3 + [vmem((cols * rows // lanes, lanes))]
    for step in range(STEPS):
        first, last = step == 0, step == STEPS - 1
        scale = U_SCALE if first else 1.0
        if first:
            corner, kick = lax.optimization_barrier((corner, kick))
            corner = passed(corner, "corner")
            u, w, *sides = call(
                first_kernel,
                [vmem(state)] * 2 + [vmem(side3)] * 2,
                [d, v, kx, ky, kz, kick],
            )
            push_scale, sides[0] = lax.optimization_barrier((push_scale, sides[0]))
        else:
            got_e, got_half = passed(rest, "rest"), passed(half, "b")
            got = [passed(sent[0], "a"), got_half, got_e, passed(sent[2], "c"), passed(sent[3], "d")]
            u, w, *sides = call(
                functools.partial(interior_kernel, last),
                [vmem(state)] * 2 + [vmem(side3)] * (0 if last else 2),
                [u, w, kx, ky, kz, kick, *moves],
                aliases={0: 0, 1: 1},
                flops=20_000_000,
            )
        if not first:
            meet = [half, rest, got_half, got_e, push_scale, chosen]
        if last:
            d, v, push = call(
                last_contact_kernel,
                [jax.ShapeDtypeStruct(state, jnp.float32)] * 2 + [vmem(face)],
                [*meet, u, w],
                [None] * 5 + [smem] + [None] * 2,
                scratch=[vmem(face), *pair_scratch, pltpu.SemaphoreType.DMA((2,))],
                hbm_outs=2,
                flops=20_000_000,
            )
            break
        if first:
            (push,) = call(
                contact_kernel, [vmem(face)], [sent[1], got[1], got_e, pick, push_scale], scratch=pair_scratch
            )
        else:
            (push,) = call(
                listed_contact_kernel,
                [vmem(face)],
                meet,
                [None] * 5 + [smem],
                scratch=[vmem(face), *pair_scratch],
                flops=20_000_000,
            )
        extra = []
        if first:
            kx, ky, kz, *rest = call(
                edge_kernel,
                [vmem(block)] * 3 + [vmem(face)] * 2 + [vmem(side)] * 2 + [vmem(face3), vmem(side3)],
                [*sent, *got, corner, kick, row_kick, high_ky, kx, ky, kz, moduli],
                [None] * 15 + [smem],
                aliases={12: 0, 13: 1, 14: 2},
            )
            edges, extra = rest[:4], rest[4:]
        *sent, half, rest, xl, xh, yl, yh = call(
            functools.partial(boundary_kernel, scale, len(extra), len(got)),
            [vmem(face3)] * 2 + [vmem(side3)] * 2 + [vmem((3, rows // 2, cols))] * 2
            + [vmem(face3)] * 2 + [vmem(side3)] * 2,
            [*extra, u, *sides, *sent, *got, *edges, push, chosen],
            [None] * (12 + len(got) + len(extra)) + [smem],
        )
        moves = [xl, xh, yl, yh]
    d, v = call(
        finish_kernel,
        [jax.ShapeDtypeStruct(state, jnp.float32)] * 2,
        [u, w, d, v, *sent, *got, *edges, push],
        [None, None, hbm, hbm] + [None] * 14,
        aliases={2: 0, 3: 1},
        scratch=[vmem((2, 2, *face3)), vmem((2, 2, 3, planes - 2, tile, cols)), pltpu.SemaphoreType.DMA((8,))],
        hbm_outs=2,
    )
    return d[None], v[None]


def solution(mesh):
    in_specs = (
        P("body", None, "gx", "yz", None),
        P("body", None, "gx", "yz", None),
        P("body", "gx", "yz", None),
        P(),
        P(),
        P(),
        P(),
    )
    out_specs = (P("body", None, "gx", "yz", None), P("body", None, "gx", "yz", None))
    return jax.shard_map(local, mesh=mesh, in_specs=in_specs, out_specs=out_specs, check_vma=False)
```

```python
import functools
import math

import jax
import jax.numpy as jnp
from jax import lax
from jax.experimental import pallas as pl
from jax.experimental.pallas import tpu as pltpu
from jax.sharding import PartitionSpec as P

STEPS = 4
STEP_TIME = 0.2
YIELD_SPAN = 0.5
PENALTY = 4.0
SOFT_WIDTH = 0.1
KERNEL_WIDTH = 1.5

U_SCALE = 1.0 / YIELD_SPAN
W_SCALE = STEP_TIME / YIELD_SPAN
KICK = STEP_TIME * STEP_TIME / YIELD_SPAN
LOG2E = math.log2(math.e)
GAP_SCALE = YIELD_SPAN / SOFT_WIDTH * LOG2E
SPAN = math.sqrt(LOG2E / (2.0 * KERNEL_WIDTH * KERNEL_WIDTH))
PRESSURE_SCALE = PENALTY * SOFT_WIDTH / LOG2E
STIFF = 0.25 * YIELD_SPAN
BIAS = 32.0

AXES = ("body", "gx", "yz")
VMEM_LIMIT = 48 * 1024 * 1024


def vmem(shape):
    return pltpu.VMEM(shape, jnp.float32)


def call(kernel, outs, args, spaces=None, aliases=None, scratch=(), flops=0, moved=0, hbm_outs=0):
    spaces = spaces or [None] * len(args)
    specs, placed = [], []
    for arg, space in zip(args, spaces):
        if space is None:
            placed.append(pltpu.with_memory_space_constraint(arg, pltpu.VMEM))
            specs.append(pl.BlockSpec(memory_space=pltpu.VMEM))
        else:
            placed.append(pltpu.with_memory_space_constraint(arg, space) if space == pltpu.HBM else arg)
            specs.append(pl.BlockSpec(memory_space=space))
    return pl.pallas_call(
        kernel,
        out_shape=outs,
        in_specs=specs,
        out_specs=[
            pl.BlockSpec(memory_space=pl.ANY if n < hbm_outs else getattr(out, "memory_space", pltpu.VMEM))
            for n, out in enumerate(outs)
        ],
        input_output_aliases=aliases or {},
        scratch_shapes=list(scratch),
        compiler_params=pltpu.CompilerParams(vmem_limit_bytes=VMEM_LIMIT),
        cost_estimate=pl.CostEstimate(flops=flops, bytes_accessed=moved, transcendentals=0),
    )(*placed)


def here_in_mesh():
    return (
        lax.axis_index("gx"), lax.axis_size("gx"), lax.axis_index("yz"), lax.axis_size("yz"), lax.axis_index("body")
    )


def pack_kernel(
    d_ref, mat_ref, sa_ref, sb_ref, sc_ref, sd_ref, se_ref, corner_ref, plane_ref, rows_ref, kinds_ref, sems,
):
    planes, rows, cols = mat_ref.shape
    place = here_in_mesh()
    ia, ib, jc, jd = links(place, planes, rows)
    tile = rows_ref.shape[3]
    tile_c, tile_d = jc // tile * tile, jd // tile * tile
    copies = []
    for n, (ref, i) in enumerate(((sa_ref, ia), (sb_ref, ib))):
        copies.append(pltpu.make_async_copy(d_ref.at[:, i], ref.at[0:3], sems.at[n]))
        copies.append(pltpu.make_async_copy(mat_ref.at[i], plane_ref.at[n], sems.at[2 + n]))
    for n, at in enumerate((tile_c, tile_d)):
        some = pl.ds(pl.multiple_of(at, tile), tile)
        copies.append(pltpu.make_async_copy(d_ref.at[:, :, some], rows_ref.at[n], sems.at[4 + n]))
        copies.append(pltpu.make_async_copy(mat_ref.at[:, some], kinds_ref.at[n], sems.at[6 + n]))
    for copy in copies:
        copy.start()
    for copy in copies:
        copy.wait()
    kinds_a, kinds_b = plane_ref[0].astype(jnp.float32), plane_ref[1].astype(jnp.float32)
    sa_ref[3], sb_ref[3] = kinds_a, kinds_b
    for c in range(3):
        se_ref[c] = sb_ref[c]
    corner_ref[...] = jnp.where(place[0] % 2 == 0, kinds_a[rows - 1 :], kinds_b[rows - 1 :])
    for n, (ref, j) in enumerate(((sc_ref, jc - tile_c), (sd_ref, jd - tile_d))):
        for i in range(planes):
            for c in range(3):
                ref[c, i : i + 1] = rows_ref[n, c, i, pl.ds(j, 1)]
            ref[3, i : i + 1] = kinds_ref[n, i, pl.ds(j, 1)].astype(jnp.float32)


def links(place, planes, rows):
    ia = jnp.where(place[0] % 2 == 0, planes - 1, 0)
    jc = jnp.where(place[2] % 2 == 0, rows - 1, 0)
    return ia, planes - 1 - ia, jc, rows - 1 - jc


def setup_kernel(
    kinds_ref, rc_in, d_ref, moduli_ref, density_ref, partner_ref, active_ref,
    kx_ref, ky_ref, kz_ref, kick_ref, row_kick_ref, high_ky_ref, push_ref, pick_ref, chosen_ref, rc_ref,
    turned_ref, live_ref,
):
    planes, rows, cols = kinds_ref.shape
    place = here_in_mesh()
    last_x = place[0] == place[1] - 1
    last_y = place[2] == place[3] - 1
    row = lax.broadcasted_iota(jnp.int32, (rows, cols), 0)
    col = lax.broadcasted_iota(jnp.int32, (rows, cols), 1)
    inside = (col < cols - 1) & ((row < rows - 1) | jnp.logical_not(last_y))

    del rc_in, d_ref

    body, blocks = place[4], place[3]
    start = place[2] * rows
    other = jnp.where(body == 0, place[2] + 1, place[2] + blocks - 1) % blocks * rows

    @pl.when(last_x)
    def _():
        lane = lax.broadcasted_iota(jnp.int32, (1, turned_ref.shape[1]), 1)

        def meet(i, counts):
            new = []
            for n, (block, count) in enumerate(zip((start, other), counts)):
                b = jnp.where(body == 0, start, block) + i
                p = partner_ref[b]
                at = p - jnp.where(body == 0, block, start)
                mine = (at >= 0) & (at < rows)
                r = jnp.where(body == 0, i, at)
                row = pl.ds(jnp.where(mine, r, rows), 1)
                turned_ref[row] = jnp.where(lane == jnp.where(body == 0, at, i) + n * rows, 1.0, 0.0)
                live_ref[row] = jnp.where(lane[:, :cols] >= 0, active_ref[b].astype(jnp.float32), 0.0)
                chosen_ref[jnp.where(mine, count, rows)] = r
                new.append(count + mine.astype(jnp.int32))
            return tuple(new)

        lax.fori_loop(0, rows, meet, (jnp.int32(0), jnp.int32(rows // 2)), unroll=4)
        turned = turned_ref[0:rows]
        pick_ref[...] = jnp.concatenate([turned] * (pick_ref.shape[1] // rows), axis=0).T
        push_ref[...] = live_ref[0:rows] * (-PRESSURE_SCALE)

    @pl.when(jnp.logical_not(last_x))
    def _():
        push_ref[...] = jnp.zeros_like(push_ref)
        pick_ref[...] = jnp.zeros_like(pick_ref)

        def any_row(r, _):
            chosen_ref[r] = 0
            return 0

        lax.fori_loop(0, chosen_ref.shape[0], any_row, 0, unroll=8)

    def plane(i, earlier):
        kinds = kinds_ref[i]
        stiff = jnp.zeros((rows, cols), jnp.float32)
        mass = jnp.ones((rows, cols), jnp.float32)
        for m in range(moduli_ref.shape[0]):
            hit = kinds == m
            stiff = jnp.where(hit, moduli_ref[m] * STIFF, stiff)
            mass = jnp.where(hit, density_ref[m], mass)
        keep = inside & ((i < planes - 1) | jnp.logical_not(last_x))
        here = jnp.where(keep, stiff, 0.0)
        kick = KICK / mass
        kick_ref[i] = kick
        row_kick_ref[0, pl.ds(i, 1)] = kick[0:1]
        row_kick_ref[1, pl.ds(i, 1)] = kick[rows - 1 : rows]
        s = here + pltpu.roll(here, 1, 1)
        both = here + earlier
        ky = both + pltpu.roll(both, 1, 1)
        high_ky_ref[pl.ds(i, 1)] = ky[rows - 1 : rows]
        kx_ref[i] = s + rows_behind(s, row)
        ky_ref[i] = jnp.where(row < rows - 1, ky, 0.0)
        kz_ref[i] = both + rows_behind(both, row)
        return here

    lax.fori_loop(0, planes, plane, jnp.zeros((rows, cols), jnp.float32), unroll=math.gcd(16, planes))
    push_ref[...] = push_ref[...] * kick_ref[planes - 1]


def rows_behind(value, row, first=0.0):
    return jnp.where(row == 0, first, pltpu.roll(value, 1, 0))


def first_kernel(d_ref, v_ref, kx_ref, ky_ref, kz_ref, kick_ref, u_ref, w_ref, yc_ref, yd_ref):
    _, planes, rows, cols = u_ref.shape
    even_y = lax.axis_index("yz") % 2 == 0

    def plane(i, carried, ahead):
        return tuple(
            advance_plane(
                c, i, d_ref[c, i] * U_SCALE, ahead and d_ref[c, i + 1] * U_SCALE, v_ref[c, i] * W_SCALE, carried[c],
                kx_ref[i], ky_ref[i], kz_ref[i], kick_ref[i], u_ref, w_ref, (yc_ref, yd_ref), even_y,
            )
            for c in range(3)
        )

    zero = jnp.zeros((rows, cols), jnp.float32)
    carried = lax.fori_loop(
        0, planes - 1, lambda i, carried: plane(i, carried, True), (zero,) * 3, unroll=math.gcd(3, planes - 1)
    )
    plane(planes - 1, carried, False)


def edge_kernel(
    sa_ref, sb_ref, sc_ref, sd_ref, ra_ref, rb_ref, rc_ref, rd_ref, corner_ref,
    kick_ref, row_kick_ref, high_ky_ref, kx_in, ky_in, kz_in, moduli_ref,
    kx_ref, ky_ref, kz_ref, ka_ref, kb_ref, kc_ref, kd_ref, ex_ref, ey_ref,
):
    planes, rows, cols = kick_ref.shape
    place = here_in_mesh()
    even_x, even_y = place[0] % 2 == 0, place[2] % 2 == 0
    inner_x, inner_y = place[0] > 0, place[2] > 0
    last_x = place[0] == place[1] - 1
    last_y = place[2] == place[3] - 1
    row = lax.broadcasted_iota(jnp.int32, (rows, cols), 0)
    plane = lax.broadcasted_iota(jnp.int32, (planes, cols), 0)

    def looked_up(kinds, keep):
        stiff = jnp.zeros(kinds.shape, jnp.float32)
        for m in range(moduli_ref.shape[0]):
            stiff = jnp.where(kinds == m, moduli_ref[m] * STIFF, stiff)
        col = lax.broadcasted_iota(jnp.int32, kinds.shape, 1)
        return jnp.where((col < cols - 1) & keep, stiff, 0.0)

    def with_behind(value):
        return value + pltpu.roll(value, 1, 1)

    below_x = looked_up(
        jnp.where(even_x, rb_ref[3], ra_ref[3]), inner_x & ((row < rows - 1) | jnp.logical_not(last_y))
    )
    below_y = looked_up(
        jnp.where(even_y, rd_ref[3], rc_ref[3]), inner_y & ((plane < planes - 1) | jnp.logical_not(last_x))
    )
    corner = looked_up(corner_ref[...], inner_x & inner_y)
    s_x, s_y, s_corner = with_behind(below_x), with_behind(below_y), with_behind(corner)

    x_low = kick_ref[0] * (s_x + rows_behind(s_x, row, s_corner))
    y_low = row_kick_ref[0] * (s_y + rows_behind(s_y, plane, s_corner))
    plane_ky = jnp.where(row < rows - 1, s_x, 0.0)
    plane_kz = below_x + rows_behind(below_x, row, corner)
    rows_kx = jnp.where(plane < planes - 1, s_y, 0.0)
    rows_kz = below_y + rows_behind(below_y, plane)

    ky_ref[0] += plane_ky
    kz_ref[0] += plane_kz
    for i in range(planes):
        kx_ref[i, 0:1] += s_y[i : i + 1]
        kz_ref[i, 0:1] += rows_kz[i : i + 1]
    x_high = kick_ref[planes - 1] * kx_ref[planes - 1]
    y_high = (high_ky_ref[...] + jnp.where(plane == 0, s_x[rows - 1 : rows], 0.0)) * row_kick_ref[1]
    ka_ref[...] = jnp.where(even_x, x_high, x_low)
    kb_ref[...] = jnp.where(even_x, x_low, x_high)
    kc_ref[...] = jnp.where(even_y, y_high, y_low)
    kd_ref[...] = jnp.where(even_y, y_low, y_high)

    for c in range(3):
        u = jnp.where(even_x, sb_ref[c], sa_ref[c]) * U_SCALE
        pull_y = plane_ky * jnp.tanh(pltpu.roll(u, rows - 1, 0) - u)
        pull_z = plane_kz * jnp.tanh(pltpu.roll(u, cols - 1, 1) - u)
        ex_ref[c] = kick_ref[0] * (pull_y - pltpu.roll(pull_y, 1, 0) + (pull_z - pltpu.roll(pull_z, 1, 1)))
        u = jnp.where(even_y, sd_ref[c], sc_ref[c]) * U_SCALE
        pull_x = rows_kx * jnp.tanh(pltpu.roll(u, planes - 1, 0) - u)
        pull_z = rows_kz * jnp.tanh(pltpu.roll(u, cols - 1, 1) - u)
        ey_ref[c] = row_kick_ref[0] * (pull_x - pltpu.roll(pull_x, 1, 0) + (pull_z - pltpu.roll(pull_z, 1, 1)))


def interior_kernel(
    last, u_in, w_in, kx_ref, ky_ref, kz_ref, kick_ref, xl_ref, xh_ref, yl_ref, yh_ref, u_ref, w_ref, *side_refs
):
    _, planes, rows, cols = u_ref.shape
    even_y = lax.axis_index("yz") % 2 == 0
    for ref in (u_ref, w_ref):
        for c in range(3):
            ref[c, 0] += xl_ref[c]
            ref[c, planes - 1] += xh_ref[c]

    def fixed(ref, c, i):
        return with_sides(ref[c, i], yl_ref[c, pl.ds(i, 1)], yh_ref[c, pl.ds(i, 1)])

    def plane(i, carried, ahead):
        return tuple(
            advance_plane(
                c, i, fixed(u_ref, c, i), ahead and fixed(u_ref, c, i + 1), fixed(w_ref, c, i), carried[c],
                kx_ref[i], ky_ref[i], kz_ref[i], kick_ref[i], u_ref, w_ref, side_refs, even_y, last,
            )
            for c in range(3)
        )

    zero = jnp.zeros((rows, cols), jnp.float32)
    carried = lax.fori_loop(
        0, planes - 1, lambda i, carried: plane(i, carried, True), (zero,) * 3, unroll=math.gcd(3, planes - 1)
    )
    plane(planes - 1, carried, False)


def with_sides(value, low, high):
    rows, cols = value.shape
    tile = math.gcd(8, rows)
    row = lax.broadcasted_iota(jnp.int32, (tile, cols), 0)
    low, high = jnp.where(row == 0, low, 0.0), jnp.where(row == tile - 1, high, 0.0)
    if rows == tile:
        return value + (low + high)
    middle = [value[tile : rows - tile]] if rows > 2 * tile else []
    return jnp.concatenate([value[0:tile] + low, *middle, value[rows - tile :] + high], axis=0)


def advance_plane(
    c, i, here, ahead, w, carried, kx, ky, kz, kick, u_ref, w_ref, side_refs, even_y, last=False
):
    rows, cols = here.shape
    force = -carried
    pull_x = None
    if ahead is not False:
        pull_x = kx * jnp.tanh(ahead - here)
        force = force + pull_x
    pull_y = ky * jnp.tanh(pltpu.roll(here, rows - 1, 0) - here)
    force = force + (pull_y - pltpu.roll(pull_y, 1, 0))
    pull_z = kz * jnp.tanh(pltpu.roll(here, cols - 1, 1) - here)
    force = force + (pull_z - pltpu.roll(pull_z, 1, 1))
    w = w + kick * force
    u = here + w
    if last:
        u_ref[c, i] = u * (1.0 / U_SCALE)
        w_ref[c, i] = w * (1.0 / W_SCALE)
        return pull_x
    w_ref[c, i] = w
    u_ref[c, i] = u
    low, high = u[0:1], u[rows - 1 : rows]
    yc_ref, yd_ref = side_refs
    yc_ref[c, pl.ds(i, 1)] = jnp.where(even_y, high, low)
    yd_ref[c, pl.ds(i, 1)] = jnp.where(even_y, low, high)
    return pull_x


def contact_kernel(own_ref, near_ref, far_ref, pick_ref, push_ref, out_ref, *scratch):
    @pl.when(on_face())
    def _():
        def matched(c):
            pool = jnp.concatenate([near_ref[c], far_ref[c]], axis=0)
            return lax.dot_general(
                pool, pick_ref[...], (((0,), (0,)), ((), ())),
                precision=lax.Precision.HIGHEST, preferred_element_type=jnp.float32,
            )

        out_ref[...] = pressures(U_SCALE, lambda c: own_ref[c], matched, out_ref.shape, *scratch) * push_ref[...]

    @pl.when(jnp.logical_not(on_face()))
    def _():
        out_ref[...] = jnp.zeros_like(out_ref)


def listed_contact_kernel(
    own_half_ref, own_rest_ref, half_ref, rest_ref, push_ref, chosen_ref, out_ref, list_ref, *scratch
):
    rows, cols = out_ref.shape

    @pl.when(on_face())
    def _():
        def matched(c):
            turned = jnp.concatenate([half_ref[c], rest_ref[c]], axis=0).T
            return jnp.concatenate([turned] * (scratch[0].shape[1] // rows), axis=1)

        def own(c):
            return jnp.concatenate([own_half_ref[c], own_rest_ref[c]], axis=0)

        list_ref[...] = pressures(1.0, own, matched, out_ref.shape, *scratch)
        for r in range(rows):
            out_ref[pl.ds(chosen_ref[r], 1)] = list_ref[r : r + 1]
        out_ref[...] = out_ref[...] * push_ref[...]

    @pl.when(jnp.logical_not(on_face()))
    def _():
        out_ref[...] = jnp.zeros_like(out_ref)


def on_face():
    return lax.axis_index("gx") == lax.axis_size("gx") - 1


def pressures(scale, own_rows, matched, shape, fp_ref, fy_ref, fz_ref, total_ref):
    rows, cols = shape
    lanes = fp_ref.shape[1]
    parts = lanes // rows
    deep = cols // parts

    def own(c):
        turned = own_rows(c).T
        return jnp.concatenate([turned[h * deep : (h + 1) * deep] for h in range(parts)], axis=1)

    gap = scale * GAP_SCALE
    along = scale * YIELD_SPAN * SPAN
    fp_ref[...] = jnp.exp2(matched(0) * gap - BIAS / 2.0)
    fy_ref[...] = matched(1) * along
    spot = lax.broadcasted_iota(jnp.int32, (cols, lanes), 0).astype(jnp.float32)
    fz_ref[...] = matched(2) * along + spot * SPAN
    lane = lax.broadcasted_iota(jnp.int32, (deep, lanes), 1)
    depth = lax.broadcasted_iota(jnp.int32, (deep, lanes), 0)
    mine = (depth + lane // rows * deep).astype(jnp.float32)
    op = jnp.exp2(own(0) * gap - BIAS / 2.0)
    oy = own(1) * along
    oz = own(2) * along + mine * SPAN

    width = math.gcd(16, deep)
    for s in range(0, deep, width):
        some = slice(s, s + width)
        total = jnp.zeros((width, lanes), jnp.float32)
        for m in range(cols):
            dy = oy[some] - fy_ref[m : m + 1]
            dz = oz[some] - fz_ref[m : m + 1]
            weight = jnp.exp2(-(dy * dy + dz * dz))
            soft = jnp.log2(op[some] * fp_ref[m : m + 1] + 2.0**-BIAS) + BIAS
            total = total + weight * soft
        total_ref[some] = total
    total = total_ref[...]
    return jnp.concatenate([total[:, h * rows : (h + 1) * rows] for h in range(parts)], axis=0).T


def last_contact_kernel(*refs):
    meet, (u_ref, w_ref, d_ref, v_ref, out_ref, *scratch, sems) = refs[:6], refs[6:]
    copies = [
        pltpu.make_async_copy(u_ref, d_ref, sems.at[0]),
        pltpu.make_async_copy(w_ref, v_ref, sems.at[1]),
    ]
    for copy in copies:
        copy.start()
    listed_contact_kernel(*meet, out_ref, *scratch)
    for copy in copies:
        copy.wait()


def link_moves(scale, extra, sent, got, edges, push_ref, c):
    moves = []
    for n in range(4):
        arrived = jnp.concatenate([half[c] for half in got[n]], axis=0) if isinstance(got[n], tuple) else got[n][c]
        stretch = arrived - sent[n][c]
        if scale != 1.0:
            stretch = stretch * scale
        moves.append(edges[n][...] * jnp.tanh(stretch))
    if c == 0:
        moves[1] = moves[1] + push_ref[...]
    a, b, c_, d = moves
    even_x, even_y = lax.axis_index("gx") % 2 == 0, lax.axis_index("yz") % 2 == 0
    moves = [jnp.where(even_x, b, a), jnp.where(even_x, a, b), jnp.where(even_y, d, c_), jnp.where(even_y, c_, d)]
    if extra:
        moves[0] = moves[0] + extra[0][c]
        moves[2] = moves[2] + extra[1][c]
    return moves


def arrivals(refs, n_got):
    sent, got, edges, refs = refs[:4], refs[4 : 4 + n_got], refs[4 + n_got : 8 + n_got], refs[8 + n_got :]
    if n_got == 5:
        a, half, rest, c, d = got
        got = [a, (half, rest), c, d]
    return sent, got, edges, refs


def boundary_kernel(scale, n_extra, n_got, *refs):
    extra, refs = refs[:n_extra], refs[n_extra:]
    u_ref, yc_ref, yd_ref, *refs = refs
    sent, got, edges, refs = arrivals(refs, n_got)
    push_ref, chosen_ref, na_ref, nb_ref, nc_ref, nd_ref, *refs = refs
    half_ref, rest_ref, xl_ref, xh_ref, yl_ref, yh_ref = refs
    _, planes, rows, cols = u_ref.shape
    even_x, even_y = lax.axis_index("gx") % 2 == 0, lax.axis_index("yz") % 2 == 0
    for c in range(3):
        xl, xh, yl, yh = link_moves(scale, extra, sent, got, edges, push_ref, c)
        xl_ref[c], xh_ref[c], yl_ref[c], yh_ref[c] = xl, xh, yl, yh
        low = with_sides(u_ref[c, 0] + xl, yl[0:1], yh[0:1])
        high = with_sides(u_ref[c, planes - 1] + xh, yl[planes - 1 :], yh[planes - 1 :])
        na_ref[c], nb_ref[c] = jnp.where(even_x, high, low), jnp.where(even_x, low, high)
        first = xl[0:1], xh[0:1]
        last = xl[rows - 1 :], xh[rows - 1 :]
        c_low, c_high = (jnp.where(even_y, y, x) for x, y in zip(first, last))
        d_low, d_high = (jnp.where(even_y, x, y) for x, y in zip(first, last))
        nc_ref[c] = with_sides(yc_ref[c] + jnp.where(even_y, yh, yl), c_low, c_high)
        nd_ref[c] = with_sides(yd_ref[c] + jnp.where(even_y, yl, yh), d_low, d_high)
    half = rows // 2

    @pl.when(on_face())
    def _():
        for n, ref in enumerate((half_ref, rest_ref)):
            for r in range(half):
                at = chosen_ref[n * half + r]
                for c in range(3):
                    ref[c, r : r + 1] = nb_ref[c, pl.ds(at, 1)]

    @pl.when(jnp.logical_not(on_face()))
    def _():
        for c in range(3):
            half_ref[c], rest_ref[c] = nb_ref[c, :half], nb_ref[c, half:]


def finish_kernel(*refs):
    u_ref, w_ref, _, _, *refs = refs
    sent, got, edges, refs = arrivals(refs, 5)
    push_ref, d_ref, v_ref, planes_ref, rows_ref, sems = refs
    _, planes, rows, cols = u_ref.shape
    tile = rows_ref.shape[4]
    inner = slice(1, planes - 1)
    copies = []
    moves = [link_moves(1.0, (), sent, got, edges, push_ref, c) for c in range(3)]
    results = ((u_ref, d_ref, 1.0 / U_SCALE), (w_ref, v_ref, 1.0 / W_SCALE))
    for n, (ref, out, scale) in enumerate(results):
        for side, at in ((0, 0), (1, rows - tile)):
            for c in range(3):
                fix = moves[c][2 + side] * scale
                for i in range(1, planes - 1):
                    value = ref[c, i, at : at + tile]
                    line = fix[i : i + 1]
                    row = lax.broadcasted_iota(jnp.int32, (tile, cols), 0)
                    rows_ref[n, side, c, i - 1] = value + jnp.where(row == (tile - 1 if side else 0), line, 0.0)
            copies.append(
                pltpu.make_async_copy(
                    rows_ref.at[n, side], out.at[:, inner, at : at + tile], sems.at[len(copies)]
                )
            )
            copies[-1].start()
    for n, (ref, out, scale) in enumerate(results):
        for side, i in ((0, 0), (1, planes - 1)):
            for c in range(3):
                xl, xh, yl, yh = moves[c]
                value = ref[c, i] + (xh if side else xl) * scale
                planes_ref[n, side, c] = with_sides(value, yl[i : i + 1] * scale, yh[i : i + 1] * scale)
            copies.append(pltpu.make_async_copy(planes_ref.at[n, side], out.at[:, i], sems.at[len(copies)]))
            copies[-1].start()
    for copy in copies:
        copy.wait()


def routes(count_body, count_x, count_y):
    def number(b, g, y):
        return (b * count_x + g) * count_y + y

    every = [(b, g, y) for b in range(count_body) for g in range(count_x) for y in range(count_y)]

    def pairs(target):
        return [(number(*at), number(*target(*at))) for at in every]

    def outer_x(b, g, y):
        if g == count_x - 1:
            return 1 - b, g, y
        return (b, (g + 1 if g % 2 else g - 1), y) if g else (b, g, y ^ 1)

    def diagonal(b, g, y):
        if g == count_x - 1:
            return 1 - b, g, (y - 1 if b else y + 1) % count_y
        return b, g, y ^ 1

    return {
        "a": pairs(lambda b, g, y: (b, g ^ 1, y)),
        "b": pairs(outer_x),
        "rest": pairs(lambda b, g, y: diagonal(b, g, y) if g == count_x - 1 else outer_x(b, g, y)),
        "c": pairs(lambda b, g, y: (b, g, y ^ 1)),
        "d": pairs(lambda b, g, y: (b, g, (y + 1 if y % 2 else y - 1) % count_y)),
        "e": pairs(diagonal),
        "corner": pairs(lambda b, g, y: (b, (g + 1) % count_x, (y + 1) % count_y)),
    }


def local(displacement, velocity, material, moduli, density, partner, active):
    planes, rows, cols = displacement.shape[2:]
    route = routes(lax.axis_size("body"), lax.axis_size("gx"), lax.axis_size("yz"))
    lanes = max(cols, 2 * rows)
    tile = math.gcd(8, rows)
    block, face, side = (planes, rows, cols), (rows, cols), (planes, cols)
    state, face3, side3 = (3, *block), (3, *face), (3, *side)
    d, v, kinds = displacement[0], velocity[0], material[0]
    smem, hbm = pltpu.SMEM, pltpu.HBM

    def passed(block, name):
        return lax.ppermute(block, AXES, route[name])

    *sent, spare, corner = call(
        pack_kernel,
        [vmem((4, *face))] * 2 + [vmem((4, *side))] * 2 + [vmem(face3), vmem((1, cols))],
        [d, kinds],
        [hbm, hbm],
        scratch=[
            pltpu.VMEM((2, *face), jnp.int32),
            vmem((2, 3, planes, tile, cols)),
            pltpu.VMEM((2, planes, tile, cols), jnp.int32),
            pltpu.SemaphoreType.DMA((8,)),
        ],
    )
    got_e = passed(spare, "e")
    got = [passed(block, name) for block, name in zip(sent, "abcd")]
    kx, ky, kz, kick, row_kick, high_ky, push_scale, pick, chosen, got[2] = call(
        setup_kernel,
        [vmem(block)] * 4 + [vmem((2, *side)), vmem(side), vmem(face), vmem((lanes, lanes))]
        + [pltpu.SMEM((rows + 1,), jnp.int32), vmem((4, *side))],
        [kinds, got[2], d, moduli, density, partner, active],
        [None, None, None] + [smem] * 4,
        aliases={1: 9},
        scratch=[vmem((rows + tile, lanes)), vmem((rows + tile, cols))],
        flops=8_000_000,
    )
    pair_scratch = [vmem((cols, lanes))] * 3 + [vmem((cols * rows // lanes, lanes))]
    for step in range(STEPS):
        first, last = step == 0, step == STEPS - 1
        scale = U_SCALE if first else 1.0
        if first:
            corner, kick = lax.optimization_barrier((corner, kick))
            corner = passed(corner, "corner")
            u, w, *sides = call(
                first_kernel,
                [vmem(state)] * 2 + [vmem(side3)] * 2,
                [d, v, kx, ky, kz, kick],
            )
            push_scale, sides[0] = lax.optimization_barrier((push_scale, sides[0]))
        else:
            got_half, got_e = passed(half, "b"), passed(rest, "rest")
            got = [passed(sent[0], "a"), got_half, got_e, passed(sent[2], "c"), passed(sent[3], "d")]
            u, w, *sides = call(
                functools.partial(interior_kernel, last),
                [vmem(state)] * 2 + [vmem(side3)] * (0 if last else 2),
                [u, w, kx, ky, kz, kick, *moves],
                aliases={0: 0, 1: 1},
                flops=20_000_000,
            )
        if not first:
            meet = [half, rest, got_half, got_e, push_scale, chosen]
        if last:
            d, v, push = call(
                last_contact_kernel,
                [jax.ShapeDtypeStruct(state, jnp.float32)] * 2 + [vmem(face)],
                [*meet, u, w],
                [None] * 5 + [smem] + [None] * 2,
                scratch=[vmem(face), *pair_scratch, pltpu.SemaphoreType.DMA((2,))],
                hbm_outs=2,
                flops=20_000_000,
            )
            break
        if first:
            (push,) = call(
                contact_kernel, [vmem(face)], [sent[1], got[1], got_e, pick, push_scale], scratch=pair_scratch
            )
        else:
            (push,) = call(
                listed_contact_kernel,
                [vmem(face)],
                meet,
                [None] * 5 + [smem],
                scratch=[vmem(face), *pair_scratch],
                flops=20_000_000,
            )
        extra = []
        if first:
            kx, ky, kz, *rest = call(
                edge_kernel,
                [vmem(block)] * 3 + [vmem(face)] * 2 + [vmem(side)] * 2 + [vmem(face3), vmem(side3)],
                [*sent, *got, corner, kick, row_kick, high_ky, kx, ky, kz, moduli],
                [None] * 15 + [smem],
                aliases={12: 0, 13: 1, 14: 2},
            )
            edges, extra = rest[:4], rest[4:]
        *sent, half, rest, xl, xh, yl, yh = call(
            functools.partial(boundary_kernel, scale, len(extra), len(got)),
            [vmem(face3)] * 2 + [vmem(side3)] * 2 + [vmem((3, rows // 2, cols))] * 2
            + [vmem(face3)] * 2 + [vmem(side3)] * 2,
            [*extra, u, *sides, *sent, *got, *edges, push, chosen],
            [None] * (12 + len(got) + len(extra)) + [smem],
        )
        moves = [xl, xh, yl, yh]
    d, v = call(
        finish_kernel,
        [jax.ShapeDtypeStruct(state, jnp.float32)] * 2,
        [u, w, d, v, *sent, *got, *edges, push],
        [None, None, hbm, hbm] + [None] * 14,
        aliases={2: 0, 3: 1},
        scratch=[vmem((2, 2, *face3)), vmem((2, 2, 3, planes - 2, tile, cols)), pltpu.SemaphoreType.DMA((8,))],
        hbm_outs=2,
    )
    return d[None], v[None]


def solution(mesh):
    in_specs = (
        P("body", None, "gx", "yz", None),
        P("body", None, "gx", "yz", None),
        P("body", "gx", "yz", None),
        P(),
        P(),
        P(),
        P(),
    )
    out_specs = (P("body", None, "gx", "yz", None), P("body", None, "gx", "yz", None))
    return jax.shard_map(local, mesh=mesh, in_specs=in_specs, out_specs=out_specs, check_vma=False)
```

```python
import functools
import math

import jax
import jax.numpy as jnp
from jax import lax
from jax.experimental import pallas as pl
from jax.experimental.pallas import tpu as pltpu
from jax.sharding import PartitionSpec as P

STEPS = 4
STEP_TIME = 0.2
YIELD_SPAN = 0.5
PENALTY = 4.0
SOFT_WIDTH = 0.1
KERNEL_WIDTH = 1.5

U_SCALE = 1.0 / YIELD_SPAN
W_SCALE = STEP_TIME / YIELD_SPAN
KICK = STEP_TIME * STEP_TIME / YIELD_SPAN
LOG2E = math.log2(math.e)
GAP_SCALE = YIELD_SPAN / SOFT_WIDTH * LOG2E
SPAN = math.sqrt(LOG2E / (2.0 * KERNEL_WIDTH * KERNEL_WIDTH))
PRESSURE_SCALE = PENALTY * SOFT_WIDTH / LOG2E
STIFF = 0.25 * YIELD_SPAN
BIAS = 32.0

AXES = ("body", "gx", "yz")
VMEM_LIMIT = 48 * 1024 * 1024


def vmem(shape):
    return pltpu.VMEM(shape, jnp.float32)


def call(kernel, outs, args, spaces=None, aliases=None, scratch=(), flops=0, moved=0, hbm_outs=0):
    spaces = spaces or [None] * len(args)
    specs, placed = [], []
    for arg, space in zip(args, spaces):
        if space is None:
            placed.append(pltpu.with_memory_space_constraint(arg, pltpu.VMEM))
            specs.append(pl.BlockSpec(memory_space=pltpu.VMEM))
        else:
            placed.append(pltpu.with_memory_space_constraint(arg, space) if space == pltpu.HBM else arg)
            specs.append(pl.BlockSpec(memory_space=space))
    return pl.pallas_call(
        kernel,
        out_shape=outs,
        in_specs=specs,
        out_specs=[
            pl.BlockSpec(memory_space=pl.ANY if n < hbm_outs else getattr(out, "memory_space", pltpu.VMEM))
            for n, out in enumerate(outs)
        ],
        input_output_aliases=aliases or {},
        scratch_shapes=list(scratch),
        compiler_params=pltpu.CompilerParams(vmem_limit_bytes=VMEM_LIMIT),
        cost_estimate=pl.CostEstimate(flops=flops, bytes_accessed=moved, transcendentals=0),
    )(*placed)


def here_in_mesh():
    return (
        lax.axis_index("gx"), lax.axis_size("gx"), lax.axis_index("yz"), lax.axis_size("yz"), lax.axis_index("body")
    )


def pack_kernel(
    d_ref, mat_ref, sa_ref, sb_ref, sc_ref, sd_ref, se_ref, corner_ref, plane_ref, rows_ref, kinds_ref, sems,
):
    planes, rows, cols = mat_ref.shape
    place = here_in_mesh()
    ia, ib, jc, jd = links(place, planes, rows)
    tile = rows_ref.shape[3]
    tile_c, tile_d = jc // tile * tile, jd // tile * tile
    copies = []
    for n, (ref, i) in enumerate(((sa_ref, ia), (sb_ref, ib))):
        copies.append(pltpu.make_async_copy(d_ref.at[:, i], ref.at[0:3], sems.at[n]))
        copies.append(pltpu.make_async_copy(mat_ref.at[i], plane_ref.at[n], sems.at[2 + n]))
    for n, at in enumerate((tile_c, tile_d)):
        some = pl.ds(pl.multiple_of(at, tile), tile)
        copies.append(pltpu.make_async_copy(d_ref.at[:, :, some], rows_ref.at[n], sems.at[4 + n]))
        copies.append(pltpu.make_async_copy(mat_ref.at[:, some], kinds_ref.at[n], sems.at[6 + n]))
    for copy in copies:
        copy.start()
    for copy in copies:
        copy.wait()
    kinds_a, kinds_b = plane_ref[0].astype(jnp.float32), plane_ref[1].astype(jnp.float32)
    sa_ref[3], sb_ref[3] = kinds_a, kinds_b
    for c in range(3):
        se_ref[c] = sb_ref[c]
    corner_ref[...] = jnp.where(place[0] % 2 == 0, kinds_a[rows - 1 :], kinds_b[rows - 1 :])
    for n, (ref, j) in enumerate(((sc_ref, jc - tile_c), (sd_ref, jd - tile_d))):
        for i in range(planes):
            for c in range(3):
                ref[c, i : i + 1] = rows_ref[n, c, i, pl.ds(j, 1)]
            ref[3, i : i + 1] = kinds_ref[n, i, pl.ds(j, 1)].astype(jnp.float32)


def links(place, planes, rows):
    ia = jnp.where(place[0] % 2 == 0, planes - 1, 0)
    jc = jnp.where(place[2] % 2 == 0, rows - 1, 0)
    return ia, planes - 1 - ia, jc, rows - 1 - jc


def setup_kernel(
    kinds_ref, rc_in, d_ref, moduli_ref, density_ref, partner_ref, active_ref,
    kx_ref, ky_ref, kz_ref, kick_ref, row_kick_ref, high_ky_ref, push_ref, pick_ref, chosen_ref, rc_ref,
    turned_ref, live_ref,
):
    planes, rows, cols = kinds_ref.shape
    place = here_in_mesh()
    last_x = place[0] == place[1] - 1
    last_y = place[2] == place[3] - 1
    row = lax.broadcasted_iota(jnp.int32, (rows, cols), 0)
    col = lax.broadcasted_iota(jnp.int32, (rows, cols), 1)
    inside = (col < cols - 1) & ((row < rows - 1) | jnp.logical_not(last_y))

    del rc_in, d_ref

    body, blocks = place[4], place[3]
    start = place[2] * rows
    other = jnp.where(body == 0, place[2] + 1, place[2] + blocks - 1) % blocks * rows

    @pl.when(last_x)
    def _():
        lane = lax.broadcasted_iota(jnp.int32, (1, turned_ref.shape[1]), 1)

        def meet(i, counts):
            new = []
            for n, (block, count) in enumerate(zip((start, other), counts)):
                b = jnp.where(body == 0, start, block) + i
                p = partner_ref[b]
                at = p - jnp.where(body == 0, block, start)
                mine = (at >= 0) & (at < rows)
                r = jnp.where(body == 0, i, at)
                row = pl.ds(jnp.where(mine, r, rows), 1)
                turned_ref[row] = jnp.where(lane == jnp.where(body == 0, at, i) + n * rows, 1.0, 0.0)
                live_ref[row] = jnp.where(lane[:, :cols] >= 0, active_ref[b].astype(jnp.float32), 0.0)
                chosen_ref[jnp.where(mine, count, rows)] = r
                new.append(count + mine.astype(jnp.int32))
            return tuple(new)

        lax.fori_loop(0, rows, meet, (jnp.int32(0), jnp.int32(rows // 2)), unroll=4)
        turned = turned_ref[0:rows]
        pick_ref[...] = jnp.concatenate([turned] * (pick_ref.shape[1] // rows), axis=0).T
        push_ref[...] = live_ref[0:rows] * (-PRESSURE_SCALE)

    @pl.when(jnp.logical_not(last_x))
    def _():
        push_ref[...] = jnp.zeros_like(push_ref)
        pick_ref[...] = jnp.zeros_like(pick_ref)

        def any_row(r, _):
            chosen_ref[r] = 0
            return 0

        lax.fori_loop(0, chosen_ref.shape[0], any_row, 0, unroll=8)

    def plane(i, earlier):
        kinds = kinds_ref[i]
        stiff = jnp.zeros((rows, cols), jnp.float32)
        mass = jnp.ones((rows, cols), jnp.float32)
        for m in range(moduli_ref.shape[0]):
            hit = kinds == m
            stiff = jnp.where(hit, moduli_ref[m] * STIFF, stiff)
            mass = jnp.where(hit, density_ref[m], mass)
        keep = inside & ((i < planes - 1) | jnp.logical_not(last_x))
        here = jnp.where(keep, stiff, 0.0)
        kick = KICK / mass
        kick_ref[i] = kick
        row_kick_ref[0, pl.ds(i, 1)] = kick[0:1]
        row_kick_ref[1, pl.ds(i, 1)] = kick[rows - 1 : rows]
        s = here + pltpu.roll(here, 1, 1)
        both = here + earlier
        ky = both + pltpu.roll(both, 1, 1)
        high_ky_ref[pl.ds(i, 1)] = ky[rows - 1 : rows]
        kx_ref[i] = s + rows_behind(s, row)
        ky_ref[i] = jnp.where(row < rows - 1, ky, 0.0)
        kz_ref[i] = both + rows_behind(both, row)
        return here

    lax.fori_loop(0, planes, plane, jnp.zeros((rows, cols), jnp.float32), unroll=math.gcd(16, planes))
    push_ref[...] = push_ref[...] * kick_ref[planes - 1]


def rows_behind(value, row, first=0.0):
    return jnp.where(row == 0, first, pltpu.roll(value, 1, 0))


def first_kernel(d_ref, v_ref, kx_ref, ky_ref, kz_ref, kick_ref, u_ref, w_ref, yc_ref, yd_ref):
    _, planes, rows, cols = u_ref.shape
    even_y = lax.axis_index("yz") % 2 == 0

    def plane(i, carried, ahead):
        return tuple(
            advance_plane(
                c, i, d_ref[c, i] * U_SCALE, ahead and d_ref[c, i + 1] * U_SCALE, v_ref[c, i] * W_SCALE, carried[c],
                kx_ref[i], ky_ref[i], kz_ref[i], kick_ref[i], u_ref, w_ref, (yc_ref, yd_ref), even_y,
            )
            for c in range(3)
        )

    zero = jnp.zeros((rows, cols), jnp.float32)
    carried = lax.fori_loop(
        0, planes - 1, lambda i, carried: plane(i, carried, True), (zero,) * 3, unroll=math.gcd(3, planes - 1)
    )
    plane(planes - 1, carried, False)


def edge_kernel(
    sa_ref, sb_ref, sc_ref, sd_ref, ra_ref, rb_ref, rc_ref, rd_ref, corner_ref,
    kick_ref, row_kick_ref, high_ky_ref, kx_in, ky_in, kz_in, moduli_ref,
    kx_ref, ky_ref, kz_ref, ka_ref, kb_ref, kc_ref, kd_ref, ex_ref, ey_ref,
):
    planes, rows, cols = kick_ref.shape
    place = here_in_mesh()
    even_x, even_y = place[0] % 2 == 0, place[2] % 2 == 0
    inner_x, inner_y = place[0] > 0, place[2] > 0
    last_x = place[0] == place[1] - 1
    last_y = place[2] == place[3] - 1
    row = lax.broadcasted_iota(jnp.int32, (rows, cols), 0)
    plane = lax.broadcasted_iota(jnp.int32, (planes, cols), 0)

    def looked_up(kinds, keep):
        stiff = jnp.zeros(kinds.shape, jnp.float32)
        for m in range(moduli_ref.shape[0]):
            stiff = jnp.where(kinds == m, moduli_ref[m] * STIFF, stiff)
        col = lax.broadcasted_iota(jnp.int32, kinds.shape, 1)
        return jnp.where((col < cols - 1) & keep, stiff, 0.0)

    def with_behind(value):
        return value + pltpu.roll(value, 1, 1)

    below_x = looked_up(
        jnp.where(even_x, rb_ref[3], ra_ref[3]), inner_x & ((row < rows - 1) | jnp.logical_not(last_y))
    )
    below_y = looked_up(
        jnp.where(even_y, rd_ref[3], rc_ref[3]), inner_y & ((plane < planes - 1) | jnp.logical_not(last_x))
    )
    corner = looked_up(corner_ref[...], inner_x & inner_y)
    s_x, s_y, s_corner = with_behind(below_x), with_behind(below_y), with_behind(corner)

    x_low = kick_ref[0] * (s_x + rows_behind(s_x, row, s_corner))
    y_low = row_kick_ref[0] * (s_y + rows_behind(s_y, plane, s_corner))
    plane_ky = jnp.where(row < rows - 1, s_x, 0.0)
    plane_kz = below_x + rows_behind(below_x, row, corner)
    rows_kx = jnp.where(plane < planes - 1, s_y, 0.0)
    rows_kz = below_y + rows_behind(below_y, plane)

    ky_ref[0] += plane_ky
    kz_ref[0] += plane_kz
    for i in range(planes):
        kx_ref[i, 0:1] += s_y[i : i + 1]
        kz_ref[i, 0:1] += rows_kz[i : i + 1]
    x_high = kick_ref[planes - 1] * kx_ref[planes - 1]
    y_high = (high_ky_ref[...] + jnp.where(plane == 0, s_x[rows - 1 : rows], 0.0)) * row_kick_ref[1]
    ka_ref[...] = jnp.where(even_x, x_high, x_low)
    kb_ref[...] = jnp.where(even_x, x_low, x_high)
    kc_ref[...] = jnp.where(even_y, y_high, y_low)
    kd_ref[...] = jnp.where(even_y, y_low, y_high)

    for c in range(3):
        u = jnp.where(even_x, sb_ref[c], sa_ref[c]) * U_SCALE
        pull_y = plane_ky * jnp.tanh(pltpu.roll(u, rows - 1, 0) - u)
        pull_z = plane_kz * jnp.tanh(pltpu.roll(u, cols - 1, 1) - u)
        ex_ref[c] = kick_ref[0] * (pull_y - pltpu.roll(pull_y, 1, 0) + (pull_z - pltpu.roll(pull_z, 1, 1)))
        u = jnp.where(even_y, sd_ref[c], sc_ref[c]) * U_SCALE
        pull_x = rows_kx * jnp.tanh(pltpu.roll(u, planes - 1, 0) - u)
        pull_z = rows_kz * jnp.tanh(pltpu.roll(u, cols - 1, 1) - u)
        ey_ref[c] = row_kick_ref[0] * (pull_x - pltpu.roll(pull_x, 1, 0) + (pull_z - pltpu.roll(pull_z, 1, 1)))


def interior_kernel(
    last, u_in, w_in, kx_ref, ky_ref, kz_ref, kick_ref, xl_ref, xh_ref, yl_ref, yh_ref, u_ref, w_ref, *side_refs
):
    _, planes, rows, cols = u_ref.shape
    even_y = lax.axis_index("yz") % 2 == 0
    for ref in (u_ref, w_ref):
        for c in range(3):
            ref[c, 0] += xl_ref[c]
            ref[c, planes - 1] += xh_ref[c]

    def fixed(ref, c, i):
        return with_sides(ref[c, i], yl_ref[c, pl.ds(i, 1)], yh_ref[c, pl.ds(i, 1)])

    def plane(i, carried, ahead):
        return tuple(
            advance_plane(
                c, i, fixed(u_ref, c, i), ahead and fixed(u_ref, c, i + 1), fixed(w_ref, c, i), carried[c],
                kx_ref[i], ky_ref[i], kz_ref[i], kick_ref[i], u_ref, w_ref, side_refs, even_y, last,
            )
            for c in range(3)
        )

    zero = jnp.zeros((rows, cols), jnp.float32)
    carried = lax.fori_loop(
        0, planes - 1, lambda i, carried: plane(i, carried, True), (zero,) * 3, unroll=math.gcd(3, planes - 1)
    )
    plane(planes - 1, carried, False)


def with_sides(value, low, high):
    rows, cols = value.shape
    tile = math.gcd(8, rows)
    row = lax.broadcasted_iota(jnp.int32, (tile, cols), 0)
    low, high = jnp.where(row == 0, low, 0.0), jnp.where(row == tile - 1, high, 0.0)
    if rows == tile:
        return value + (low + high)
    middle = [value[tile : rows - tile]] if rows > 2 * tile else []
    return jnp.concatenate([value[0:tile] + low, *middle, value[rows - tile :] + high], axis=0)


def advance_plane(
    c, i, here, ahead, w, carried, kx, ky, kz, kick, u_ref, w_ref, side_refs, even_y, last=False
):
    rows, cols = here.shape
    force = -carried
    pull_x = None
    if ahead is not False:
        pull_x = kx * jnp.tanh(ahead - here)
        force = force + pull_x
    pull_y = ky * jnp.tanh(pltpu.roll(here, rows - 1, 0) - here)
    force = force + (pull_y - pltpu.roll(pull_y, 1, 0))
    pull_z = kz * jnp.tanh(pltpu.roll(here, cols - 1, 1) - here)
    force = force + (pull_z - pltpu.roll(pull_z, 1, 1))
    w = w + kick * force
    u = here + w
    if last:
        u_ref[c, i] = u * (1.0 / U_SCALE)
        w_ref[c, i] = w * (1.0 / W_SCALE)
        return pull_x
    w_ref[c, i] = w
    u_ref[c, i] = u
    low, high = u[0:1], u[rows - 1 : rows]
    yc_ref, yd_ref = side_refs
    yc_ref[c, pl.ds(i, 1)] = jnp.where(even_y, high, low)
    yd_ref[c, pl.ds(i, 1)] = jnp.where(even_y, low, high)
    return pull_x


def contact_kernel(own_ref, near_ref, far_ref, pick_ref, push_ref, out_ref, *scratch):
    @pl.when(on_face())
    def _():
        def matched(c):
            pool = jnp.concatenate([near_ref[c], far_ref[c]], axis=0)
            return lax.dot_general(
                pool, pick_ref[...], (((0,), (0,)), ((), ())),
                precision=lax.Precision.HIGHEST, preferred_element_type=jnp.float32,
            )

        out_ref[...] = pressures(U_SCALE, lambda c: own_ref[c], matched, out_ref.shape, *scratch) * push_ref[...]

    @pl.when(jnp.logical_not(on_face()))
    def _():
        out_ref[...] = jnp.zeros_like(out_ref)


def listed_contact_kernel(
    own_half_ref, own_rest_ref, half_ref, rest_ref, push_ref, chosen_ref, out_ref, list_ref, *scratch
):
    rows, cols = out_ref.shape

    @pl.when(on_face())
    def _():
        def matched(c):
            return jnp.concatenate([half_ref[c], rest_ref[c]] * (scratch[0].shape[1] // rows), axis=0).T

        def own(c):
            return jnp.concatenate([own_half_ref[c], own_rest_ref[c]], axis=0)

        list_ref[...] = pressures(1.0, own, matched, out_ref.shape, *scratch)
        for r in range(rows):
            out_ref[pl.ds(chosen_ref[r], 1)] = list_ref[r : r + 1]
        out_ref[...] = out_ref[...] * push_ref[...]

    @pl.when(jnp.logical_not(on_face()))
    def _():
        out_ref[...] = jnp.zeros_like(out_ref)


def on_face():
    return lax.axis_index("gx") == lax.axis_size("gx") - 1


def pressures(scale, own_rows, matched, shape, fp_ref, fy_ref, fz_ref, total_ref):
    rows, cols = shape
    lanes = fp_ref.shape[1]
    parts = lanes // rows
    deep = cols // parts

    lane = lax.broadcasted_iota(jnp.int32, (deep, lanes), 1)
    depth = lax.broadcasted_iota(jnp.int32, (deep, lanes), 0)

    def own(c):
        turned = jnp.concatenate([own_rows(c)] * parts, axis=0).T
        value = turned[0:deep]
        for h in range(1, parts):
            value = jnp.where(lane >= h * rows, turned[h * deep : (h + 1) * deep], value)
        return value

    gap = scale * GAP_SCALE
    along = scale * YIELD_SPAN * SPAN
    fp_ref[...] = jnp.exp2(matched(0) * gap - BIAS / 2.0)
    fy_ref[...] = matched(1) * along
    spot = lax.broadcasted_iota(jnp.int32, (cols, lanes), 0).astype(jnp.float32)
    fz_ref[...] = matched(2) * along + spot * SPAN
    mine = (depth + lane // rows * deep).astype(jnp.float32)
    op = jnp.exp2(own(0) * gap - BIAS / 2.0)
    oy = own(1) * along
    oz = own(2) * along + mine * SPAN

    width = math.gcd(16, deep)
    for s in range(0, deep, width):
        some = slice(s, s + width)
        total = jnp.zeros((width, lanes), jnp.float32)
        for m in range(cols):
            dy = oy[some] - fy_ref[m : m + 1]
            dz = oz[some] - fz_ref[m : m + 1]
            weight = jnp.exp2(-(dy * dy + dz * dz))
            soft = jnp.log2(op[some] * fp_ref[m : m + 1] + 2.0**-BIAS) + BIAS
            total = total + weight * soft
        total_ref[some] = total
    turned = jnp.concatenate([total_ref[...]] * parts, axis=0).T
    column = lax.broadcasted_iota(jnp.int32, (rows, cols), 1)
    value = turned[0:rows]
    for h in range(1, parts):
        value = jnp.where(column >= h * deep, turned[h * rows : (h + 1) * rows], value)
    return value


def last_contact_kernel(*refs):
    meet, (u_ref, w_ref, d_ref, v_ref, out_ref, *scratch, sems) = refs[:6], refs[6:]
    copies = [
        pltpu.make_async_copy(u_ref, d_ref, sems.at[0]),
        pltpu.make_async_copy(w_ref, v_ref, sems.at[1]),
    ]
    for copy in copies:
        copy.start()
    listed_contact_kernel(*meet, out_ref, *scratch)
    for copy in copies:
        copy.wait()


def link_moves(scale, extra, sent, got, edges, push_ref, c):
    moves = []
    for n in range(4):
        arrived = jnp.concatenate([half[c] for half in got[n]], axis=0) if isinstance(got[n], tuple) else got[n][c]
        stretch = arrived - sent[n][c]
        if scale != 1.0:
            stretch = stretch * scale
        moves.append(edges[n][...] * jnp.tanh(stretch))
    if c == 0:
        moves[1] = moves[1] + push_ref[...]
    a, b, c_, d = moves
    even_x, even_y = lax.axis_index("gx") % 2 == 0, lax.axis_index("yz") % 2 == 0
    moves = [jnp.where(even_x, b, a), jnp.where(even_x, a, b), jnp.where(even_y, d, c_), jnp.where(even_y, c_, d)]
    if extra:
        moves[0] = moves[0] + extra[0][c]
        moves[2] = moves[2] + extra[1][c]
    return moves


def arrivals(refs, n_got):
    sent, got, edges, refs = refs[:4], refs[4 : 4 + n_got], refs[4 + n_got : 8 + n_got], refs[8 + n_got :]
    if n_got == 5:
        a, half, rest, c, d = got
        got = [a, (half, rest), c, d]
    return sent, got, edges, refs


def boundary_kernel(scale, n_extra, n_got, *refs):
    extra, refs = refs[:n_extra], refs[n_extra:]
    u_ref, yc_ref, yd_ref, *refs = refs
    sent, got, edges, refs = arrivals(refs, n_got)
    push_ref, chosen_ref, na_ref, nb_ref, nc_ref, nd_ref, *refs = refs
    half_ref, rest_ref, xl_ref, xh_ref, yl_ref, yh_ref = refs
    _, planes, rows, cols = u_ref.shape
    even_x, even_y = lax.axis_index("gx") % 2 == 0, lax.axis_index("yz") % 2 == 0
    for c in range(3):
        xl, xh, yl, yh = link_moves(scale, extra, sent, got, edges, push_ref, c)
        xl_ref[c], xh_ref[c], yl_ref[c], yh_ref[c] = xl, xh, yl, yh
        low = with_sides(u_ref[c, 0] + xl, yl[0:1], yh[0:1])
        high = with_sides(u_ref[c, planes - 1] + xh, yl[planes - 1 :], yh[planes - 1 :])
        na_ref[c], nb_ref[c] = jnp.where(even_x, high, low), jnp.where(even_x, low, high)
        first = xl[0:1], xh[0:1]
        last = xl[rows - 1 :], xh[rows - 1 :]
        c_low, c_high = (jnp.where(even_y, y, x) for x, y in zip(first, last))
        d_low, d_high = (jnp.where(even_y, x, y) for x, y in zip(first, last))
        nc_ref[c] = with_sides(yc_ref[c] + jnp.where(even_y, yh, yl), c_low, c_high)
        nd_ref[c] = with_sides(yd_ref[c] + jnp.where(even_y, yl, yh), d_low, d_high)
    half = rows // 2

    @pl.when(on_face())
    def _():
        for n, ref in enumerate((half_ref, rest_ref)):
            for r in range(half):
                at = chosen_ref[n * half + r]
                for c in range(3):
                    ref[c, r : r + 1] = nb_ref[c, pl.ds(at, 1)]

    @pl.when(jnp.logical_not(on_face()))
    def _():
        for c in range(3):
            half_ref[c], rest_ref[c] = nb_ref[c, :half], nb_ref[c, half:]


def finish_kernel(*refs):
    u_ref, w_ref, _, _, *refs = refs
    sent, got, edges, refs = arrivals(refs, 5)
    push_ref, d_ref, v_ref, planes_ref, rows_ref, sems = refs
    _, planes, rows, cols = u_ref.shape
    tile = rows_ref.shape[4]
    inner = slice(1, planes - 1)
    copies = []
    moves = [link_moves(1.0, (), sent, got, edges, push_ref, c) for c in range(3)]
    results = ((u_ref, d_ref, 1.0 / U_SCALE), (w_ref, v_ref, 1.0 / W_SCALE))
    for n, (ref, out, scale) in enumerate(results):
        for side, at in ((0, 0), (1, rows - tile)):
            for c in range(3):
                fix = moves[c][2 + side] * scale
                for i in range(1, planes - 1):
                    value = ref[c, i, at : at + tile]
                    line = fix[i : i + 1]
                    row = lax.broadcasted_iota(jnp.int32, (tile, cols), 0)
                    rows_ref[n, side, c, i - 1] = value + jnp.where(row == (tile - 1 if side else 0), line, 0.0)
            copies.append(
                pltpu.make_async_copy(
                    rows_ref.at[n, side], out.at[:, inner, at : at + tile], sems.at[len(copies)]
                )
            )
            copies[-1].start()
    for n, (ref, out, scale) in enumerate(results):
        for side, i in ((0, 0), (1, planes - 1)):
            for c in range(3):
                xl, xh, yl, yh = moves[c]
                value = ref[c, i] + (xh if side else xl) * scale
                planes_ref[n, side, c] = with_sides(value, yl[i : i + 1] * scale, yh[i : i + 1] * scale)
            copies.append(pltpu.make_async_copy(planes_ref.at[n, side], out.at[:, i], sems.at[len(copies)]))
            copies[-1].start()
    for copy in copies:
        copy.wait()


def routes(count_body, count_x, count_y):
    def number(b, g, y):
        return (b * count_x + g) * count_y + y

    every = [(b, g, y) for b in range(count_body) for g in range(count_x) for y in range(count_y)]

    def pairs(target):
        return [(number(*at), number(*target(*at))) for at in every]

    def outer_x(b, g, y):
        if g == count_x - 1:
            return 1 - b, g, y
        return (b, (g + 1 if g % 2 else g - 1), y) if g else (b, g, y ^ 1)

    def diagonal(b, g, y):
        if g == count_x - 1:
            return 1 - b, g, (y - 1 if b else y + 1) % count_y
        return b, g, y ^ 1

    return {
        "a": pairs(lambda b, g, y: (b, g ^ 1, y)),
        "b": pairs(outer_x),
        "rest": pairs(lambda b, g, y: diagonal(b, g, y) if g == count_x - 1 else outer_x(b, g, y)),
        "c": pairs(lambda b, g, y: (b, g, y ^ 1)),
        "d": pairs(lambda b, g, y: (b, g, (y + 1 if y % 2 else y - 1) % count_y)),
        "e": pairs(diagonal),
        "corner": pairs(lambda b, g, y: (b, (g + 1) % count_x, (y + 1) % count_y)),
    }


def local(displacement, velocity, material, moduli, density, partner, active):
    planes, rows, cols = displacement.shape[2:]
    route = routes(lax.axis_size("body"), lax.axis_size("gx"), lax.axis_size("yz"))
    lanes = max(cols, 2 * rows)
    tile = math.gcd(8, rows)
    block, face, side = (planes, rows, cols), (rows, cols), (planes, cols)
    state, face3, side3 = (3, *block), (3, *face), (3, *side)
    d, v, kinds = displacement[0], velocity[0], material[0]
    smem, hbm = pltpu.SMEM, pltpu.HBM

    def passed(block, name):
        return lax.ppermute(block, AXES, route[name])

    *sent, spare, corner = call(
        pack_kernel,
        [vmem((4, *face))] * 2 + [vmem((4, *side))] * 2 + [vmem(face3), vmem((1, cols))],
        [d, kinds],
        [hbm, hbm],
        scratch=[
            pltpu.VMEM((2, *face), jnp.int32),
            vmem((2, 3, planes, tile, cols)),
            pltpu.VMEM((2, planes, tile, cols), jnp.int32),
            pltpu.SemaphoreType.DMA((8,)),
        ],
    )
    got_e = passed(spare, "e")
    got = [passed(block, name) for block, name in zip(sent, "abcd")]
    kx, ky, kz, kick, row_kick, high_ky, push_scale, pick, chosen, got[2] = call(
        setup_kernel,
        [vmem(block)] * 4 + [vmem((2, *side)), vmem(side), vmem(face), vmem((lanes, lanes))]
        + [pltpu.SMEM((rows + 1,), jnp.int32), vmem((4, *side))],
        [kinds, got[2], d, moduli, density, partner, active],
        [None, None, None] + [smem] * 4,
        aliases={1: 9},
        scratch=[vmem((rows + tile, lanes)), vmem((rows + tile, cols))],
        flops=8_000_000,
    )
    pair_scratch = [vmem((cols, lanes))] * 3 + [vmem((cols * rows // lanes, lanes))]
    for step in range(STEPS):
        first, last = step == 0, step == STEPS - 1
        scale = U_SCALE if first else 1.0
        if first:
            corner, kick = lax.optimization_barrier((corner, kick))
            corner = passed(corner, "corner")
            u, w, *sides = call(
                first_kernel,
                [vmem(state)] * 2 + [vmem(side3)] * 2,
                [d, v, kx, ky, kz, kick],
            )
            push_scale, sides[0] = lax.optimization_barrier((push_scale, sides[0]))
        else:
            got_half, got_e = passed(half, "b"), passed(rest, "rest")
            got = [passed(sent[0], "a"), got_half, got_e, passed(sent[2], "c"), passed(sent[3], "d")]
            u, w, *sides = call(
                functools.partial(interior_kernel, last),
                [vmem(state)] * 2 + [vmem(side3)] * (0 if last else 2),
                [u, w, kx, ky, kz, kick, *moves],
                aliases={0: 0, 1: 1},
                flops=20_000_000,
            )
        if not first:
            meet = [half, rest, got_half, got_e, push_scale, chosen]
        if last:
            d, v, push = call(
                last_contact_kernel,
                [jax.ShapeDtypeStruct(state, jnp.float32)] * 2 + [vmem(face)],
                [*meet, u, w],
                [None] * 5 + [smem] + [None] * 2,
                scratch=[vmem(face), *pair_scratch, pltpu.SemaphoreType.DMA((2,))],
                hbm_outs=2,
                flops=20_000_000,
            )
            break
        if first:
            (push,) = call(
                contact_kernel, [vmem(face)], [sent[1], got[1], got_e, pick, push_scale], scratch=pair_scratch
            )
        else:
            (push,) = call(
                listed_contact_kernel,
                [vmem(face)],
                meet,
                [None] * 5 + [smem],
                scratch=[vmem(face), *pair_scratch],
                flops=20_000_000,
            )
        extra = []
        if first:
            kx, ky, kz, *rest = call(
                edge_kernel,
                [vmem(block)] * 3 + [vmem(face)] * 2 + [vmem(side)] * 2 + [vmem(face3), vmem(side3)],
                [*sent, *got, corner, kick, row_kick, high_ky, kx, ky, kz, moduli],
                [None] * 15 + [smem],
                aliases={12: 0, 13: 1, 14: 2},
            )
            edges, extra = rest[:4], rest[4:]
        *sent, half, rest, xl, xh, yl, yh = call(
            functools.partial(boundary_kernel, scale, len(extra), len(got)),
            [vmem(face3)] * 2 + [vmem(side3)] * 2 + [vmem((3, rows // 2, cols))] * 2
            + [vmem(face3)] * 2 + [vmem(side3)] * 2,
            [*extra, u, *sides, *sent, *got, *edges, push, chosen],
            [None] * (12 + len(got) + len(extra)) + [smem],
        )
        moves = [xl, xh, yl, yh]
    d, v = call(
        finish_kernel,
        [jax.ShapeDtypeStruct(state, jnp.float32)] * 2,
        [u, w, d, v, *sent, *got, *edges, push],
        [None, None, hbm, hbm] + [None] * 14,
        aliases={2: 0, 3: 1},
        scratch=[vmem((2, 2, *face3)), vmem((2, 2, 3, planes - 2, tile, cols)), pltpu.SemaphoreType.DMA((8,))],
        hbm_outs=2,
    )
    return d[None], v[None]


def solution(mesh):
    in_specs = (
        P("body", None, "gx", "yz", None),
        P("body", None, "gx", "yz", None),
        P("body", "gx", "yz", None),
        P(),
        P(),
        P(),
        P(),
    )
    out_specs = (P("body", None, "gx", "yz", None), P("body", None, "gx", "yz", None))
    return jax.shard_map(local, mesh=mesh, in_specs=in_specs, out_specs=out_specs, check_vma=False)
```

```python
import functools
import math

import jax
import jax.numpy as jnp
from jax import lax
from jax.experimental import pallas as pl
from jax.experimental.pallas import tpu as pltpu
from jax.sharding import PartitionSpec as P

STEPS = 4
STEP_TIME = 0.2
YIELD_SPAN = 0.5
PENALTY = 4.0
SOFT_WIDTH = 0.1
KERNEL_WIDTH = 1.5

U_SCALE = 1.0 / YIELD_SPAN
W_SCALE = STEP_TIME / YIELD_SPAN
KICK = STEP_TIME * STEP_TIME / YIELD_SPAN
LOG2E = math.log2(math.e)
GAP_SCALE = YIELD_SPAN / SOFT_WIDTH * LOG2E
SPAN = math.sqrt(LOG2E / (2.0 * KERNEL_WIDTH * KERNEL_WIDTH))
PRESSURE_SCALE = PENALTY * SOFT_WIDTH / LOG2E
STIFF = 0.25 * YIELD_SPAN
BIAS = 32.0
SHIFT = 64.0

AXES = ("body", "gx", "yz")
VMEM_LIMIT = 48 * 1024 * 1024


def vmem(shape):
    return pltpu.VMEM(shape, jnp.float32)


def call(kernel, outs, args, spaces=None, aliases=None, scratch=(), flops=0, moved=0, hbm_outs=0):
    spaces = spaces or [None] * len(args)
    specs, placed = [], []
    for arg, space in zip(args, spaces):
        if space is None:
            placed.append(pltpu.with_memory_space_constraint(arg, pltpu.VMEM))
            specs.append(pl.BlockSpec(memory_space=pltpu.VMEM))
        else:
            placed.append(pltpu.with_memory_space_constraint(arg, space) if space == pltpu.HBM else arg)
            specs.append(pl.BlockSpec(memory_space=space))
    return pl.pallas_call(
        kernel,
        out_shape=outs,
        in_specs=specs,
        out_specs=[
            pl.BlockSpec(memory_space=pl.ANY if n < hbm_outs else getattr(out, "memory_space", pltpu.VMEM))
            for n, out in enumerate(outs)
        ],
        input_output_aliases=aliases or {},
        scratch_shapes=list(scratch),
        compiler_params=pltpu.CompilerParams(vmem_limit_bytes=VMEM_LIMIT),
        cost_estimate=pl.CostEstimate(flops=flops, bytes_accessed=moved, transcendentals=0),
    )(*placed)


def here_in_mesh():
    return (
        lax.axis_index("gx"), lax.axis_size("gx"), lax.axis_index("yz"), lax.axis_size("yz"), lax.axis_index("body")
    )


def pack_kernel(
    d_ref, mat_ref, sa_ref, sb_ref, sc_ref, sd_ref, se_ref, corner_ref, plane_ref, rows_ref, kinds_ref, sems,
):
    planes, rows, cols = mat_ref.shape
    place = here_in_mesh()
    ia, ib, jc, jd = links(place, planes, rows)
    tile = rows_ref.shape[3]
    tile_c, tile_d = jc // tile * tile, jd // tile * tile
    copies = []
    for n, (ref, i) in enumerate(((sa_ref, ia), (sb_ref, ib))):
        copies.append(pltpu.make_async_copy(d_ref.at[:, i], ref.at[0:3], sems.at[n]))
        copies.append(pltpu.make_async_copy(mat_ref.at[i], plane_ref.at[n], sems.at[2 + n]))
    for n, at in enumerate((tile_c, tile_d)):
        some = pl.ds(pl.multiple_of(at, tile), tile)
        copies.append(pltpu.make_async_copy(d_ref.at[:, :, some], rows_ref.at[n], sems.at[4 + n]))
        copies.append(pltpu.make_async_copy(mat_ref.at[:, some], kinds_ref.at[n], sems.at[6 + n]))
    for copy in copies:
        copy.start()
    for copy in copies:
        copy.wait()
    kinds_a, kinds_b = plane_ref[0].astype(jnp.float32), plane_ref[1].astype(jnp.float32)
    sa_ref[3], sb_ref[3] = kinds_a, kinds_b
    for c in range(3):
        se_ref[c] = sb_ref[c]
    corner_ref[...] = jnp.where(place[0] % 2 == 0, kinds_a[rows - 1 :], kinds_b[rows - 1 :])
    for n, (ref, j) in enumerate(((sc_ref, jc - tile_c), (sd_ref, jd - tile_d))):
        for i in range(planes):
            for c in range(3):
                ref[c, i : i + 1] = rows_ref[n, c, i, pl.ds(j, 1)]
            ref[3, i : i + 1] = kinds_ref[n, i, pl.ds(j, 1)].astype(jnp.float32)


def links(place, planes, rows):
    ia = jnp.where(place[0] % 2 == 0, planes - 1, 0)
    jc = jnp.where(place[2] % 2 == 0, rows - 1, 0)
    return ia, planes - 1 - ia, jc, rows - 1 - jc


def setup_kernel(
    kinds_ref, rc_in, d_ref, moduli_ref, density_ref, partner_ref, active_ref,
    kx_ref, ky_ref, kz_ref, kick_ref, row_kick_ref, high_ky_ref, push_ref, pick_ref, chosen_ref, rc_ref,
    turned_ref, live_ref,
):
    planes, rows, cols = kinds_ref.shape
    place = here_in_mesh()
    last_x = place[0] == place[1] - 1
    last_y = place[2] == place[3] - 1
    row = lax.broadcasted_iota(jnp.int32, (rows, cols), 0)
    col = lax.broadcasted_iota(jnp.int32, (rows, cols), 1)
    inside = (col < cols - 1) & ((row < rows - 1) | jnp.logical_not(last_y))

    del rc_in, d_ref

    body, blocks = place[4], place[3]
    start = place[2] * rows
    other = jnp.where(body == 0, place[2] + 1, place[2] + blocks - 1) % blocks * rows

    @pl.when(last_x)
    def _():
        lane = lax.broadcasted_iota(jnp.int32, (1, turned_ref.shape[1]), 1)

        def meet(i, counts):
            new = []
            for n, (block, count) in enumerate(zip((start, other), counts)):
                b = jnp.where(body == 0, start, block) + i
                p = partner_ref[b]
                at = p - jnp.where(body == 0, block, start)
                mine = (at >= 0) & (at < rows)
                r = jnp.where(body == 0, i, at)
                row = pl.ds(jnp.where(mine, r, rows), 1)
                turned_ref[row] = jnp.where(lane == jnp.where(body == 0, at, i) + n * rows, 1.0, 0.0)
                live_ref[row] = jnp.where(lane[:, :cols] >= 0, active_ref[b].astype(jnp.float32), 0.0)
                chosen_ref[jnp.where(mine, count, rows)] = r
                new.append(count + mine.astype(jnp.int32))
            return tuple(new)

        lax.fori_loop(0, rows, meet, (jnp.int32(0), jnp.int32(rows // 2)), unroll=4)
        turned = turned_ref[0:rows]
        pick_ref[...] = jnp.concatenate([turned] * (pick_ref.shape[1] // rows), axis=0).T
        push_ref[...] = live_ref[0:rows] * (-PRESSURE_SCALE)

    @pl.when(jnp.logical_not(last_x))
    def _():
        push_ref[...] = jnp.zeros_like(push_ref)
        pick_ref[...] = jnp.zeros_like(pick_ref)

        def any_row(r, _):
            chosen_ref[r] = 0
            return 0

        lax.fori_loop(0, chosen_ref.shape[0], any_row, 0, unroll=8)

    def plane(i, earlier):
        kinds = kinds_ref[i]
        stiff = jnp.zeros((rows, cols), jnp.float32)
        mass = jnp.ones((rows, cols), jnp.float32)
        for m in range(moduli_ref.shape[0]):
            hit = kinds == m
            stiff = jnp.where(hit, moduli_ref[m] * STIFF, stiff)
            mass = jnp.where(hit, density_ref[m], mass)
        keep = inside & ((i < planes - 1) | jnp.logical_not(last_x))
        here = jnp.where(keep, stiff, 0.0)
        kick = KICK / mass
        kick_ref[i] = kick
        row_kick_ref[0, pl.ds(i, 1)] = kick[0:1]
        row_kick_ref[1, pl.ds(i, 1)] = kick[rows - 1 : rows]
        s = here + pltpu.roll(here, 1, 1)
        both = here + earlier
        ky = both + pltpu.roll(both, 1, 1)
        high_ky_ref[pl.ds(i, 1)] = ky[rows - 1 : rows]
        kx_ref[i] = s + rows_behind(s, row)
        ky_ref[i] = jnp.where(row < rows - 1, ky, 0.0)
        kz_ref[i] = both + rows_behind(both, row)
        return here

    lax.fori_loop(0, planes, plane, jnp.zeros((rows, cols), jnp.float32), unroll=math.gcd(16, planes))
    push_ref[...] = push_ref[...] * kick_ref[planes - 1]


def rows_behind(value, row, first=0.0):
    return jnp.where(row == 0, first, pltpu.roll(value, 1, 0))


def first_kernel(d_ref, v_ref, kx_ref, ky_ref, kz_ref, kick_ref, u_ref, w_ref, yc_ref, yd_ref):
    _, planes, rows, cols = u_ref.shape
    even_y = lax.axis_index("yz") % 2 == 0

    def plane(i, carried, ahead):
        return tuple(
            advance_plane(
                c, i, d_ref[c, i] * U_SCALE, ahead and d_ref[c, i + 1] * U_SCALE, v_ref[c, i] * W_SCALE, carried[c],
                kx_ref[i], ky_ref[i], kz_ref[i], kick_ref[i], u_ref, w_ref, (yc_ref, yd_ref), even_y,
            )
            for c in range(3)
        )

    zero = jnp.zeros((rows, cols), jnp.float32)
    carried = lax.fori_loop(
        0, planes - 1, lambda i, carried: plane(i, carried, True), (zero,) * 3, unroll=math.gcd(3, planes - 1)
    )
    plane(planes - 1, carried, False)


def edge_kernel(
    sa_ref, sb_ref, sc_ref, sd_ref, ra_ref, rb_ref, rc_ref, rd_ref, corner_ref,
    kick_ref, row_kick_ref, high_ky_ref, kx_in, ky_in, kz_in, moduli_ref,
    kx_ref, ky_ref, kz_ref, ka_ref, kb_ref, kc_ref, kd_ref, ex_ref, ey_ref,
):
    planes, rows, cols = kick_ref.shape
    place = here_in_mesh()
    even_x, even_y = place[0] % 2 == 0, place[2] % 2 == 0
    inner_x, inner_y = place[0] > 0, place[2] > 0
    last_x = place[0] == place[1] - 1
    last_y = place[2] == place[3] - 1
    row = lax.broadcasted_iota(jnp.int32, (rows, cols), 0)
    plane = lax.broadcasted_iota(jnp.int32, (planes, cols), 0)

    def looked_up(kinds, keep):
        stiff = jnp.zeros(kinds.shape, jnp.float32)
        for m in range(moduli_ref.shape[0]):
            stiff = jnp.where(kinds == m, moduli_ref[m] * STIFF, stiff)
        col = lax.broadcasted_iota(jnp.int32, kinds.shape, 1)
        return jnp.where((col < cols - 1) & keep, stiff, 0.0)

    def with_behind(value):
        return value + pltpu.roll(value, 1, 1)

    below_x = looked_up(
        jnp.where(even_x, rb_ref[3], ra_ref[3]), inner_x & ((row < rows - 1) | jnp.logical_not(last_y))
    )
    below_y = looked_up(
        jnp.where(even_y, rd_ref[3], rc_ref[3]), inner_y & ((plane < planes - 1) | jnp.logical_not(last_x))
    )
    corner = looked_up(corner_ref[...], inner_x & inner_y)
    s_x, s_y, s_corner = with_behind(below_x), with_behind(below_y), with_behind(corner)

    x_low = kick_ref[0] * (s_x + rows_behind(s_x, row, s_corner))
    y_low = row_kick_ref[0] * (s_y + rows_behind(s_y, plane, s_corner))
    plane_ky = jnp.where(row < rows - 1, s_x, 0.0)
    plane_kz = below_x + rows_behind(below_x, row, corner)
    rows_kx = jnp.where(plane < planes - 1, s_y, 0.0)
    rows_kz = below_y + rows_behind(below_y, plane)

    ky_ref[0] += plane_ky
    kz_ref[0] += plane_kz
    for i in range(planes):
        kx_ref[i, 0:1] += s_y[i : i + 1]
        kz_ref[i, 0:1] += rows_kz[i : i + 1]
    x_high = kick_ref[planes - 1] * kx_ref[planes - 1]
    y_high = (high_ky_ref[...] + jnp.where(plane == 0, s_x[rows - 1 : rows], 0.0)) * row_kick_ref[1]
    ka_ref[...] = jnp.where(even_x, x_high, x_low)
    kb_ref[...] = jnp.where(even_x, x_low, x_high)
    kc_ref[...] = jnp.where(even_y, y_high, y_low)
    kd_ref[...] = jnp.where(even_y, y_low, y_high)

    for c in range(3):
        u = jnp.where(even_x, sb_ref[c], sa_ref[c]) * U_SCALE
        pull_y = plane_ky * jnp.tanh(pltpu.roll(u, rows - 1, 0) - u)
        pull_z = plane_kz * jnp.tanh(pltpu.roll(u, cols - 1, 1) - u)
        ex_ref[c] = kick_ref[0] * (pull_y - pltpu.roll(pull_y, 1, 0) + (pull_z - pltpu.roll(pull_z, 1, 1)))
        u = jnp.where(even_y, sd_ref[c], sc_ref[c]) * U_SCALE
        pull_x = rows_kx * jnp.tanh(pltpu.roll(u, planes - 1, 0) - u)
        pull_z = rows_kz * jnp.tanh(pltpu.roll(u, cols - 1, 1) - u)
        ey_ref[c] = row_kick_ref[0] * (pull_x - pltpu.roll(pull_x, 1, 0) + (pull_z - pltpu.roll(pull_z, 1, 1)))


def interior_kernel(
    last, u_in, w_in, kx_ref, ky_ref, kz_ref, kick_ref, xl_ref, xh_ref, yl_ref, yh_ref, u_ref, w_ref, *side_refs
):
    _, planes, rows, cols = u_ref.shape
    even_y = lax.axis_index("yz") % 2 == 0
    for ref in (u_ref, w_ref):
        for c in range(3):
            ref[c, 0] += xl_ref[c]
            ref[c, planes - 1] += xh_ref[c]

    def fixed(ref, c, i):
        return with_sides(ref[c, i], yl_ref[c, pl.ds(i, 1)], yh_ref[c, pl.ds(i, 1)])

    def plane(i, carried, ahead):
        return tuple(
            advance_plane(
                c, i, fixed(u_ref, c, i), ahead and fixed(u_ref, c, i + 1), fixed(w_ref, c, i), carried[c],
                kx_ref[i], ky_ref[i], kz_ref[i], kick_ref[i], u_ref, w_ref, side_refs, even_y, last,
            )
            for c in range(3)
        )

    zero = jnp.zeros((rows, cols), jnp.float32)
    carried = lax.fori_loop(
        0, planes - 1, lambda i, carried: plane(i, carried, True), (zero,) * 3, unroll=math.gcd(3, planes - 1)
    )
    plane(planes - 1, carried, False)


def with_sides(value, low, high):
    rows, cols = value.shape
    tile = math.gcd(8, rows)
    row = lax.broadcasted_iota(jnp.int32, (tile, cols), 0)
    low, high = jnp.where(row == 0, low, 0.0), jnp.where(row == tile - 1, high, 0.0)
    if rows == tile:
        return value + (low + high)
    middle = [value[tile : rows - tile]] if rows > 2 * tile else []
    return jnp.concatenate([value[0:tile] + low, *middle, value[rows - tile :] + high], axis=0)


def advance_plane(
    c, i, here, ahead, w, carried, kx, ky, kz, kick, u_ref, w_ref, side_refs, even_y, last=False
):
    rows, cols = here.shape
    force = -carried
    pull_x = None
    if ahead is not False:
        pull_x = kx * jnp.tanh(ahead - here)
        force = force + pull_x
    pull_y = ky * jnp.tanh(pltpu.roll(here, rows - 1, 0) - here)
    force = force + (pull_y - pltpu.roll(pull_y, 1, 0))
    pull_z = kz * jnp.tanh(pltpu.roll(here, cols - 1, 1) - here)
    force = force + (pull_z - pltpu.roll(pull_z, 1, 1))
    w = w + kick * force
    u = here + w
    if last:
        u_ref[c, i] = u * (1.0 / U_SCALE)
        w_ref[c, i] = w * (1.0 / W_SCALE)
        return pull_x
    w_ref[c, i] = w
    u_ref[c, i] = u
    low, high = u[0:1], u[rows - 1 : rows]
    yc_ref, yd_ref = side_refs
    yc_ref[c, pl.ds(i, 1)] = jnp.where(even_y, high, low)
    yd_ref[c, pl.ds(i, 1)] = jnp.where(even_y, low, high)
    return pull_x


def contact_kernel(own_ref, near_ref, far_ref, pick_ref, push_ref, out_ref, *scratch):
    @pl.when(on_face())
    def _():
        def matched(c):
            pool = jnp.concatenate([near_ref[c], far_ref[c]], axis=0)
            return lax.dot_general(
                pool, pick_ref[...], (((0,), (0,)), ((), ())),
                precision=lax.Precision.HIGHEST, preferred_element_type=jnp.float32,
            )

        out_ref[...] = pressures(U_SCALE, lambda c: own_ref[c], matched, out_ref.shape, *scratch) * push_ref[...]

    @pl.when(jnp.logical_not(on_face()))
    def _():
        out_ref[...] = jnp.zeros_like(out_ref)


def listed_contact_kernel(
    own_half_ref, own_rest_ref, half_ref, rest_ref, push_ref, chosen_ref, out_ref, list_ref, *scratch
):
    rows, cols = out_ref.shape

    @pl.when(on_face())
    def _():
        def matched(c):
            return jnp.concatenate([half_ref[c], rest_ref[c]] * (scratch[0].shape[1] // rows), axis=0).T

        def own(c):
            return jnp.concatenate([own_half_ref[c], own_rest_ref[c]], axis=0)

        list_ref[...] = pressures(1.0, own, matched, out_ref.shape, *scratch)
        for r in range(rows):
            out_ref[pl.ds(chosen_ref[r], 1)] = list_ref[r : r + 1]
        out_ref[...] = out_ref[...] * push_ref[...]

    @pl.when(jnp.logical_not(on_face()))
    def _():
        out_ref[...] = jnp.zeros_like(out_ref)


def on_face():
    return lax.axis_index("gx") == lax.axis_size("gx") - 1


def pressures(scale, own_rows, matched, shape, fp_ref, fy_ref, fz_ref, base_ref, total_ref):
    rows, cols = shape
    lanes = fp_ref.shape[1]
    parts = lanes // rows
    deep = cols // parts

    lane = lax.broadcasted_iota(jnp.int32, (deep, lanes), 1)
    depth = lax.broadcasted_iota(jnp.int32, (deep, lanes), 0)

    def own(c):
        turned = jnp.concatenate([own_rows(c)] * parts, axis=0).T
        value = turned[0:deep]
        for h in range(1, parts):
            value = jnp.where(lane >= h * rows, turned[h * deep : (h + 1) * deep], value)
        return value

    gap = scale * GAP_SCALE
    along = scale * YIELD_SPAN * SPAN
    fp_ref[...] = jnp.exp2(matched(0) * gap - BIAS / 2.0)
    fy = matched(1) * along
    fy_ref[...] = fy
    spot = lax.broadcasted_iota(jnp.int32, (cols, lanes), 0).astype(jnp.float32)
    fz = matched(2) * along
    fy_square = fy * fy + SHIFT
    width = math.gcd(32, deep)
    middle = (lax.broadcasted_iota(jnp.int32, (cols, lanes), 1) // rows * deep + width // 2).astype(jnp.float32)
    for k in range(deep // width):
        z = fz + (spot - (middle + k * width)) * SPAN
        fz_ref[k] = z
        base_ref[k] = -(z * z + fy_square)
    mine = (depth % width - width // 2).astype(jnp.float32)
    op = jnp.exp2(own(0) * gap - BIAS / 2.0)
    oy = own(1) * along
    oz = own(2) * along + mine * SPAN

    own_power = jnp.exp2(SHIFT - (oy * oy + oz * oz))
    oy, oz = oy * 2.0, oz * 2.0
    for k in range(deep // width):
        some = slice(k * width, (k + 1) * width)
        total = jnp.zeros((width, lanes), jnp.float32)
        for m in range(cols):
            at = slice(m, m + 1)
            weight = jnp.exp2(oz[some] * fz_ref[k, at] + (oy[some] * fy_ref[at] + base_ref[k, at]))
            soft = jnp.log2(op[some] * fp_ref[at] + 2.0**-BIAS) + BIAS
            total = total + weight * soft
        total = total * own_power[some]
        total_ref[some] = total
    turned = jnp.concatenate([total_ref[...]] * parts, axis=0).T
    column = lax.broadcasted_iota(jnp.int32, (rows, cols), 1)
    value = turned[0:rows]
    for h in range(1, parts):
        value = jnp.where(column >= h * deep, turned[h * rows : (h + 1) * rows], value)
    return value


def last_contact_kernel(*refs):
    meet, (u_ref, w_ref, d_ref, v_ref, out_ref, *scratch, sems) = refs[:6], refs[6:]
    copies = [
        pltpu.make_async_copy(u_ref, d_ref, sems.at[0]),
        pltpu.make_async_copy(w_ref, v_ref, sems.at[1]),
    ]
    for copy in copies:
        copy.start()
    listed_contact_kernel(*meet, out_ref, *scratch)
    for copy in copies:
        copy.wait()


def link_moves(scale, extra, sent, got, edges, push_ref, c):
    moves = []
    for n in range(4):
        arrived = jnp.concatenate([half[c] for half in got[n]], axis=0) if isinstance(got[n], tuple) else got[n][c]
        stretch = arrived - sent[n][c]
        if scale != 1.0:
            stretch = stretch * scale
        moves.append(edges[n][...] * jnp.tanh(stretch))
    if c == 0:
        moves[1] = moves[1] + push_ref[...]
    a, b, c_, d = moves
    even_x, even_y = lax.axis_index("gx") % 2 == 0, lax.axis_index("yz") % 2 == 0
    moves = [jnp.where(even_x, b, a), jnp.where(even_x, a, b), jnp.where(even_y, d, c_), jnp.where(even_y, c_, d)]
    if extra:
        moves[0] = moves[0] + extra[0][c]
        moves[2] = moves[2] + extra[1][c]
    return moves


def arrivals(refs, n_got):
    sent, got, edges, refs = refs[:4], refs[4 : 4 + n_got], refs[4 + n_got : 8 + n_got], refs[8 + n_got :]
    if n_got == 5:
        a, half, rest, c, d = got
        got = [a, (half, rest), c, d]
    return sent, got, edges, refs


def boundary_kernel(scale, n_extra, n_got, *refs):
    extra, refs = refs[:n_extra], refs[n_extra:]
    u_ref, yc_ref, yd_ref, *refs = refs
    sent, got, edges, refs = arrivals(refs, n_got)
    push_ref, chosen_ref, na_ref, nb_ref, nc_ref, nd_ref, *refs = refs
    half_ref, rest_ref, xl_ref, xh_ref, yl_ref, yh_ref = refs
    _, planes, rows, cols = u_ref.shape
    even_x, even_y = lax.axis_index("gx") % 2 == 0, lax.axis_index("yz") % 2 == 0
    for c in range(3):
        xl, xh, yl, yh = link_moves(scale, extra, sent, got, edges, push_ref, c)
        xl_ref[c], xh_ref[c], yl_ref[c], yh_ref[c] = xl, xh, yl, yh
        low = with_sides(u_ref[c, 0] + xl, yl[0:1], yh[0:1])
        high = with_sides(u_ref[c, planes - 1] + xh, yl[planes - 1 :], yh[planes - 1 :])
        na_ref[c], nb_ref[c] = jnp.where(even_x, high, low), jnp.where(even_x, low, high)
        first = xl[0:1], xh[0:1]
        last = xl[rows - 1 :], xh[rows - 1 :]
        c_low, c_high = (jnp.where(even_y, y, x) for x, y in zip(first, last))
        d_low, d_high = (jnp.where(even_y, x, y) for x, y in zip(first, last))
        nc_ref[c] = with_sides(yc_ref[c] + jnp.where(even_y, yh, yl), c_low, c_high)
        nd_ref[c] = with_sides(yd_ref[c] + jnp.where(even_y, yl, yh), d_low, d_high)
    half = rows // 2

    @pl.when(on_face())
    def _():
        for n, ref in enumerate((half_ref, rest_ref)):
            for r in range(half):
                at = chosen_ref[n * half + r]
                for c in range(3):
                    ref[c, r : r + 1] = nb_ref[c, pl.ds(at, 1)]

    @pl.when(jnp.logical_not(on_face()))
    def _():
        for c in range(3):
            half_ref[c], rest_ref[c] = nb_ref[c, :half], nb_ref[c, half:]


def finish_kernel(*refs):
    u_ref, w_ref, _, _, *refs = refs
    sent, got, edges, refs = arrivals(refs, 5)
    push_ref, d_ref, v_ref, planes_ref, rows_ref, sems = refs
    _, planes, rows, cols = u_ref.shape
    tile = rows_ref.shape[4]
    inner = slice(1, planes - 1)
    copies = []
    moves = [link_moves(1.0, (), sent, got, edges, push_ref, c) for c in range(3)]
    results = ((u_ref, d_ref, 1.0 / U_SCALE), (w_ref, v_ref, 1.0 / W_SCALE))
    for n, (ref, out, scale) in enumerate(results):
        for side, at in ((0, 0), (1, rows - tile)):
            for c in range(3):
                fix = moves[c][2 + side] * scale
                for i in range(1, planes - 1):
                    value = ref[c, i, at : at + tile]
                    line = fix[i : i + 1]
                    row = lax.broadcasted_iota(jnp.int32, (tile, cols), 0)
                    rows_ref[n, side, c, i - 1] = value + jnp.where(row == (tile - 1 if side else 0), line, 0.0)
            copies.append(
                pltpu.make_async_copy(
                    rows_ref.at[n, side], out.at[:, inner, at : at + tile], sems.at[len(copies)]
                )
            )
            copies[-1].start()
    for n, (ref, out, scale) in enumerate(results):
        for side, i in ((0, 0), (1, planes - 1)):
            for c in range(3):
                xl, xh, yl, yh = moves[c]
                value = ref[c, i] + (xh if side else xl) * scale
                planes_ref[n, side, c] = with_sides(value, yl[i : i + 1] * scale, yh[i : i + 1] * scale)
            copies.append(pltpu.make_async_copy(planes_ref.at[n, side], out.at[:, i], sems.at[len(copies)]))
            copies[-1].start()
    for copy in copies:
        copy.wait()


def routes(count_body, count_x, count_y):
    def number(b, g, y):
        return (b * count_x + g) * count_y + y

    every = [(b, g, y) for b in range(count_body) for g in range(count_x) for y in range(count_y)]

    def pairs(target):
        return [(number(*at), number(*target(*at))) for at in every]

    def outer_x(b, g, y):
        if g == count_x - 1:
            return 1 - b, g, y
        return (b, (g + 1 if g % 2 else g - 1), y) if g else (b, g, y ^ 1)

    def diagonal(b, g, y):
        if g == count_x - 1:
            return 1 - b, g, (y - 1 if b else y + 1) % count_y
        return b, g, y ^ 1

    return {
        "a": pairs(lambda b, g, y: (b, g ^ 1, y)),
        "b": pairs(outer_x),
        "rest": pairs(lambda b, g, y: diagonal(b, g, y) if g == count_x - 1 else outer_x(b, g, y)),
        "c": pairs(lambda b, g, y: (b, g, y ^ 1)),
        "d": pairs(lambda b, g, y: (b, g, (y + 1 if y % 2 else y - 1) % count_y)),
        "e": pairs(diagonal),
        "corner": pairs(lambda b, g, y: (b, (g + 1) % count_x, (y + 1) % count_y)),
    }


def local(displacement, velocity, material, moduli, density, partner, active):
    planes, rows, cols = displacement.shape[2:]
    route = routes(lax.axis_size("body"), lax.axis_size("gx"), lax.axis_size("yz"))
    lanes = max(cols, 2 * rows)
    tile = math.gcd(8, rows)
    block, face, side = (planes, rows, cols), (rows, cols), (planes, cols)
    state, face3, side3 = (3, *block), (3, *face), (3, *side)
    d, v, kinds = displacement[0], velocity[0], material[0]
    smem, hbm = pltpu.SMEM, pltpu.HBM

    def passed(block, name):
        return lax.ppermute(block, AXES, route[name])

    *sent, spare, corner = call(
        pack_kernel,
        [vmem((4, *face))] * 2 + [vmem((4, *side))] * 2 + [vmem(face3), vmem((1, cols))],
        [d, kinds],
        [hbm, hbm],
        scratch=[
            pltpu.VMEM((2, *face), jnp.int32),
            vmem((2, 3, planes, tile, cols)),
            pltpu.VMEM((2, planes, tile, cols), jnp.int32),
            pltpu.SemaphoreType.DMA((8,)),
        ],
    )
    got_e = passed(spare, "e")
    got = [passed(block, name) for block, name in zip(sent, "abcd")]
    kx, ky, kz, kick, row_kick, high_ky, push_scale, pick, chosen, got[2] = call(
        setup_kernel,
        [vmem(block)] * 4 + [vmem((2, *side)), vmem(side), vmem(face), vmem((lanes, lanes))]
        + [pltpu.SMEM((rows + 1,), jnp.int32), vmem((4, *side))],
        [kinds, got[2], d, moduli, density, partner, active],
        [None, None, None] + [smem] * 4,
        aliases={1: 9},
        scratch=[vmem((rows + tile, lanes)), vmem((rows + tile, cols))],
        flops=8_000_000,
    )
    deep = cols * rows // lanes
    pair_scratch = [vmem((cols, lanes))] * 2 + [vmem((deep // math.gcd(32, deep), cols, lanes))] * 2 + [vmem((deep, lanes))]
    for step in range(STEPS):
        first, last = step == 0, step == STEPS - 1
        scale = U_SCALE if first else 1.0
        if first:
            corner, kick = lax.optimization_barrier((corner, kick))
            corner = passed(corner, "corner")
            u, w, *sides = call(
                first_kernel,
                [vmem(state)] * 2 + [vmem(side3)] * 2,
                [d, v, kx, ky, kz, kick],
            )
            push_scale, sides[0] = lax.optimization_barrier((push_scale, sides[0]))
        else:
            got_half, got_e = passed(half, "b"), passed(rest, "rest")
            got = [passed(sent[0], "a"), got_half, got_e, passed(sent[2], "c"), passed(sent[3], "d")]
            u, w, *sides = call(
                functools.partial(interior_kernel, last),
                [vmem(state)] * 2 + [vmem(side3)] * (0 if last else 2),
                [u, w, kx, ky, kz, kick, *moves],
                aliases={0: 0, 1: 1},
                flops=20_000_000,
            )
        if not first:
            meet = [half, rest, got_half, got_e, push_scale, chosen]
        if last:
            d, v, push = call(
                last_contact_kernel,
                [jax.ShapeDtypeStruct(state, jnp.float32)] * 2 + [vmem(face)],
                [*meet, u, w],
                [None] * 5 + [smem] + [None] * 2,
                scratch=[vmem(face), *pair_scratch, pltpu.SemaphoreType.DMA((2,))],
                hbm_outs=2,
                flops=20_000_000,
            )
            break
        if first:
            (push,) = call(
                contact_kernel, [vmem(face)], [sent[1], got[1], got_e, pick, push_scale], scratch=pair_scratch
            )
        else:
            (push,) = call(
                listed_contact_kernel,
                [vmem(face)],
                meet,
                [None] * 5 + [smem],
                scratch=[vmem(face), *pair_scratch],
                flops=20_000_000,
            )
        extra = []
        if first:
            kx, ky, kz, *rest = call(
                edge_kernel,
                [vmem(block)] * 3 + [vmem(face)] * 2 + [vmem(side)] * 2 + [vmem(face3), vmem(side3)],
                [*sent, *got, corner, kick, row_kick, high_ky, kx, ky, kz, moduli],
                [None] * 15 + [smem],
                aliases={12: 0, 13: 1, 14: 2},
            )
            edges, extra = rest[:4], rest[4:]
        *sent, half, rest, xl, xh, yl, yh = call(
            functools.partial(boundary_kernel, scale, len(extra), len(got)),
            [vmem(face3)] * 2 + [vmem(side3)] * 2 + [vmem((3, rows // 2, cols))] * 2
            + [vmem(face3)] * 2 + [vmem(side3)] * 2,
            [*extra, u, *sides, *sent, *got, *edges, push, chosen],
            [None] * (12 + len(got) + len(extra)) + [smem],
        )
        moves = [xl, xh, yl, yh]
    d, v = call(
        finish_kernel,
        [jax.ShapeDtypeStruct(state, jnp.float32)] * 2,
        [u, w, d, v, *sent, *got, *edges, push],
        [None, None, hbm, hbm] + [None] * 14,
        aliases={2: 0, 3: 1},
        scratch=[vmem((2, 2, *face3)), vmem((2, 2, 3, planes - 2, tile, cols)), pltpu.SemaphoreType.DMA((8,))],
        hbm_outs=2,
    )
    return d[None], v[None]


def solution(mesh):
    in_specs = (
        P("body", None, "gx", "yz", None),
        P("body", None, "gx", "yz", None),
        P("body", "gx", "yz", None),
        P(),
        P(),
        P(),
        P(),
    )
    out_specs = (P("body", None, "gx", "yz", None), P("body", None, "gx", "yz", None))
    return jax.shard_map(local, mesh=mesh, in_specs=in_specs, out_specs=out_specs, check_vma=False)
```

```python
import functools
import math

import jax
import jax.numpy as jnp
from jax import lax
from jax.experimental import pallas as pl
from jax.experimental.pallas import tpu as pltpu
from jax.sharding import PartitionSpec as P

STEPS = 4
STEP_TIME = 0.2
YIELD_SPAN = 0.5
PENALTY = 4.0
SOFT_WIDTH = 0.1
KERNEL_WIDTH = 1.5

U_SCALE = 1.0 / YIELD_SPAN
W_SCALE = STEP_TIME / YIELD_SPAN
KICK = STEP_TIME * STEP_TIME / YIELD_SPAN
LOG2E = math.log2(math.e)
GAP_SCALE = YIELD_SPAN / SOFT_WIDTH * LOG2E
SPAN = math.sqrt(LOG2E / (2.0 * KERNEL_WIDTH * KERNEL_WIDTH))
PRESSURE_SCALE = PENALTY * SOFT_WIDTH / LOG2E
STIFF = 0.25 * YIELD_SPAN
BIAS = 32.0
SHIFT = 64.0

AXES = ("body", "gx", "yz")
VMEM_LIMIT = 48 * 1024 * 1024


def vmem(shape):
    return pltpu.VMEM(shape, jnp.float32)


def call(kernel, outs, args, spaces=None, aliases=None, scratch=(), flops=0, moved=0, hbm_outs=0):
    spaces = spaces or [None] * len(args)
    specs, placed = [], []
    for arg, space in zip(args, spaces):
        if space is None:
            placed.append(pltpu.with_memory_space_constraint(arg, pltpu.VMEM))
            specs.append(pl.BlockSpec(memory_space=pltpu.VMEM))
        else:
            placed.append(pltpu.with_memory_space_constraint(arg, space) if space == pltpu.HBM else arg)
            specs.append(pl.BlockSpec(memory_space=space))
    return pl.pallas_call(
        kernel,
        out_shape=outs,
        in_specs=specs,
        out_specs=[
            pl.BlockSpec(memory_space=pl.ANY if n < hbm_outs else getattr(out, "memory_space", pltpu.VMEM))
            for n, out in enumerate(outs)
        ],
        input_output_aliases=aliases or {},
        scratch_shapes=list(scratch),
        compiler_params=pltpu.CompilerParams(vmem_limit_bytes=VMEM_LIMIT),
        cost_estimate=pl.CostEstimate(flops=flops, bytes_accessed=moved, transcendentals=0),
    )(*placed)


def here_in_mesh():
    return (
        lax.axis_index("gx"), lax.axis_size("gx"), lax.axis_index("yz"), lax.axis_size("yz"), lax.axis_index("body")
    )


def pack_kernel(
    d_ref, mat_ref, sa_ref, sb_ref, sc_ref, sd_ref, se_ref, corner_ref, plane_ref, rows_ref, kinds_ref, sems,
):
    planes, rows, cols = mat_ref.shape
    place = here_in_mesh()
    ia, ib, jc, jd = links(place, planes, rows)
    copies = []
    for n, (ref, i) in enumerate(((sa_ref, ia), (sb_ref, ib))):
        copies.append(pltpu.make_async_copy(d_ref.at[:, i], ref.at[0:3], sems.at[n]))
        copies.append(pltpu.make_async_copy(mat_ref.at[i], plane_ref.at[n], sems.at[2 + n]))
    for n, j in enumerate((jc, jd)):
        copies.append(pltpu.make_async_copy(d_ref.at[:, :, pl.ds(j, 1)], rows_ref.at[n], sems.at[4 + n]))
        copies.append(pltpu.make_async_copy(mat_ref.at[:, pl.ds(j, 1)], kinds_ref.at[n], sems.at[6 + n]))
    for copy in copies:
        copy.start()
    for copy in copies:
        copy.wait()
    kinds_a, kinds_b = plane_ref[0].astype(jnp.float32), plane_ref[1].astype(jnp.float32)
    sa_ref[3], sb_ref[3] = kinds_a, kinds_b
    for c in range(3):
        se_ref[c] = sb_ref[c]
    corner_ref[...] = jnp.where(place[0] % 2 == 0, kinds_a[rows - 1 :], kinds_b[rows - 1 :])
    for n, ref in enumerate((sc_ref, sd_ref)):
        for i in range(planes):
            for c in range(3):
                ref[c, i : i + 1] = rows_ref[n, c, i]
            ref[3, i : i + 1] = kinds_ref[n, i].astype(jnp.float32)


def links(place, planes, rows):
    ia = jnp.where(place[0] % 2 == 0, planes - 1, 0)
    jc = jnp.where(place[2] % 2 == 0, rows - 1, 0)
    return ia, planes - 1 - ia, jc, rows - 1 - jc


def setup_kernel(
    kinds_ref, rc_in, d_ref, moduli_ref, density_ref, partner_ref, active_ref,
    kx_ref, ky_ref, kz_ref, kick_ref, row_kick_ref, high_ky_ref, push_ref, pick_ref, chosen_ref, rc_ref,
    turned_ref, live_ref,
):
    planes, rows, cols = kinds_ref.shape
    place = here_in_mesh()
    last_x = place[0] == place[1] - 1
    last_y = place[2] == place[3] - 1
    row = lax.broadcasted_iota(jnp.int32, (rows, cols), 0)
    col = lax.broadcasted_iota(jnp.int32, (rows, cols), 1)
    inside = (col < cols - 1) & ((row < rows - 1) | jnp.logical_not(last_y))

    del rc_in, d_ref

    body, blocks = place[4], place[3]
    start = place[2] * rows
    other = jnp.where(body == 0, place[2] + 1, place[2] + blocks - 1) % blocks * rows

    @pl.when(last_x)
    def _():
        lane = lax.broadcasted_iota(jnp.int32, (1, turned_ref.shape[1]), 1)

        def meet(i, counts):
            new = []
            for n, (block, count) in enumerate(zip((start, other), counts)):
                b = jnp.where(body == 0, start, block) + i
                p = partner_ref[b]
                at = p - jnp.where(body == 0, block, start)
                mine = (at >= 0) & (at < rows)
                r = jnp.where(body == 0, i, at)
                row = pl.ds(jnp.where(mine, r, rows), 1)
                turned_ref[row] = jnp.where(lane == jnp.where(body == 0, at, i) + n * rows, 1.0, 0.0)
                live_ref[row] = jnp.where(lane[:, :cols] >= 0, active_ref[b].astype(jnp.float32), 0.0)
                chosen_ref[jnp.where(mine, count, rows)] = r
                new.append(count + mine.astype(jnp.int32))
            return tuple(new)

        lax.fori_loop(0, rows, meet, (jnp.int32(0), jnp.int32(rows // 2)), unroll=4)
        turned = turned_ref[0:rows]
        pick_ref[...] = jnp.concatenate([turned] * (pick_ref.shape[1] // rows), axis=0).T
        push_ref[...] = live_ref[0:rows] * (-PRESSURE_SCALE)

    @pl.when(jnp.logical_not(last_x))
    def _():
        push_ref[...] = jnp.zeros_like(push_ref)
        pick_ref[...] = jnp.zeros_like(pick_ref)

        def any_row(r, _):
            chosen_ref[r] = 0
            return 0

        lax.fori_loop(0, chosen_ref.shape[0], any_row, 0, unroll=8)

    def plane(i, earlier):
        kinds = kinds_ref[i]
        stiff = jnp.zeros((rows, cols), jnp.float32)
        mass = jnp.ones((rows, cols), jnp.float32)
        for m in range(moduli_ref.shape[0]):
            hit = kinds == m
            stiff = jnp.where(hit, moduli_ref[m] * STIFF, stiff)
            mass = jnp.where(hit, density_ref[m], mass)
        keep = inside & ((i < planes - 1) | jnp.logical_not(last_x))
        here = jnp.where(keep, stiff, 0.0)
        kick = KICK / mass
        kick_ref[i] = kick
        row_kick_ref[0, pl.ds(i, 1)] = kick[0:1]
        row_kick_ref[1, pl.ds(i, 1)] = kick[rows - 1 : rows]
        s = here + pltpu.roll(here, 1, 1)
        both = here + earlier
        ky = both + pltpu.roll(both, 1, 1)
        high_ky_ref[pl.ds(i, 1)] = ky[rows - 1 : rows]
        kx_ref[i] = s + rows_behind(s, row)
        ky_ref[i] = jnp.where(row < rows - 1, ky, 0.0)
        kz_ref[i] = both + rows_behind(both, row)
        return here

    lax.fori_loop(0, planes, plane, jnp.zeros((rows, cols), jnp.float32), unroll=math.gcd(16, planes))
    push_ref[...] = push_ref[...] * kick_ref[planes - 1]


def rows_behind(value, row, first=0.0):
    return jnp.where(row == 0, first, pltpu.roll(value, 1, 0))


def first_kernel(d_ref, v_ref, kx_ref, ky_ref, kz_ref, kick_ref, u_ref, w_ref, yc_ref, yd_ref):
    _, planes, rows, cols = u_ref.shape
    even_y = lax.axis_index("yz") % 2 == 0

    def plane(i, carried, ahead):
        return tuple(
            advance_plane(
                c, i, d_ref[c, i] * U_SCALE, ahead and d_ref[c, i + 1] * U_SCALE, v_ref[c, i] * W_SCALE, carried[c],
                kx_ref[i], ky_ref[i], kz_ref[i], kick_ref[i], u_ref, w_ref, (yc_ref, yd_ref), even_y,
            )
            for c in range(3)
        )

    zero = jnp.zeros((rows, cols), jnp.float32)
    carried = lax.fori_loop(
        0, planes - 1, lambda i, carried: plane(i, carried, True), (zero,) * 3, unroll=math.gcd(3, planes - 1)
    )
    plane(planes - 1, carried, False)


def edge_kernel(
    sa_ref, sb_ref, sc_ref, sd_ref, ra_ref, rb_ref, rc_ref, rd_ref, corner_ref,
    kick_ref, row_kick_ref, high_ky_ref, kx_in, ky_in, kz_in, moduli_ref,
    kx_ref, ky_ref, kz_ref, ka_ref, kb_ref, kc_ref, kd_ref, ex_ref, ey_ref,
):
    planes, rows, cols = kick_ref.shape
    place = here_in_mesh()
    even_x, even_y = place[0] % 2 == 0, place[2] % 2 == 0
    inner_x, inner_y = place[0] > 0, place[2] > 0
    last_x = place[0] == place[1] - 1
    last_y = place[2] == place[3] - 1
    row = lax.broadcasted_iota(jnp.int32, (rows, cols), 0)
    plane = lax.broadcasted_iota(jnp.int32, (planes, cols), 0)

    def looked_up(kinds, keep):
        stiff = jnp.zeros(kinds.shape, jnp.float32)
        for m in range(moduli_ref.shape[0]):
            stiff = jnp.where(kinds == m, moduli_ref[m] * STIFF, stiff)
        col = lax.broadcasted_iota(jnp.int32, kinds.shape, 1)
        return jnp.where((col < cols - 1) & keep, stiff, 0.0)

    def with_behind(value):
        return value + pltpu.roll(value, 1, 1)

    below_x = looked_up(
        jnp.where(even_x, rb_ref[3], ra_ref[3]), inner_x & ((row < rows - 1) | jnp.logical_not(last_y))
    )
    below_y = looked_up(
        jnp.where(even_y, rd_ref[3], rc_ref[3]), inner_y & ((plane < planes - 1) | jnp.logical_not(last_x))
    )
    corner = looked_up(corner_ref[...], inner_x & inner_y)
    s_x, s_y, s_corner = with_behind(below_x), with_behind(below_y), with_behind(corner)

    x_low = kick_ref[0] * (s_x + rows_behind(s_x, row, s_corner))
    y_low = row_kick_ref[0] * (s_y + rows_behind(s_y, plane, s_corner))
    plane_ky = jnp.where(row < rows - 1, s_x, 0.0)
    plane_kz = below_x + rows_behind(below_x, row, corner)
    rows_kx = jnp.where(plane < planes - 1, s_y, 0.0)
    rows_kz = below_y + rows_behind(below_y, plane)

    ky_ref[0] += plane_ky
    kz_ref[0] += plane_kz
    for i in range(planes):
        kx_ref[i, 0:1] += s_y[i : i + 1]
        kz_ref[i, 0:1] += rows_kz[i : i + 1]
    x_high = kick_ref[planes - 1] * kx_ref[planes - 1]
    y_high = (high_ky_ref[...] + jnp.where(plane == 0, s_x[rows - 1 : rows], 0.0)) * row_kick_ref[1]
    ka_ref[...] = jnp.where(even_x, x_high, x_low)
    kb_ref[...] = jnp.where(even_x, x_low, x_high)
    kc_ref[...] = jnp.where(even_y, y_high, y_low)
    kd_ref[...] = jnp.where(even_y, y_low, y_high)

    for c in range(3):
        u = jnp.where(even_x, sb_ref[c], sa_ref[c]) * U_SCALE
        pull_y = plane_ky * jnp.tanh(pltpu.roll(u, rows - 1, 0) - u)
        pull_z = plane_kz * jnp.tanh(pltpu.roll(u, cols - 1, 1) - u)
        ex_ref[c] = kick_ref[0] * (pull_y - pltpu.roll(pull_y, 1, 0) + (pull_z - pltpu.roll(pull_z, 1, 1)))
        u = jnp.where(even_y, sd_ref[c], sc_ref[c]) * U_SCALE
        pull_x = rows_kx * jnp.tanh(pltpu.roll(u, planes - 1, 0) - u)
        pull_z = rows_kz * jnp.tanh(pltpu.roll(u, cols - 1, 1) - u)
        ey_ref[c] = row_kick_ref[0] * (pull_x - pltpu.roll(pull_x, 1, 0) + (pull_z - pltpu.roll(pull_z, 1, 1)))


def interior_kernel(
    last, u_in, w_in, kx_ref, ky_ref, kz_ref, kick_ref, xl_ref, xh_ref, yl_ref, yh_ref, u_ref, w_ref, *side_refs
):
    _, planes, rows, cols = u_ref.shape
    even_y = lax.axis_index("yz") % 2 == 0
    for ref in (u_ref, w_ref):
        for c in range(3):
            ref[c, 0] += xl_ref[c]
            ref[c, planes - 1] += xh_ref[c]

    def fixed(ref, c, i):
        return with_sides(ref[c, i], yl_ref[c, pl.ds(i, 1)], yh_ref[c, pl.ds(i, 1)])

    def plane(i, carried, ahead):
        return tuple(
            advance_plane(
                c, i, fixed(u_ref, c, i), ahead and fixed(u_ref, c, i + 1), fixed(w_ref, c, i), carried[c],
                kx_ref[i], ky_ref[i], kz_ref[i], kick_ref[i], u_ref, w_ref, side_refs, even_y, last,
            )
            for c in range(3)
        )

    zero = jnp.zeros((rows, cols), jnp.float32)
    carried = lax.fori_loop(
        0, planes - 1, lambda i, carried: plane(i, carried, True), (zero,) * 3, unroll=math.gcd(3, planes - 1)
    )
    plane(planes - 1, carried, False)


def with_sides(value, low, high):
    rows, cols = value.shape
    tile = math.gcd(8, rows)
    row = lax.broadcasted_iota(jnp.int32, (tile, cols), 0)
    low, high = jnp.where(row == 0, low, 0.0), jnp.where(row == tile - 1, high, 0.0)
    if rows == tile:
        return value + (low + high)
    middle = [value[tile : rows - tile]] if rows > 2 * tile else []
    return jnp.concatenate([value[0:tile] + low, *middle, value[rows - tile :] + high], axis=0)


def advance_plane(
    c, i, here, ahead, w, carried, kx, ky, kz, kick, u_ref, w_ref, side_refs, even_y, last=False
):
    rows, cols = here.shape
    force = -carried
    pull_x = None
    if ahead is not False:
        pull_x = kx * jnp.tanh(ahead - here)
        force = force + pull_x
    pull_y = ky * jnp.tanh(pltpu.roll(here, rows - 1, 0) - here)
    force = force + (pull_y - pltpu.roll(pull_y, 1, 0))
    pull_z = kz * jnp.tanh(pltpu.roll(here, cols - 1, 1) - here)
    force = force + (pull_z - pltpu.roll(pull_z, 1, 1))
    w = w + kick * force
    u = here + w
    if last:
        u_ref[c, i] = u * (1.0 / U_SCALE)
        w_ref[c, i] = w * (1.0 / W_SCALE)
        return pull_x
    w_ref[c, i] = w
    u_ref[c, i] = u
    low, high = u[0:1], u[rows - 1 : rows]
    yc_ref, yd_ref = side_refs
    yc_ref[c, pl.ds(i, 1)] = jnp.where(even_y, high, low)
    yd_ref[c, pl.ds(i, 1)] = jnp.where(even_y, low, high)
    return pull_x


def contact_kernel(own_ref, near_ref, far_ref, pick_ref, push_ref, out_ref, *scratch):
    @pl.when(on_face())
    def _():
        def matched(c):
            pool = jnp.concatenate([near_ref[c], far_ref[c]], axis=0)
            return lax.dot_general(
                pool, pick_ref[...], (((0,), (0,)), ((), ())),
                precision=lax.Precision.HIGHEST, preferred_element_type=jnp.float32,
            )

        out_ref[...] = pressures(U_SCALE, lambda c: own_ref[c], matched, out_ref.shape, *scratch) * push_ref[...]

    @pl.when(jnp.logical_not(on_face()))
    def _():
        out_ref[...] = jnp.zeros_like(out_ref)


def listed_contact_kernel(
    own_half_ref, own_rest_ref, half_ref, rest_ref, push_ref, chosen_ref, out_ref, list_ref, *scratch
):
    rows, cols = out_ref.shape

    @pl.when(on_face())
    def _():
        def matched(c):
            return jnp.concatenate([half_ref[c], rest_ref[c]] * (scratch[0].shape[1] // rows), axis=0).T

        def own(c):
            return jnp.concatenate([own_half_ref[c], own_rest_ref[c]], axis=0)

        list_ref[...] = pressures(1.0, own, matched, out_ref.shape, *scratch)
        for r in range(rows):
            out_ref[pl.ds(chosen_ref[r], 1)] = list_ref[r : r + 1]
        out_ref[...] = out_ref[...] * push_ref[...]

    @pl.when(jnp.logical_not(on_face()))
    def _():
        out_ref[...] = jnp.zeros_like(out_ref)


def on_face():
    return lax.axis_index("gx") == lax.axis_size("gx") - 1


def pressures(scale, own_rows, matched, shape, fp_ref, fy_ref, fz_ref, base_ref, total_ref):
    rows, cols = shape
    lanes = fp_ref.shape[1]
    parts = lanes // rows
    deep = cols // parts

    lane = lax.broadcasted_iota(jnp.int32, (deep, lanes), 1)
    depth = lax.broadcasted_iota(jnp.int32, (deep, lanes), 0)

    def own(c):
        turned = jnp.concatenate([own_rows(c)] * parts, axis=0).T
        value = turned[0:deep]
        for h in range(1, parts):
            value = jnp.where(lane >= h * rows, turned[h * deep : (h + 1) * deep], value)
        return value

    gap = scale * GAP_SCALE
    along = scale * YIELD_SPAN * SPAN
    fp_ref[...] = jnp.exp2(matched(0) * gap - BIAS / 2.0)
    fy = matched(1) * along
    fy_ref[...] = fy
    spot = lax.broadcasted_iota(jnp.int32, (cols, lanes), 0).astype(jnp.float32)
    fz = matched(2) * along
    fy_square = fy * fy + SHIFT
    width = math.gcd(32, deep)
    middle = (lax.broadcasted_iota(jnp.int32, (cols, lanes), 1) // rows * deep + width // 2).astype(jnp.float32)
    for k in range(deep // width):
        z = fz + (spot - (middle + k * width)) * SPAN
        fz_ref[k] = z
        base_ref[k] = -(z * z + fy_square)
    mine = (depth % width - width // 2).astype(jnp.float32)
    op = jnp.exp2(own(0) * gap - BIAS / 2.0)
    oy = own(1) * along
    oz = own(2) * along + mine * SPAN

    own_power = jnp.exp2(SHIFT - (oy * oy + oz * oz))
    oy, oz = oy * 2.0, oz * 2.0
    for k in range(deep // width):
        some = slice(k * width, (k + 1) * width)
        total = jnp.zeros((width, lanes), jnp.float32)
        for m in range(cols):
            at = slice(m, m + 1)
            weight = jnp.exp2(oz[some] * fz_ref[k, at] + (oy[some] * fy_ref[at] + base_ref[k, at]))
            soft = jnp.log2(op[some] * fp_ref[at] + 2.0**-BIAS) + BIAS
            total = total + weight * soft
        total = total * own_power[some]
        total_ref[some] = total
    turned = jnp.concatenate([total_ref[...]] * parts, axis=0).T
    column = lax.broadcasted_iota(jnp.int32, (rows, cols), 1)
    value = turned[0:rows]
    for h in range(1, parts):
        value = jnp.where(column >= h * deep, turned[h * rows : (h + 1) * rows], value)
    return value


def last_contact_kernel(*refs):
    meet, (u_ref, w_ref, d_ref, v_ref, out_ref, *scratch, sems) = refs[:6], refs[6:]
    copies = [
        pltpu.make_async_copy(u_ref, d_ref, sems.at[0]),
        pltpu.make_async_copy(w_ref, v_ref, sems.at[1]),
    ]
    for copy in copies:
        copy.start()
    listed_contact_kernel(*meet, out_ref, *scratch)
    for copy in copies:
        copy.wait()


def link_moves(scale, extra, sent, got, edges, push_ref, c):
    moves = []
    for n in range(4):
        arrived = jnp.concatenate([half[c] for half in got[n]], axis=0) if isinstance(got[n], tuple) else got[n][c]
        stretch = arrived - sent[n][c]
        if scale != 1.0:
            stretch = stretch * scale
        moves.append(edges[n][...] * jnp.tanh(stretch))
    if c == 0:
        moves[1] = moves[1] + push_ref[...]
    a, b, c_, d = moves
    even_x, even_y = lax.axis_index("gx") % 2 == 0, lax.axis_index("yz") % 2 == 0
    moves = [jnp.where(even_x, b, a), jnp.where(even_x, a, b), jnp.where(even_y, d, c_), jnp.where(even_y, c_, d)]
    if extra:
        moves[0] = moves[0] + extra[0][c]
        moves[2] = moves[2] + extra[1][c]
    return moves


def arrivals(refs, n_got):
    sent, got, edges, refs = refs[:4], refs[4 : 4 + n_got], refs[4 + n_got : 8 + n_got], refs[8 + n_got :]
    if n_got == 5:
        a, half, rest, c, d = got
        got = [a, (half, rest), c, d]
    return sent, got, edges, refs


def boundary_kernel(scale, n_extra, n_got, *refs):
    extra, refs = refs[:n_extra], refs[n_extra:]
    u_ref, yc_ref, yd_ref, *refs = refs
    sent, got, edges, refs = arrivals(refs, n_got)
    push_ref, chosen_ref, na_ref, nb_ref, nc_ref, nd_ref, *refs = refs
    half_ref, rest_ref, xl_ref, xh_ref, yl_ref, yh_ref = refs
    _, planes, rows, cols = u_ref.shape
    even_x, even_y = lax.axis_index("gx") % 2 == 0, lax.axis_index("yz") % 2 == 0
    for c in range(3):
        xl, xh, yl, yh = link_moves(scale, extra, sent, got, edges, push_ref, c)
        xl_ref[c], xh_ref[c], yl_ref[c], yh_ref[c] = xl, xh, yl, yh
        low = with_sides(u_ref[c, 0] + xl, yl[0:1], yh[0:1])
        high = with_sides(u_ref[c, planes - 1] + xh, yl[planes - 1 :], yh[planes - 1 :])
        na_ref[c], nb_ref[c] = jnp.where(even_x, high, low), jnp.where(even_x, low, high)
        first = xl[0:1], xh[0:1]
        last = xl[rows - 1 :], xh[rows - 1 :]
        c_low, c_high = (jnp.where(even_y, y, x) for x, y in zip(first, last))
        d_low, d_high = (jnp.where(even_y, x, y) for x, y in zip(first, last))
        nc_ref[c] = with_sides(yc_ref[c] + jnp.where(even_y, yh, yl), c_low, c_high)
        nd_ref[c] = with_sides(yd_ref[c] + jnp.where(even_y, yl, yh), d_low, d_high)
    half = rows // 2

    @pl.when(on_face())
    def _():
        for n, ref in enumerate((half_ref, rest_ref)):
            for r in range(half):
                at = chosen_ref[n * half + r]
                for c in range(3):
                    ref[c, r : r + 1] = nb_ref[c, pl.ds(at, 1)]

    @pl.when(jnp.logical_not(on_face()))
    def _():
        for c in range(3):
            half_ref[c], rest_ref[c] = nb_ref[c, :half], nb_ref[c, half:]


def finish_kernel(*refs):
    u_ref, w_ref, _, _, *refs = refs
    sent, got, edges, refs = arrivals(refs, 5)
    push_ref, d_ref, v_ref, planes_ref, rows_ref, sems = refs
    _, planes, rows, cols = u_ref.shape
    tile = rows_ref.shape[4]
    inner = slice(1, planes - 1)
    copies = []
    moves = [link_moves(1.0, (), sent, got, edges, push_ref, c) for c in range(3)]
    results = ((u_ref, d_ref, 1.0 / U_SCALE), (w_ref, v_ref, 1.0 / W_SCALE))
    for n, (ref, out, scale) in enumerate(results):
        for side, at in ((0, 0), (1, rows - tile)):
            for c in range(3):
                fix = moves[c][2 + side] * scale
                for i in range(1, planes - 1):
                    value = ref[c, i, at : at + tile]
                    line = fix[i : i + 1]
                    row = lax.broadcasted_iota(jnp.int32, (tile, cols), 0)
                    rows_ref[n, side, c, i - 1] = value + jnp.where(row == (tile - 1 if side else 0), line, 0.0)
            copies.append(
                pltpu.make_async_copy(
                    rows_ref.at[n, side], out.at[:, inner, at : at + tile], sems.at[len(copies)]
                )
            )
            copies[-1].start()
    for n, (ref, out, scale) in enumerate(results):
        for side, i in ((0, 0), (1, planes - 1)):
            for c in range(3):
                xl, xh, yl, yh = moves[c]
                value = ref[c, i] + (xh if side else xl) * scale
                planes_ref[n, side, c] = with_sides(value, yl[i : i + 1] * scale, yh[i : i + 1] * scale)
            copies.append(pltpu.make_async_copy(planes_ref.at[n, side], out.at[:, i], sems.at[len(copies)]))
            copies[-1].start()
    for copy in copies:
        copy.wait()


def routes(count_body, count_x, count_y):
    def number(b, g, y):
        return (b * count_x + g) * count_y + y

    every = [(b, g, y) for b in range(count_body) for g in range(count_x) for y in range(count_y)]

    def pairs(target):
        return [(number(*at), number(*target(*at))) for at in every]

    def outer_x(b, g, y):
        if g == count_x - 1:
            return 1 - b, g, y
        return (b, (g + 1 if g % 2 else g - 1), y) if g else (b, g, y ^ 1)

    def diagonal(b, g, y):
        if g == count_x - 1:
            return 1 - b, g, (y - 1 if b else y + 1) % count_y
        return b, g, y ^ 1

    return {
        "a": pairs(lambda b, g, y: (b, g ^ 1, y)),
        "b": pairs(outer_x),
        "rest": pairs(lambda b, g, y: diagonal(b, g, y) if g == count_x - 1 else outer_x(b, g, y)),
        "c": pairs(lambda b, g, y: (b, g, y ^ 1)),
        "d": pairs(lambda b, g, y: (b, g, (y + 1 if y % 2 else y - 1) % count_y)),
        "e": pairs(diagonal),
        "corner": pairs(lambda b, g, y: (b, (g + 1) % count_x, (y + 1) % count_y)),
    }


def local(displacement, velocity, material, moduli, density, partner, active):
    planes, rows, cols = displacement.shape[2:]
    route = routes(lax.axis_size("body"), lax.axis_size("gx"), lax.axis_size("yz"))
    lanes = max(cols, 2 * rows)
    tile = math.gcd(8, rows)
    block, face, side = (planes, rows, cols), (rows, cols), (planes, cols)
    state, face3, side3 = (3, *block), (3, *face), (3, *side)
    d, v, kinds = displacement[0], velocity[0], material[0]
    smem, hbm = pltpu.SMEM, pltpu.HBM

    def passed(block, name):
        return lax.ppermute(block, AXES, route[name])

    *sent, spare, corner = call(
        pack_kernel,
        [vmem((4, *face))] * 2 + [vmem((4, *side))] * 2 + [vmem(face3), vmem((1, cols))],
        [d, kinds],
        [hbm, hbm],
        scratch=[
            pltpu.VMEM((2, *face), jnp.int32),
            vmem((2, 3, planes, 1, cols)),
            pltpu.VMEM((2, planes, 1, cols), jnp.int32),
            pltpu.SemaphoreType.DMA((8,)),
        ],
    )
    got_e = passed(spare, "e")
    got = [passed(block, name) for block, name in zip(sent, "abcd")]
    kx, ky, kz, kick, row_kick, high_ky, push_scale, pick, chosen, got[2] = call(
        setup_kernel,
        [vmem(block)] * 4 + [vmem((2, *side)), vmem(side), vmem(face), vmem((lanes, lanes))]
        + [pltpu.SMEM((rows + 1,), jnp.int32), vmem((4, *side))],
        [kinds, got[2], d, moduli, density, partner, active],
        [None, None, None] + [smem] * 4,
        aliases={1: 9},
        scratch=[vmem((rows + tile, lanes)), vmem((rows + tile, cols))],
        flops=8_000_000,
    )
    deep = cols * rows // lanes
    pair_scratch = [vmem((cols, lanes))] * 2 + [vmem((deep // math.gcd(32, deep), cols, lanes))] * 2 + [vmem((deep, lanes))]
    for step in range(STEPS):
        first, last = step == 0, step == STEPS - 1
        scale = U_SCALE if first else 1.0
        if first:
            corner, kick = lax.optimization_barrier((corner, kick))
            corner = passed(corner, "corner")
            u, w, *sides = call(
                first_kernel,
                [vmem(state)] * 2 + [vmem(side3)] * 2,
                [d, v, kx, ky, kz, kick],
            )
            push_scale, sides[0] = lax.optimization_barrier((push_scale, sides[0]))
        else:
            got_half, got_e = passed(half, "b"), passed(rest, "rest")
            got = [passed(sent[0], "a"), got_half, got_e, passed(sent[2], "c"), passed(sent[3], "d")]
            u, w, *sides = call(
                functools.partial(interior_kernel, last),
                [vmem(state)] * 2 + [vmem(side3)] * (0 if last else 2),
                [u, w, kx, ky, kz, kick, *moves],
                aliases={0: 0, 1: 1},
                flops=20_000_000,
            )
        if not first:
            meet = [half, rest, got_half, got_e, push_scale, chosen]
        if last:
            d, v, push = call(
                last_contact_kernel,
                [jax.ShapeDtypeStruct(state, jnp.float32)] * 2 + [vmem(face)],
                [*meet, u, w],
                [None] * 5 + [smem] + [None] * 2,
                scratch=[vmem(face), *pair_scratch, pltpu.SemaphoreType.DMA((2,))],
                hbm_outs=2,
                flops=20_000_000,
            )
            break
        if first:
            (push,) = call(
                contact_kernel, [vmem(face)], [sent[1], got[1], got_e, pick, push_scale], scratch=pair_scratch
            )
        else:
            (push,) = call(
                listed_contact_kernel,
                [vmem(face)],
                meet,
                [None] * 5 + [smem],
                scratch=[vmem(face), *pair_scratch],
                flops=20_000_000,
            )
        extra = []
        if first:
            kx, ky, kz, *rest = call(
                edge_kernel,
                [vmem(block)] * 3 + [vmem(face)] * 2 + [vmem(side)] * 2 + [vmem(face3), vmem(side3)],
                [*sent, *got, corner, kick, row_kick, high_ky, kx, ky, kz, moduli],
                [None] * 15 + [smem],
                aliases={12: 0, 13: 1, 14: 2},
            )
            edges, extra = rest[:4], rest[4:]
        *sent, half, rest, xl, xh, yl, yh = call(
            functools.partial(boundary_kernel, scale, len(extra), len(got)),
            [vmem(face3)] * 2 + [vmem(side3)] * 2 + [vmem((3, rows // 2, cols))] * 2
            + [vmem(face3)] * 2 + [vmem(side3)] * 2,
            [*extra, u, *sides, *sent, *got, *edges, push, chosen],
            [None] * (12 + len(got) + len(extra)) + [smem],
        )
        moves = [xl, xh, yl, yh]
    d, v = call(
        finish_kernel,
        [jax.ShapeDtypeStruct(state, jnp.float32)] * 2,
        [u, w, d, v, *sent, *got, *edges, push],
        [None, None, hbm, hbm] + [None] * 14,
        aliases={2: 0, 3: 1},
        scratch=[vmem((2, 2, *face3)), vmem((2, 2, 3, planes - 2, tile, cols)), pltpu.SemaphoreType.DMA((8,))],
        hbm_outs=2,
    )
    return d[None], v[None]


def solution(mesh):
    in_specs = (
        P("body", None, "gx", "yz", None),
        P("body", None, "gx", "yz", None),
        P("body", "gx", "yz", None),
        P(),
        P(),
        P(),
        P(),
    )
    out_specs = (P("body", None, "gx", "yz", None), P("body", None, "gx", "yz", None))
    return jax.shard_map(local, mesh=mesh, in_specs=in_specs, out_specs=out_specs, check_vma=False)
```

```python
import functools
import math

import jax
import jax.numpy as jnp
from jax import lax
from jax.experimental import pallas as pl
from jax.experimental.pallas import tpu as pltpu
from jax.sharding import PartitionSpec as P

STEPS = 4
STEP_TIME = 0.2
YIELD_SPAN = 0.5
PENALTY = 4.0
SOFT_WIDTH = 0.1
KERNEL_WIDTH = 1.5

U_SCALE = 1.0 / YIELD_SPAN
W_SCALE = STEP_TIME / YIELD_SPAN
KICK = STEP_TIME * STEP_TIME / YIELD_SPAN
LOG2E = math.log2(math.e)
GAP_SCALE = YIELD_SPAN / SOFT_WIDTH * LOG2E
SPAN = math.sqrt(LOG2E / (2.0 * KERNEL_WIDTH * KERNEL_WIDTH))
PRESSURE_SCALE = PENALTY * SOFT_WIDTH / LOG2E
STIFF = 0.25 * YIELD_SPAN
BIAS = 32.0
SHIFT = 64.0

AXES = ("body", "gx", "yz")
VMEM_LIMIT = 48 * 1024 * 1024


def vmem(shape):
    return pltpu.VMEM(shape, jnp.float32)


def call(kernel, outs, args, spaces=None, aliases=None, scratch=(), flops=0, moved=0, hbm_outs=0):
    spaces = spaces or [None] * len(args)
    specs, placed = [], []
    for arg, space in zip(args, spaces):
        if space is None:
            placed.append(pltpu.with_memory_space_constraint(arg, pltpu.VMEM))
            specs.append(pl.BlockSpec(memory_space=pltpu.VMEM))
        else:
            placed.append(pltpu.with_memory_space_constraint(arg, space) if space == pltpu.HBM else arg)
            specs.append(pl.BlockSpec(memory_space=space))
    return pl.pallas_call(
        kernel,
        out_shape=outs,
        in_specs=specs,
        out_specs=[
            pl.BlockSpec(memory_space=pl.ANY if n < hbm_outs else getattr(out, "memory_space", pltpu.VMEM))
            for n, out in enumerate(outs)
        ],
        input_output_aliases=aliases or {},
        scratch_shapes=list(scratch),
        compiler_params=pltpu.CompilerParams(vmem_limit_bytes=VMEM_LIMIT),
        cost_estimate=pl.CostEstimate(flops=flops, bytes_accessed=moved, transcendentals=0),
    )(*placed)


def here_in_mesh():
    return (
        lax.axis_index("gx"), lax.axis_size("gx"), lax.axis_index("yz"), lax.axis_size("yz"), lax.axis_index("body")
    )


def pack_kernel(
    d_ref, mat_ref, sa_ref, sb_ref, sc_ref, sd_ref, se_ref, corner_ref, plane_ref, rows_ref, kinds_ref, sems,
):
    planes, rows, cols = mat_ref.shape
    place = here_in_mesh()
    ia, ib, jc, jd = links(place, planes, rows)
    copies = []
    for n, (ref, i) in enumerate(((sa_ref, ia), (sb_ref, ib))):
        copies.append(pltpu.make_async_copy(d_ref.at[:, i], ref.at[0:3], sems.at[n]))
        copies.append(pltpu.make_async_copy(mat_ref.at[i], plane_ref.at[n], sems.at[2 + n]))
    for n, j in enumerate((jc, jd)):
        copies.append(pltpu.make_async_copy(d_ref.at[:, :, pl.ds(j, 1)], rows_ref.at[n], sems.at[4 + n]))
        copies.append(pltpu.make_async_copy(mat_ref.at[:, pl.ds(j, 1)], kinds_ref.at[n], sems.at[6 + n]))
    for copy in copies:
        copy.start()
    for copy in copies:
        copy.wait()
    kinds_a, kinds_b = plane_ref[0].astype(jnp.float32), plane_ref[1].astype(jnp.float32)
    sa_ref[3], sb_ref[3] = kinds_a, kinds_b
    for c in range(3):
        se_ref[c] = sb_ref[c]
    corner_ref[...] = jnp.where(place[0] % 2 == 0, kinds_a[rows - 1 :], kinds_b[rows - 1 :])
    for n, ref in enumerate((sc_ref, sd_ref)):
        for i in range(planes):
            for c in range(3):
                ref[c, i : i + 1] = rows_ref[n, c, i]
            ref[3, i : i + 1] = kinds_ref[n, i].astype(jnp.float32)


def links(place, planes, rows):
    ia = jnp.where(place[0] % 2 == 0, planes - 1, 0)
    jc = jnp.where(place[2] % 2 == 0, rows - 1, 0)
    return ia, planes - 1 - ia, jc, rows - 1 - jc


def setup_kernel(
    kinds_ref, rc_in, d_ref, moduli_ref, density_ref, partner_ref, active_ref,
    kx_ref, ky_ref, kz_ref, kick_ref, row_kick_ref, high_ky_ref, push_ref, pick_ref, chosen_ref, rc_ref,
    turned_ref, live_ref,
):
    planes, rows, cols = kinds_ref.shape
    place = here_in_mesh()
    last_x = place[0] == place[1] - 1
    last_y = place[2] == place[3] - 1
    row = lax.broadcasted_iota(jnp.int32, (rows, cols), 0)
    col = lax.broadcasted_iota(jnp.int32, (rows, cols), 1)
    inside = (col < cols - 1) & ((row < rows - 1) | jnp.logical_not(last_y))

    del rc_in, d_ref

    body, blocks = place[4], place[3]
    start = place[2] * rows
    other = jnp.where(body == 0, place[2] + 1, place[2] + blocks - 1) % blocks * rows

    @pl.when(last_x)
    def _():
        lane = lax.broadcasted_iota(jnp.int32, (1, turned_ref.shape[1]), 1)

        def meet(i, counts):
            new = []
            for n, (block, count) in enumerate(zip((start, other), counts)):
                b = jnp.where(body == 0, start, block) + i
                p = partner_ref[b]
                at = p - jnp.where(body == 0, block, start)
                mine = (at >= 0) & (at < rows)
                r = jnp.where(body == 0, i, at)
                row = pl.ds(jnp.where(mine, r, rows), 1)
                turned_ref[row] = jnp.where(lane == jnp.where(body == 0, at, i) + n * rows, 1.0, 0.0)
                live_ref[row] = jnp.where(lane[:, :cols] >= 0, active_ref[b].astype(jnp.float32), 0.0)
                chosen_ref[jnp.where(mine, count, rows)] = r
                new.append(count + mine.astype(jnp.int32))
            return tuple(new)

        lax.fori_loop(0, rows, meet, (jnp.int32(0), jnp.int32(rows // 2)), unroll=4)
        turned = turned_ref[0:rows]
        pick_ref[...] = jnp.concatenate([turned] * (pick_ref.shape[1] // rows), axis=0).T
        push_ref[...] = live_ref[0:rows] * (-PRESSURE_SCALE)

    @pl.when(jnp.logical_not(last_x))
    def _():
        push_ref[...] = jnp.zeros_like(push_ref)
        pick_ref[...] = jnp.zeros_like(pick_ref)

        def any_row(r, _):
            chosen_ref[r] = 0
            return 0

        lax.fori_loop(0, chosen_ref.shape[0], any_row, 0, unroll=8)

    def plane(i, earlier):
        kinds = kinds_ref[i]
        stiff = jnp.zeros((rows, cols), jnp.float32)
        mass = jnp.ones((rows, cols), jnp.float32)
        for m in range(moduli_ref.shape[0]):
            hit = kinds == m
            stiff = jnp.where(hit, moduli_ref[m] * STIFF, stiff)
            mass = jnp.where(hit, density_ref[m], mass)
        keep = inside & ((i < planes - 1) | jnp.logical_not(last_x))
        here = jnp.where(keep, stiff, 0.0)
        kick = KICK / mass
        kick_ref[i] = kick
        row_kick_ref[0, pl.ds(i, 1)] = kick[0:1]
        row_kick_ref[1, pl.ds(i, 1)] = kick[rows - 1 : rows]
        s = here + pltpu.roll(here, 1, 1)
        both = here + earlier
        ky = both + pltpu.roll(both, 1, 1)
        high_ky_ref[pl.ds(i, 1)] = ky[rows - 1 : rows]
        kx_ref[i] = s + rows_behind(s, row)
        ky_ref[i] = jnp.where(row < rows - 1, ky, 0.0)
        kz_ref[i] = both + rows_behind(both, row)
        return here

    lax.fori_loop(0, planes, plane, jnp.zeros((rows, cols), jnp.float32), unroll=math.gcd(16, planes))
    push_ref[...] = push_ref[...] * kick_ref[planes - 1]


def rows_behind(value, row, first=0.0):
    return jnp.where(row == 0, first, pltpu.roll(value, 1, 0))


def first_kernel(d_ref, v_ref, kx_ref, ky_ref, kz_ref, kick_ref, u_ref, w_ref, yc_ref, yd_ref):
    _, planes, rows, cols = u_ref.shape
    even_y = lax.axis_index("yz") % 2 == 0

    def plane(i, carried, ahead):
        return tuple(
            advance_plane(
                c, i, d_ref[c, i] * U_SCALE, ahead and d_ref[c, i + 1] * U_SCALE, v_ref[c, i] * W_SCALE, carried[c],
                kx_ref[i], ky_ref[i], kz_ref[i], kick_ref[i], u_ref, w_ref, (yc_ref, yd_ref), even_y,
            )
            for c in range(3)
        )

    zero = jnp.zeros((rows, cols), jnp.float32)
    carried = lax.fori_loop(
        0, planes - 1, lambda i, carried: plane(i, carried, True), (zero,) * 3, unroll=math.gcd(3, planes - 1)
    )
    plane(planes - 1, carried, False)


def edge_kernel(
    sa_ref, sb_ref, sc_ref, sd_ref, ra_ref, rb_ref, rc_ref, rd_ref, corner_ref,
    kick_ref, row_kick_ref, high_ky_ref, kx_in, ky_in, kz_in, moduli_ref,
    kx_ref, ky_ref, kz_ref, ka_ref, kb_ref, kc_ref, kd_ref, ex_ref, ey_ref,
):
    planes, rows, cols = kick_ref.shape
    place = here_in_mesh()
    even_x, even_y = place[0] % 2 == 0, place[2] % 2 == 0
    inner_x, inner_y = place[0] > 0, place[2] > 0
    last_x = place[0] == place[1] - 1
    last_y = place[2] == place[3] - 1
    row = lax.broadcasted_iota(jnp.int32, (rows, cols), 0)
    plane = lax.broadcasted_iota(jnp.int32, (planes, cols), 0)

    def looked_up(kinds, keep):
        stiff = jnp.zeros(kinds.shape, jnp.float32)
        for m in range(moduli_ref.shape[0]):
            stiff = jnp.where(kinds == m, moduli_ref[m] * STIFF, stiff)
        col = lax.broadcasted_iota(jnp.int32, kinds.shape, 1)
        return jnp.where((col < cols - 1) & keep, stiff, 0.0)

    def with_behind(value):
        return value + pltpu.roll(value, 1, 1)

    below_x = looked_up(
        jnp.where(even_x, rb_ref[3], ra_ref[3]), inner_x & ((row < rows - 1) | jnp.logical_not(last_y))
    )
    below_y = looked_up(
        jnp.where(even_y, rd_ref[3], rc_ref[3]), inner_y & ((plane < planes - 1) | jnp.logical_not(last_x))
    )
    corner = looked_up(corner_ref[...], inner_x & inner_y)
    s_x, s_y, s_corner = with_behind(below_x), with_behind(below_y), with_behind(corner)

    x_low = kick_ref[0] * (s_x + rows_behind(s_x, row, s_corner))
    y_low = row_kick_ref[0] * (s_y + rows_behind(s_y, plane, s_corner))
    plane_ky = jnp.where(row < rows - 1, s_x, 0.0)
    plane_kz = below_x + rows_behind(below_x, row, corner)
    rows_kx = jnp.where(plane < planes - 1, s_y, 0.0)
    rows_kz = below_y + rows_behind(below_y, plane)

    ky_ref[0] += plane_ky
    kz_ref[0] += plane_kz
    for i in range(planes):
        kx_ref[i, 0:1] += s_y[i : i + 1]
        kz_ref[i, 0:1] += rows_kz[i : i + 1]
    x_high = kick_ref[planes - 1] * kx_ref[planes - 1]
    y_high = (high_ky_ref[...] + jnp.where(plane == 0, s_x[rows - 1 : rows], 0.0)) * row_kick_ref[1]
    ka_ref[...] = jnp.where(even_x, x_high, x_low)
    kb_ref[...] = jnp.where(even_x, x_low, x_high)
    kc_ref[...] = jnp.where(even_y, y_high, y_low)
    kd_ref[...] = jnp.where(even_y, y_low, y_high)

    for c in range(3):
        u = jnp.where(even_x, sb_ref[c], sa_ref[c]) * U_SCALE
        pull_y = plane_ky * jnp.tanh(pltpu.roll(u, rows - 1, 0) - u)
        pull_z = plane_kz * jnp.tanh(pltpu.roll(u, cols - 1, 1) - u)
        ex_ref[c] = kick_ref[0] * (pull_y - pltpu.roll(pull_y, 1, 0) + (pull_z - pltpu.roll(pull_z, 1, 1)))
        u = jnp.where(even_y, sd_ref[c], sc_ref[c]) * U_SCALE
        pull_x = rows_kx * jnp.tanh(pltpu.roll(u, planes - 1, 0) - u)
        pull_z = rows_kz * jnp.tanh(pltpu.roll(u, cols - 1, 1) - u)
        ey_ref[c] = row_kick_ref[0] * (pull_x - pltpu.roll(pull_x, 1, 0) + (pull_z - pltpu.roll(pull_z, 1, 1)))


def interior_kernel(
    last, u_in, w_in, kx_ref, ky_ref, kz_ref, kick_ref, xl_ref, xh_ref, yl_ref, yh_ref, u_ref, w_ref, *side_refs
):
    _, planes, rows, cols = u_ref.shape
    even_y = lax.axis_index("yz") % 2 == 0
    for ref in (u_ref, w_ref):
        for c in range(3):
            ref[c, 0] += xl_ref[c]
            ref[c, planes - 1] += xh_ref[c]

    def fixed(ref, c, i):
        return with_sides(ref[c, i], yl_ref[c, pl.ds(i, 1)], yh_ref[c, pl.ds(i, 1)])

    def plane(i, carried, ahead):
        return tuple(
            advance_plane(
                c, i, fixed(u_ref, c, i), ahead and fixed(u_ref, c, i + 1), fixed(w_ref, c, i), carried[c],
                kx_ref[i], ky_ref[i], kz_ref[i], kick_ref[i], u_ref, w_ref, side_refs, even_y, last,
            )
            for c in range(3)
        )

    zero = jnp.zeros((rows, cols), jnp.float32)
    carried = lax.fori_loop(
        0, planes - 1, lambda i, carried: plane(i, carried, True), (zero,) * 3, unroll=math.gcd(3, planes - 1)
    )
    plane(planes - 1, carried, False)


def with_sides(value, low, high):
    rows, cols = value.shape
    tile = math.gcd(8, rows)
    row = lax.broadcasted_iota(jnp.int32, (tile, cols), 0)
    low, high = jnp.where(row == 0, low, 0.0), jnp.where(row == tile - 1, high, 0.0)
    if rows == tile:
        return value + (low + high)
    middle = [value[tile : rows - tile]] if rows > 2 * tile else []
    return jnp.concatenate([value[0:tile] + low, *middle, value[rows - tile :] + high], axis=0)


def advance_plane(
    c, i, here, ahead, w, carried, kx, ky, kz, kick, u_ref, w_ref, side_refs, even_y, last=False
):
    rows, cols = here.shape
    force = -carried
    pull_x = None
    if ahead is not False:
        pull_x = kx * jnp.tanh(ahead - here)
        force = force + pull_x
    pull_y = ky * jnp.tanh(pltpu.roll(here, rows - 1, 0) - here)
    force = force + (pull_y - pltpu.roll(pull_y, 1, 0))
    pull_z = kz * jnp.tanh(pltpu.roll(here, cols - 1, 1) - here)
    force = force + (pull_z - pltpu.roll(pull_z, 1, 1))
    w = w + kick * force
    u = here + w
    if last:
        u_ref[c, i] = u * (1.0 / U_SCALE)
        w_ref[c, i] = w * (1.0 / W_SCALE)
        return pull_x
    w_ref[c, i] = w
    u_ref[c, i] = u
    low, high = u[0:1], u[rows - 1 : rows]
    yc_ref, yd_ref = side_refs
    yc_ref[c, pl.ds(i, 1)] = jnp.where(even_y, high, low)
    yd_ref[c, pl.ds(i, 1)] = jnp.where(even_y, low, high)
    return pull_x


def contact_kernel(own_ref, near_ref, far_ref, pick_ref, push_ref, out_ref, *scratch):
    @pl.when(on_face())
    def _():
        def matched(c):
            pool = jnp.concatenate([near_ref[c], far_ref[c]], axis=0)
            return lax.dot_general(
                pool, pick_ref[...], (((0,), (0,)), ((), ())),
                precision=lax.Precision.HIGHEST, preferred_element_type=jnp.float32,
            )

        out_ref[...] = pressures(U_SCALE, lambda c: own_ref[c], matched, out_ref.shape, *scratch) * push_ref[...]

    @pl.when(jnp.logical_not(on_face()))
    def _():
        out_ref[...] = jnp.zeros_like(out_ref)


def listed_contact_kernel(
    own_half_ref, own_rest_ref, half_ref, rest_ref, push_ref, chosen_ref, out_ref, list_ref, *scratch
):
    rows, cols = out_ref.shape

    @pl.when(on_face())
    def _():
        def matched(c):
            return jnp.concatenate([half_ref[c], rest_ref[c]] * (scratch[0].shape[1] // rows), axis=0).T

        def own(c):
            return jnp.concatenate([own_half_ref[c], own_rest_ref[c]], axis=0)

        list_ref[...] = pressures(1.0, own, matched, out_ref.shape, *scratch)
        for r in range(rows):
            out_ref[pl.ds(chosen_ref[r], 1)] = list_ref[r : r + 1]
        out_ref[...] = out_ref[...] * push_ref[...]

    @pl.when(jnp.logical_not(on_face()))
    def _():
        out_ref[...] = jnp.zeros_like(out_ref)


def on_face():
    return lax.axis_index("gx") == lax.axis_size("gx") - 1


def pressures(scale, own_rows, matched, shape, fp_ref, fy_ref, fz_ref, base_ref, total_ref):
    rows, cols = shape
    lanes = fp_ref.shape[1]
    parts = lanes // rows
    deep = cols // parts

    lane = lax.broadcasted_iota(jnp.int32, (deep, lanes), 1)
    depth = lax.broadcasted_iota(jnp.int32, (deep, lanes), 0)

    def own(c):
        turned = jnp.concatenate([own_rows(c)] * parts, axis=0).T
        value = turned[0:deep]
        for h in range(1, parts):
            value = jnp.where(lane >= h * rows, turned[h * deep : (h + 1) * deep], value)
        return value

    gap = scale * GAP_SCALE
    along = scale * YIELD_SPAN * SPAN
    fp_ref[...] = jnp.exp2(matched(0) * gap - BIAS / 2.0)
    fy = matched(1) * along
    fy_ref[...] = fy
    spot = lax.broadcasted_iota(jnp.int32, (cols, lanes), 0).astype(jnp.float32)
    fz = matched(2) * along
    fy_square = fy * fy + SHIFT
    width = math.gcd(32, deep)
    middle = (lax.broadcasted_iota(jnp.int32, (cols, lanes), 1) // rows * deep + width // 2).astype(jnp.float32)
    for k in range(deep // width):
        z = fz + (spot - (middle + k * width)) * SPAN
        fz_ref[k] = z
        base_ref[k] = -(z * z + fy_square)
    mine = (depth % width - width // 2).astype(jnp.float32)
    op = jnp.exp2(own(0) * gap - BIAS / 2.0)
    oy = own(1) * along
    oz = own(2) * along + mine * SPAN

    own_power = jnp.exp2(SHIFT - (oy * oy + oz * oz))
    oy, oz = oy * 2.0, oz * 2.0
    for k in range(deep // width):
        some = slice(k * width, (k + 1) * width)
        total = jnp.zeros((width, lanes), jnp.float32)
        for m in range(cols):
            at = slice(m, m + 1)
            weight = jnp.exp2(oz[some] * fz_ref[k, at] + (oy[some] * fy_ref[at] + base_ref[k, at]))
            soft = jnp.log2(op[some] * fp_ref[at] + 2.0**-BIAS) + BIAS
            total = total + weight * soft
        total = total * own_power[some]
        total_ref[some] = total
    turned = jnp.concatenate([total_ref[...]] * parts, axis=0).T
    column = lax.broadcasted_iota(jnp.int32, (rows, cols), 1)
    value = turned[0:rows]
    for h in range(1, parts):
        value = jnp.where(column >= h * deep, turned[h * rows : (h + 1) * rows], value)
    return value


def last_contact_kernel(*refs):
    meet, (u_ref, w_ref, d_ref, v_ref, out_ref, *scratch, sems) = refs[:6], refs[6:]
    copies = [
        pltpu.make_async_copy(u_ref, d_ref, sems.at[0]),
        pltpu.make_async_copy(w_ref, v_ref, sems.at[1]),
    ]
    for copy in copies:
        copy.start()
    listed_contact_kernel(*meet, out_ref, *scratch)
    for copy in copies:
        copy.wait()


def link_moves(scale, extra, sent, got, edges, push_ref, c):
    moves = []
    for n in range(4):
        arrived = jnp.concatenate([half[c] for half in got[n]], axis=0) if isinstance(got[n], tuple) else got[n][c]
        stretch = arrived - sent[n][c]
        if scale != 1.0:
            stretch = stretch * scale
        moves.append(edges[n][...] * jnp.tanh(stretch))
    if c == 0:
        moves[1] = moves[1] + push_ref[...]
    a, b, c_, d = moves
    even_x, even_y = lax.axis_index("gx") % 2 == 0, lax.axis_index("yz") % 2 == 0
    moves = [jnp.where(even_x, b, a), jnp.where(even_x, a, b), jnp.where(even_y, d, c_), jnp.where(even_y, c_, d)]
    if extra:
        moves[0] = moves[0] + extra[0][c]
        moves[2] = moves[2] + extra[1][c]
    return moves


def arrivals(refs, n_got):
    sent, got, edges, refs = refs[:4], refs[4 : 4 + n_got], refs[4 + n_got : 8 + n_got], refs[8 + n_got :]
    if n_got == 5:
        a, half, rest, c, d = got
        got = [a, (half, rest), c, d]
    return sent, got, edges, refs


def boundary_kernel(scale, n_extra, n_got, *refs):
    extra, refs = refs[:n_extra], refs[n_extra:]
    u_ref, yc_ref, yd_ref, *refs = refs
    sent, got, edges, refs = arrivals(refs, n_got)
    push_ref, chosen_ref, na_ref, nb_ref, nc_ref, nd_ref, *refs = refs
    half_ref, rest_ref, xl_ref, xh_ref, yl_ref, yh_ref = refs
    _, planes, rows, cols = u_ref.shape
    even_x, even_y = lax.axis_index("gx") % 2 == 0, lax.axis_index("yz") % 2 == 0
    for c in range(3):
        xl, xh, yl, yh = link_moves(scale, extra, sent, got, edges, push_ref, c)
        xl_ref[c], xh_ref[c], yl_ref[c], yh_ref[c] = xl, xh, yl, yh
        low = with_sides(u_ref[c, 0] + xl, yl[0:1], yh[0:1])
        high = with_sides(u_ref[c, planes - 1] + xh, yl[planes - 1 :], yh[planes - 1 :])
        na_ref[c], nb_ref[c] = jnp.where(even_x, high, low), jnp.where(even_x, low, high)
        first = xl[0:1], xh[0:1]
        last = xl[rows - 1 :], xh[rows - 1 :]
        c_low, c_high = (jnp.where(even_y, y, x) for x, y in zip(first, last))
        d_low, d_high = (jnp.where(even_y, x, y) for x, y in zip(first, last))
        nc_ref[c] = with_sides(yc_ref[c] + jnp.where(even_y, yh, yl), c_low, c_high)
        nd_ref[c] = with_sides(yd_ref[c] + jnp.where(even_y, yl, yh), d_low, d_high)
    half = rows // 2

    @pl.when(on_face())
    def _():
        for n, ref in enumerate((half_ref, rest_ref)):
            for r in range(half):
                at = chosen_ref[n * half + r]
                for c in range(3):
                    ref[c, r : r + 1] = nb_ref[c, pl.ds(at, 1)]

    @pl.when(jnp.logical_not(on_face()))
    def _():
        for c in range(3):
            half_ref[c], rest_ref[c] = nb_ref[c, :half], nb_ref[c, half:]


def finish_kernel(*refs):
    u_ref, w_ref, _, _, *refs = refs
    sent, got, edges, refs = arrivals(refs, 5)
    push_ref, d_ref, v_ref, planes_ref, rows_ref, sems = refs
    _, planes, rows, cols = u_ref.shape
    inner = slice(1, planes - 1)
    copies = []
    moves = [link_moves(1.0, (), sent, got, edges, push_ref, c) for c in range(3)]
    results = ((u_ref, d_ref, 1.0 / U_SCALE), (w_ref, v_ref, 1.0 / W_SCALE))
    for n, (ref, out, scale) in enumerate(results):
        for side, at in ((0, 0), (1, rows - 1)):
            for c in range(3):
                fix = moves[c][2 + side] * scale
                for i in range(1, planes - 1):
                    rows_ref[n, side, c, i - 1] = ref[c, i, at : at + 1] + fix[i : i + 1]
            copies.append(
                pltpu.make_async_copy(rows_ref.at[n, side], out.at[:, inner, at : at + 1], sems.at[len(copies)])
            )
            copies[-1].start()
    for n, (ref, out, scale) in enumerate(results):
        for side, i in ((0, 0), (1, planes - 1)):
            for c in range(3):
                xl, xh, yl, yh = moves[c]
                value = ref[c, i] + (xh if side else xl) * scale
                planes_ref[n, side, c] = with_sides(value, yl[i : i + 1] * scale, yh[i : i + 1] * scale)
            copies.append(pltpu.make_async_copy(planes_ref.at[n, side], out.at[:, i], sems.at[len(copies)]))
            copies[-1].start()
    for copy in copies:
        copy.wait()


def routes(count_body, count_x, count_y):
    def number(b, g, y):
        return (b * count_x + g) * count_y + y

    every = [(b, g, y) for b in range(count_body) for g in range(count_x) for y in range(count_y)]

    def pairs(target):
        return [(number(*at), number(*target(*at))) for at in every]

    def outer_x(b, g, y):
        if g == count_x - 1:
            return 1 - b, g, y
        return (b, (g + 1 if g % 2 else g - 1), y) if g else (b, g, y ^ 1)

    def diagonal(b, g, y):
        if g == count_x - 1:
            return 1 - b, g, (y - 1 if b else y + 1) % count_y
        return b, g, y ^ 1

    return {
        "a": pairs(lambda b, g, y: (b, g ^ 1, y)),
        "b": pairs(outer_x),
        "rest": pairs(lambda b, g, y: diagonal(b, g, y) if g == count_x - 1 else outer_x(b, g, y)),
        "c": pairs(lambda b, g, y: (b, g, y ^ 1)),
        "d": pairs(lambda b, g, y: (b, g, (y + 1 if y % 2 else y - 1) % count_y)),
        "e": pairs(diagonal),
        "corner": pairs(lambda b, g, y: (b, (g + 1) % count_x, (y + 1) % count_y)),
    }


def local(displacement, velocity, material, moduli, density, partner, active):
    planes, rows, cols = displacement.shape[2:]
    route = routes(lax.axis_size("body"), lax.axis_size("gx"), lax.axis_size("yz"))
    lanes = max(cols, 2 * rows)
    tile = math.gcd(8, rows)
    block, face, side = (planes, rows, cols), (rows, cols), (planes, cols)
    state, face3, side3 = (3, *block), (3, *face), (3, *side)
    d, v, kinds = displacement[0], velocity[0], material[0]
    smem, hbm = pltpu.SMEM, pltpu.HBM

    def passed(block, name):
        return lax.ppermute(block, AXES, route[name])

    *sent, spare, corner = call(
        pack_kernel,
        [vmem((4, *face))] * 2 + [vmem((4, *side))] * 2 + [vmem(face3), vmem((1, cols))],
        [d, kinds],
        [hbm, hbm],
        scratch=[
            pltpu.VMEM((2, *face), jnp.int32),
            vmem((2, 3, planes, 1, cols)),
            pltpu.VMEM((2, planes, 1, cols), jnp.int32),
            pltpu.SemaphoreType.DMA((8,)),
        ],
    )
    got_e = passed(spare, "e")
    got = [passed(block, name) for block, name in zip(sent, "abcd")]
    kx, ky, kz, kick, row_kick, high_ky, push_scale, pick, chosen, got[2] = call(
        setup_kernel,
        [vmem(block)] * 4 + [vmem((2, *side)), vmem(side), vmem(face), vmem((lanes, lanes))]
        + [pltpu.SMEM((rows + 1,), jnp.int32), vmem((4, *side))],
        [kinds, got[2], d, moduli, density, partner, active],
        [None, None, None] + [smem] * 4,
        aliases={1: 9},
        scratch=[vmem((rows + tile, lanes)), vmem((rows + tile, cols))],
        flops=8_000_000,
    )
    deep = cols * rows // lanes
    pair_scratch = [vmem((cols, lanes))] * 2 + [vmem((deep // math.gcd(32, deep), cols, lanes))] * 2 + [vmem((deep, lanes))]
    for step in range(STEPS):
        first, last = step == 0, step == STEPS - 1
        scale = U_SCALE if first else 1.0
        if first:
            corner, kick = lax.optimization_barrier((corner, kick))
            corner = passed(corner, "corner")
            u, w, *sides = call(
                first_kernel,
                [vmem(state)] * 2 + [vmem(side3)] * 2,
                [d, v, kx, ky, kz, kick],
            )
            push_scale, sides[0] = lax.optimization_barrier((push_scale, sides[0]))
        else:
            got_half, got_e = passed(half, "b"), passed(rest, "rest")
            got = [passed(sent[0], "a"), got_half, got_e, passed(sent[2], "c"), passed(sent[3], "d")]
            u, w, *sides = call(
                functools.partial(interior_kernel, last),
                [vmem(state)] * 2 + [vmem(side3)] * (0 if last else 2),
                [u, w, kx, ky, kz, kick, *moves],
                aliases={0: 0, 1: 1},
                flops=20_000_000,
            )
        if not first:
            meet = [half, rest, got_half, got_e, push_scale, chosen]
        if last:
            d, v, push = call(
                last_contact_kernel,
                [jax.ShapeDtypeStruct(state, jnp.float32)] * 2 + [vmem(face)],
                [*meet, u, w],
                [None] * 5 + [smem] + [None] * 2,
                scratch=[vmem(face), *pair_scratch, pltpu.SemaphoreType.DMA((2,))],
                hbm_outs=2,
                flops=20_000_000,
            )
            break
        if first:
            (push,) = call(
                contact_kernel, [vmem(face)], [sent[1], got[1], got_e, pick, push_scale], scratch=pair_scratch
            )
        else:
            (push,) = call(
                listed_contact_kernel,
                [vmem(face)],
                meet,
                [None] * 5 + [smem],
                scratch=[vmem(face), *pair_scratch],
                flops=20_000_000,
            )
        extra = []
        if first:
            kx, ky, kz, *rest = call(
                edge_kernel,
                [vmem(block)] * 3 + [vmem(face)] * 2 + [vmem(side)] * 2 + [vmem(face3), vmem(side3)],
                [*sent, *got, corner, kick, row_kick, high_ky, kx, ky, kz, moduli],
                [None] * 15 + [smem],
                aliases={12: 0, 13: 1, 14: 2},
            )
            edges, extra = rest[:4], rest[4:]
        *sent, half, rest, xl, xh, yl, yh = call(
            functools.partial(boundary_kernel, scale, len(extra), len(got)),
            [vmem(face3)] * 2 + [vmem(side3)] * 2 + [vmem((3, rows // 2, cols))] * 2
            + [vmem(face3)] * 2 + [vmem(side3)] * 2,
            [*extra, u, *sides, *sent, *got, *edges, push, chosen],
            [None] * (12 + len(got) + len(extra)) + [smem],
        )
        moves = [xl, xh, yl, yh]
    d, v = call(
        finish_kernel,
        [jax.ShapeDtypeStruct(state, jnp.float32)] * 2,
        [u, w, d, v, *sent, *got, *edges, push],
        [None, None, hbm, hbm] + [None] * 14,
        aliases={2: 0, 3: 1},
        scratch=[vmem((2, 2, *face3)), vmem((2, 2, 3, planes - 2, 1, cols)), pltpu.SemaphoreType.DMA((8,))],
        hbm_outs=2,
    )
    return d[None], v[None]


def solution(mesh):
    in_specs = (
        P("body", None, "gx", "yz", None),
        P("body", None, "gx", "yz", None),
        P("body", "gx", "yz", None),
        P(),
        P(),
        P(),
        P(),
    )
    out_specs = (P("body", None, "gx", "yz", None), P("body", None, "gx", "yz", None))
    return jax.shard_map(local, mesh=mesh, in_specs=in_specs, out_specs=out_specs, check_vma=False)
```
